32 devices in a mesh: ctx: 2 (over x), fsdp: 16 (over z, y, core).
Axes of the slice: x: 2, y: 2, z: 4, core: 2. Of those that a mesh axis runs over, the one named last changes fastest.
Arguments:
- layer_input: bfloat16 [2, 16, 1024, 768], P(None, 'fsdp', 'ctx'), may hold values from -6 to 6
- segments: int32 [2, 16, 1024], P(None, 'fsdp'), may hold values from 0 to 2, as said below
- ln1_gain: bfloat16 [768], P('fsdp'), may hold values from 0.5 to 1.5
- ln1_bias: bfloat16 [768], P('fsdp'), may hold values from -1.1953125 to 1.1953125
- w_qkv: bfloat16 [768, 2304], P('fsdp'), may hold values from -0.21875 to 0.21875
- q_bias: bfloat16 [768], P('fsdp'), may hold values from -1.796875 to 1.796875
- v_bias: bfloat16 [768], P('fsdp'), may hold values from -1.796875 to 1.796875
- w_attn_out: bfloat16 [768, 768], P('fsdp'), may hold values from -0.625 to 0.625
- b_attn_out: bfloat16 [768], P('fsdp'), may hold values from -1.1953125 to 1.1953125
- ln2_gain: bfloat16 [768], P('fsdp'), may hold values from 0.5 to 1.5
- ln2_bias: bfloat16 [768], P('fsdp'), may hold values from -1.1953125 to 1.1953125
- w_up: bfloat16 [768, 3072], P('fsdp'), may hold values from -0.21875 to 0.21875
- b_up: bfloat16 [3072], P('fsdp'), may hold values from -1.1953125 to 1.1953125
- w_down: bfloat16 [3072, 768], P('fsdp'), may hold values from -0.109375 to 0.109375
- b_down: bfloat16 [768], P('fsdp'), may hold values from -1.1953125 to 1.1953125
- cotangent: bfloat16 [2, 16, 1024, 768], P(None, 'fsdp', 'ctx'), may hold values from -6 to 6
Outputs:
- activations: bfloat16 [2, 16, 1024, 768], P(None, 'fsdp', 'ctx')
- input_grad: bfloat16 [2, 16, 1024, 768], P(None, 'fsdp', 'ctx')
- grad_ln1_gain: float32 [768], P('fsdp')
- grad_ln1_bias: float32 [768], P('fsdp')
- grad_w_qkv: float32 [768, 2304], P('fsdp')
- grad_q_bias: float32 [768], P('fsdp')
- grad_v_bias: float32 [768], P('fsdp')
- grad_w_attn_out: float32 [768, 768], P('fsdp')
- grad_b_attn_out: float32 [768], P('fsdp')
- grad_ln2_gain: float32 [768], P('fsdp')
- grad_ln2_bias: float32 [768], P('fsdp')
- grad_w_up: float32 [768, 3072], P('fsdp')
- grad_b_up: float32 [3072], P('fsdp')
- grad_w_down: float32 [3072, 768], P('fsdp')
- grad_b_down: float32 [768], P('fsdp')
The draws below stay inside these ranges and needn't reach their ends.
Inputs may be any that keep to these rules, and one draw needn't show every extreme that they name: `segments`: along each sequence's positions (stored rows ordered by pos) segment numbers start at 0 and rise by at most one from a position to the next; one document covers exactly the first or exactly the second half of the positions.
All inputs are finite; a program needn't handle non-finite values.
Results may differ from the reference program's by a relative error of at most 0.012.
Values may be sent and summed in bfloat16 or wider, within the bound.
A program may use at most 256 MiB of HBM per device.

```python
import jax
import jax.numpy as jnp
from jax import lax

H = 12
HD = 64
FF = 3072
D = 768
TOK_DEV = 512
MB = 2
SEQS = 16
SEQ_LEN = 1024
N_CTX = 2


def stored_positions_drawn(length, groups):
    block_size = length // (2 * groups)
    stored = jnp.arange(length, dtype=jnp.int32)
    holder = stored // (2 * block_size)
    within = stored % (2 * block_size)
    second = within // block_size
    offset = within % block_size
    block_index = jnp.where(second == 0, holder, 2 * groups - 1 - holder)
    return (block_index * block_size + offset).astype(jnp.int32)


def draw_segments(key, part):
    length = SEQ_LEN
    middle = length // 2
    count_rows = MB * SEQS
    bounds = max(SEQ_LEN // 2048, 1)
    first_key = jax.random.fold_in(key, 11)
    second_key = jax.random.fold_in(key, 23)
    which = jax.random.randint(first_key, (count_rows, 1), 0, 2)
    row_keys = jax.random.split(second_key, count_rows)

    def pick(row_key):
        return jax.random.permutation(row_key, middle - 1)[:bounds].astype(jnp.int32)
    chosen = jax.vmap(pick)(row_keys)
    offset = jnp.where(which == 0, middle + 1, 1).astype(jnp.int32)
    marked = (chosen + offset).astype(jnp.int32)
    place = jnp.arange(length, dtype=jnp.int32)[None, :]
    hits = jnp.sum((place[:, :, None] == marked[:, None, :]).astype(jnp.int32), axis=2)
    flags = jnp.where(place == middle, 1, hits).astype(jnp.int32)
    real_ids = jnp.cumsum(flags, axis=1).astype(jnp.int32)
    order = stored_positions_drawn(length, length // TOK_DEV)
    return real_ids[:, order].reshape(MB, SEQS, length).astype(jnp.int32)


def strengthened(values, key, source, target, parts, factor):
    def block_of(position):
        return (jnp.arange(values.shape[position]) // (values.shape[position] // parts)).reshape((-1,) + (1,) * (values.ndim - 1 - position))

    first = jax.random.permutation(key, parts)[block_of(target)]
    other_side = (block_of(target) + parts // 2) % parts
    return jnp.where((block_of(source) == first) | (block_of(source) == other_side), factor * values, values)


def shard_levels(rng, extent, cuts, least, top_value):
    def one(position, blocks):
        steps = jax.random.uniform(jax.random.fold_in(jax.random.fold_in(rng, 6), position), (blocks,), jnp.float32, least / len(cuts), top_value / len(cuts))
        return jnp.repeat(jnp.exp(steps), extent[position] // blocks).reshape((-1,) + (1,) * (len(extent) - position - 1))

    level = one(*cuts[0])
    for cut in cuts[1:]:
        level = level * one(*cut)
    return level


def noise(key, shape, deviation, bound, shards=(), kind=jnp.bfloat16):
    values = jax.random.normal(key, shape, jnp.float32) * deviation
    if len(shards) > 0:
        values = shard_levels(key, shape, shards, -0.22, 0.18) * values
    return jnp.clip(values, min=-bound, max=bound).astype(kind)


def gaussian_with(own_key, dims, spread, most, cuts, heavy, held_as=jnp.bfloat16):
    result = spread * jax.random.normal(own_key, dims, jnp.float32)
    if cuts:
        result = result * shard_levels(own_key, dims, cuts, -0.22, 0.18)
    return jnp.clip(strengthened(result, jax.random.fold_in(own_key, 3), *heavy), -most, most).astype(held_as)


def setup_inputs(seed: int = 0) -> dict:
    arg_keys = jax.random.split(jax.random.key(seed), 17)
    layer_input = gaussian_with(arg_keys[0], (MB, SEQS, SEQ_LEN, D), 1.0, 6.0, ((1, 16), (2, 2)), (1, 3, 16, 2.0))
    segments = draw_segments(jax.random.fold_in(arg_keys[16], 71), 0)
    ln1_gain = jnp.clip(1.0 + 0.1 * jax.random.normal(arg_keys[2], (D,), jnp.float32), 0.5, 1.5).astype(jnp.bfloat16)
    ln1_bias = noise(arg_keys[3], (D,), 0.2, 1.1953125, ((0, 16),))
    w_qkv = noise(arg_keys[4], (D, 3 * D), D ** -0.5, 0.21875, ((0, 16),))
    q_bias = noise(arg_keys[5], (D,), 0.3, 1.796875, ((0, 16),))
    v_bias = noise(arg_keys[6], (D,), 0.3, 1.796875, ((0, 16),))
    w_attn_out = noise(arg_keys[7], (D, D), (D // 8) ** -0.5, 0.625, ((0, 16),))
    b_attn_out = noise(arg_keys[8], (D,), 0.2, 1.1953125, ((0, 16),))
    ln2_gain = jnp.clip(1.0 + 0.1 * jax.random.normal(arg_keys[9], (D,), jnp.float32), 0.5, 1.5).astype(jnp.bfloat16)
    ln2_bias = noise(arg_keys[10], (D,), 0.2, 1.1953125, ((0, 16),))
    w_up = noise(arg_keys[11], (D, FF), D ** -0.5, 0.21875, ((0, 16),))
    b_up = noise(arg_keys[12], (FF,), 0.2, 1.1953125, ((0, 16),))
    w_down = noise(arg_keys[13], (FF, D), FF ** -0.5, 0.109375, ((0, 16),))
    b_down = noise(arg_keys[14], (D,), 0.2, 1.1953125, ((0, 16),))
    cotangent = gaussian_with(arg_keys[15], (MB, SEQS, SEQ_LEN, D), 1.0, 6.0, ((1, 16), (2, 2)), (1, 3, 16, 2.0))
    return dict(layer_input=layer_input, segments=segments, ln1_gain=ln1_gain, ln1_bias=ln1_bias, w_qkv=w_qkv, q_bias=q_bias, v_bias=v_bias, w_attn_out=w_attn_out, b_attn_out=b_attn_out, ln2_gain=ln2_gain, ln2_bias=ln2_bias, w_up=w_up, b_up=b_up, w_down=w_down, b_down=b_down, cotangent=cotangent)


@jax.custom_vjp
def low(v):
    return lax.optimization_barrier(v.astype(jnp.bfloat16)).astype(jnp.float32)

@jax.custom_vjp
def low_back(v):
    return v

def low_keep(v):
    return (low(v), None)

def low_pass(kept, grad):
    return (grad,)

def back_keep(v):
    return (v, None)

def back_low(kept, grad):
    return (low(grad),)
low.defvjp(low_keep, low_pass)
low_back.defvjp(back_keep, back_low)

def stored_positions(length, groups):
    block_size = length // (2 * groups)
    stored = jnp.arange(length, dtype=jnp.int32)
    holder = stored // (2 * block_size)
    within = stored % (2 * block_size)
    second = within // block_size
    offset = within % block_size
    block_index = jnp.where(second == 0, holder, 2 * groups - 1 - holder)
    return (block_index * block_size + offset).astype(jnp.int32)

def normalize(values, gain, shift):
    center = lax.optimization_barrier(jnp.mean(values, -1, keepdims=True))
    centered = values - center
    variance = lax.optimization_barrier(jnp.mean(centered * centered, -1, keepdims=True))
    return centered * lax.rsqrt(variance + 1e-05) * gain + shift

def attend_block(query, query_pos, query_seg, keys, values, key_pos, key_seg):
    highest = lax.Precision.HIGHEST
    scores = jnp.einsum('qhd,khd->hqk', query, keys, precision=highest)
    scores = low_back(scores * 0.125)
    allowed = (key_pos[None, :] <= query_pos[:, None]) & (key_seg[None, :] == query_seg[:, None])
    scores = jnp.where(allowed[None], scores, -1e+30)
    weights = low(jax.nn.softmax(scores, axis=-1))
    return jnp.einsum('hqk,khd->qhd', weights, values, precision=highest)

def layer(inputs, seg_row, positions, params):
    highest = lax.Precision.HIGHEST
    gain_one, shift_one, proj_mixed, bias_query, bias_value, proj_out, bias_out, gain_two, shift_two, proj_up, bias_up, proj_down, bias_down = params
    length = inputs.shape[0]
    lowered_one = low(normalize(inputs, gain_one, shift_one))
    mixed = jnp.dot(lowered_one, proj_mixed, precision=highest)
    mixed = mixed + jnp.concatenate([bias_query, jnp.zeros_like(bias_query), bias_value])
    mixed = low_back(low(mixed))
    query = mixed[:, :D].reshape(length, H, HD)
    keys = mixed[:, D:2 * D].reshape(length, H, HD)
    values = mixed[:, 2 * D:].reshape(length, H, HD)
    block = min(512, length)
    count = length // block

    def one_block(item):
        return jax.checkpoint(attend_block)(item[0], item[1], item[2], keys, values, positions, seg_row)
    attended = lax.map(one_block, (query.reshape(count, block, H, HD), positions.reshape(count, block), seg_row.reshape(count, block)))
    attended = low_back(low(attended.reshape(length, D)))
    branch = low_back(jnp.dot(attended, proj_out, precision=highest) + bias_out)
    resid = inputs + branch
    lowered_two = low(normalize(resid, gain_two, shift_two))
    hidden = low_back(jnp.dot(lowered_two, proj_up, precision=highest) + bias_up)
    active = low(jax.nn.gelu(hidden, approximate=True))
    down = low_back(jnp.dot(active, proj_down, precision=highest) + bias_down)
    return resid + down

def reference(layer_input, segments, ln1_gain, ln1_bias, w_qkv, q_bias, v_bias, w_attn_out, b_attn_out, ln2_gain, ln2_bias, w_up, b_up, w_down, b_down, cotangent):
    params = tuple((p.astype(jnp.float32) for p in (ln1_gain, ln1_bias, w_qkv, q_bias, v_bias, w_attn_out, b_attn_out, ln2_gain, ln2_bias, w_up, b_up, w_down, b_down)))
    positions = stored_positions(SEQ_LEN, N_CTX)
    flat_input = layer_input.reshape(MB * SEQS, SEQ_LEN, D)
    flat_seg = segments.reshape(MB * SEQS, SEQ_LEN)
    flat_cot = cotangent.reshape(MB * SEQS, SEQ_LEN, D)
    start_totals = tuple((jnp.zeros_like(p) for p in params))

    def one(totals, item):
        inputs, seg_row, cots = item

        def forward(values_in, *weights):
            return layer(values_in, seg_row, positions, weights)
        outputs, pullback = jax.vjp(forward, inputs.astype(jnp.float32), *params)
        grads = pullback(cots.astype(jnp.float32))
        new_totals = tuple((total + grad for total, grad in zip(totals, grads[1:])))
        return (new_totals, (outputs.astype(jnp.bfloat16), grads[0].astype(jnp.bfloat16)))
    totals, (outs, back) = lax.scan(one, start_totals, (flat_input, flat_seg, flat_cot))
    activations = outs.reshape(MB, SEQS, SEQ_LEN, D)
    input_grad = back.reshape(MB, SEQS, SEQ_LEN, D)
    return (activations, input_grad, totals[0], totals[1], totals[2], totals[3], totals[4], totals[5], totals[6], totals[7], totals[8], totals[9], totals[10], totals[11], totals[12])
```

```python
import jax
import jax.numpy as jnp
from jax import lax
from jax.experimental import pallas as pl
from jax.experimental.pallas import tpu as pltpu
from jax.sharding import PartitionSpec as P

H = 12


def stored_positions(length, groups):
    block_size = length // (2 * groups)
    stored = jnp.arange(length, dtype=jnp.int32)
    holder = stored // (2 * block_size)
    within = stored % (2 * block_size)
    second = within // block_size
    offset = within % block_size
    block_index = jnp.where(second == 0, holder, 2 * groups - 1 - holder)
    return block_index * block_size + offset


def normalize_parts(values):
    center = jnp.mean(values, -1, keepdims=True)
    centered = values - center
    inverse = lax.rsqrt(jnp.mean(centered * centered, -1, keepdims=True) + 1e-05)
    return (centered * inverse, inverse)


def normalize_back(grad_normed, normed, inverse):
    first = jnp.mean(grad_normed, -1, keepdims=True)
    second = jnp.mean(grad_normed * normed, -1, keepdims=True)
    return inverse * (grad_normed - first - normed * second)


def tile_allowed(query_pos, query_seg, key_pos, key_seg):
    return (key_pos[None, :] <= query_pos[:, None]) & (key_seg[None, :] == query_seg[:, None])


def tile_scores(query, keys_tile, allowed):
    scores = (
        jnp.einsum("qhd,khd->hqk", query, keys_tile, preferred_element_type=jnp.float32) * 0.125
    )
    return jnp.where(allowed[None], scores, -1e30)


def online_softmax(query, query_pos, query_seg, tiles):
    heads = query.shape[1]
    count_rows = query.shape[0]

    def advance(carry, tile):
        keys_tile, values_tile, key_pos, key_seg = tile
        allowed = tile_allowed(query_pos, query_seg, key_pos, key_seg)

        def compute(state):
            peak, total, accum = state
            scores = tile_scores(query, keys_tile, allowed)
            new_peak = jnp.maximum(peak, jnp.max(scores, -1))
            terms = jnp.where(allowed[None], jnp.exp(scores - new_peak[..., None]), 0.0)
            factor = jnp.exp(peak - new_peak)
            upper = terms.astype(jnp.bfloat16)
            lower = (terms - upper.astype(jnp.float32)).astype(jnp.bfloat16)
            added = jnp.einsum(
                "hqk,khd->qhd", upper, values_tile, preferred_element_type=jnp.float32
            )
            added = added + jnp.einsum(
                "hqk,khd->qhd", lower, values_tile, preferred_element_type=jnp.float32
            )
            accum = accum * jnp.transpose(factor)[..., None] + added
            return (new_peak, total * factor + jnp.sum(terms, -1), accum)

        return (compute(carry), None)

    start_state = (
        jnp.full((heads, count_rows), -1e30, jnp.float32),
        jnp.zeros((heads, count_rows), jnp.float32),
        jnp.zeros(query.shape, jnp.float32),
    )
    (peak, total, accum), unused = lax.scan(advance, start_state, tiles)
    exact = accum / jnp.transpose(total)[..., None]
    return (peak + jnp.log(total), exact)


def attention_out(query, log_total, query_pos, query_seg, tiles):

    def advance(carry, tile):
        keys_tile, values_tile, key_pos, key_seg = tile
        allowed = tile_allowed(query_pos, query_seg, key_pos, key_seg)

        def compute(summed):
            scores = tile_scores(query, keys_tile, allowed)
            probs = jnp.where(allowed[None], jnp.exp(scores - log_total[..., None]), 0.0)
            lowered = probs.astype(jnp.bfloat16)
            return summed + jnp.einsum(
                "hqk,khd->qhd", lowered, values_tile, preferred_element_type=jnp.float32
            )

        return (compute(carry), None)

    summed, unused = lax.scan(advance, jnp.zeros(query.shape, jnp.float32), tiles)
    return summed


def attention_back(query, log_total, grad_attended, delta, query_pos, query_seg, tiles):

    def advance(grad_query, tile):
        keys_tile, values_tile, key_pos, key_seg = tile
        allowed = tile_allowed(query_pos, query_seg, key_pos, key_seg)

        def compute(carry_query):
            scores = tile_scores(query, keys_tile, allowed)
            probs = jnp.where(allowed[None], jnp.exp(scores - log_total[..., None]), 0.0)
            lowered = probs.astype(jnp.bfloat16)
            grad_values = jnp.einsum(
                "hqk,qhd->khd", lowered, grad_attended, preferred_element_type=jnp.float32
            )
            grad_probs = jnp.einsum(
                "qhd,khd->hqk", grad_attended, values_tile, preferred_element_type=jnp.float32
            )
            grad_scores = (probs * (grad_probs - delta[..., None])).astype(jnp.bfloat16)
            new_query = carry_query + 0.125 * jnp.einsum(
                "hqk,khd->qhd", grad_scores, keys_tile, preferred_element_type=jnp.float32
            )
            grad_keys = 0.125 * jnp.einsum(
                "hqk,qhd->khd", grad_scores, query, preferred_element_type=jnp.float32
            )
            return (new_query, grad_keys, grad_values)

        new_query, grad_keys, grad_values = compute(grad_query)
        return (new_query, (grad_keys, grad_values))

    grad_query, (grad_keys, grad_values) = lax.scan(
        advance, jnp.zeros(query.shape, jnp.float32), tiles
    )
    return (grad_query, grad_keys, grad_values)


def column_sums(values):
    return jnp.sum(values.astype(jnp.float32), 0)


def layer_pass(inputs, cots, seg_row, weights, positions, start):
    (
        gain_one,
        shift_one,
        proj_mixed,
        bias_query,
        bias_value,
        proj_out,
        bias_out,
        gain_two,
        shift_two,
        proj_up,
        bias_up,
        proj_down,
        bias_down,
    ) = weights
    count_rows = inputs.shape[0]
    width = inputs.shape[1]
    heads = H
    head_size = width // heads
    length = seg_row.shape[0]
    query_pos = lax.dynamic_slice_in_dim(positions, start, count_rows)
    query_seg = lax.dynamic_slice_in_dim(seg_row, start, count_rows)
    values_in = inputs.astype(jnp.float32)
    normed_one, inverse_one = normalize_parts(values_in)
    lowered_one = (
        normed_one * gain_one.astype(jnp.float32) + shift_one.astype(jnp.float32)
    ).astype(jnp.bfloat16)
    mixed_bias = jnp.concatenate(
        [
            bias_query.astype(jnp.float32),
            jnp.zeros((width,), jnp.float32),
            bias_value.astype(jnp.float32),
        ]
    )
    mixed = (
        jnp.dot(lowered_one, proj_mixed, preferred_element_type=jnp.float32) + mixed_bias
    ).astype(jnp.bfloat16)
    query = mixed[:, :width].reshape(count_rows, heads, head_size)
    keys_values = lax.all_gather(mixed[:, width:], "ctx", axis=0, tiled=True)
    block = min(512, length)
    count = length // block
    tiles = (
        keys_values[:, :width].reshape(count, block, heads, head_size),
        keys_values[:, width:].reshape(count, block, heads, head_size),
        positions.reshape(count, block),
        seg_row.reshape(count, block),
    )
    log_total, exact = online_softmax(query, query_pos, query_seg, tiles)
    summed = attention_out(query, log_total, query_pos, query_seg, tiles)
    attended = summed.reshape(count_rows, width).astype(jnp.bfloat16)
    branch = jnp.dot(attended, proj_out, preferred_element_type=jnp.float32) + bias_out.astype(
        jnp.float32
    )
    resid = values_in + branch
    normed_two, inverse_two = normalize_parts(resid)
    lowered_two = (
        normed_two * gain_two.astype(jnp.float32) + shift_two.astype(jnp.float32)
    ).astype(jnp.bfloat16)
    hidden = jnp.dot(lowered_two, proj_up, preferred_element_type=jnp.float32) + bias_up.astype(
        jnp.float32
    )

    def smooth(pre_active):
        return jax.nn.gelu(pre_active, approximate=True)

    active_full, gelu_back = jax.vjp(smooth, hidden)
    active = active_full.astype(jnp.bfloat16)
    down = jnp.dot(active, proj_down, preferred_element_type=jnp.float32) + bias_down.astype(
        jnp.float32
    )
    output = (resid + down).astype(jnp.bfloat16)
    grad_out = cots.astype(jnp.float32)
    grad_bias_down = column_sums(cots)
    grad_proj_down = jnp.einsum("tf,td->fd", active, cots, preferred_element_type=jnp.float32)
    grad_active = jnp.einsum("td,fd->tf", cots, proj_down, preferred_element_type=jnp.float32)
    grad_hidden = gelu_back(grad_active)[0].astype(jnp.bfloat16)
    grad_bias_up = column_sums(grad_hidden)
    grad_proj_up = jnp.einsum(
        "td,tf->df", lowered_two, grad_hidden, preferred_element_type=jnp.float32
    )
    grad_lowered_two = jnp.einsum(
        "tf,df->td", grad_hidden, proj_up, preferred_element_type=jnp.float32
    )
    grad_gain_two = jnp.sum(grad_lowered_two * normed_two, 0)
    grad_shift_two = jnp.sum(grad_lowered_two, 0)
    grad_resid = grad_out + normalize_back(
        grad_lowered_two * gain_two.astype(jnp.float32), normed_two, inverse_two
    )
    grad_branch = grad_resid.astype(jnp.bfloat16)
    grad_bias_out = column_sums(grad_branch)
    grad_proj_out = jnp.einsum(
        "td,te->de", attended, grad_branch, preferred_element_type=jnp.float32
    )
    grad_attended = jnp.einsum(
        "te,de->td", grad_branch, proj_out, preferred_element_type=jnp.float32
    ).astype(jnp.bfloat16)
    grad_attended = grad_attended.reshape(count_rows, heads, head_size)
    delta = jnp.einsum("qhd,qhd->hq", grad_attended.astype(jnp.float32), exact)
    grad_query, grad_keys, grad_values = attention_back(
        query, log_total, grad_attended, delta, query_pos, query_seg, tiles
    )
    grad_pairs = jnp.concatenate(
        [grad_keys.reshape(length, width), grad_values.reshape(length, width)], 1
    )
    grad_pairs_local = lax.psum_scatter(grad_pairs, "ctx", scatter_dimension=0, tiled=True)
    grad_mixed = jnp.concatenate(
        [grad_query.reshape(count_rows, width), grad_pairs_local], 1
    ).astype(jnp.bfloat16)
    grad_bias_query = column_sums(grad_mixed[:, :width])
    grad_bias_value = column_sums(grad_mixed[:, 2 * width :])
    grad_proj_mixed = jnp.einsum(
        "td,te->de", lowered_one, grad_mixed, preferred_element_type=jnp.float32
    )
    grad_lowered_one = jnp.einsum(
        "te,de->td", grad_mixed, proj_mixed, preferred_element_type=jnp.float32
    )
    grad_gain_one = jnp.sum(grad_lowered_one * normed_one, 0)
    grad_shift_one = jnp.sum(grad_lowered_one, 0)
    grad_input = grad_resid + normalize_back(
        grad_lowered_one * gain_one.astype(jnp.float32), normed_one, inverse_one
    )
    grads = (
        grad_gain_one,
        grad_shift_one,
        grad_proj_mixed,
        grad_bias_query,
        grad_bias_value,
        grad_proj_out,
        grad_bias_out,
        grad_gain_two,
        grad_shift_two,
        grad_proj_up,
        grad_bias_up,
        grad_proj_down,
        grad_bias_down,
    )
    return (output, grad_input.astype(jnp.bfloat16), grads)


def fetch(shards):
    return (
        lax.all_gather(shards[0], "fsdp", axis=0, tiled=True),
        lax.all_gather(shards[1], "fsdp", axis=0, tiled=True),
        lax.all_gather(shards[2], "fsdp", axis=0, tiled=True),
        lax.all_gather(shards[3], "fsdp", axis=0, tiled=True),
        lax.all_gather(shards[4], "fsdp", axis=0, tiled=True),
        lax.all_gather(shards[5], "fsdp", axis=0, tiled=True),
        lax.all_gather(shards[6], "fsdp", axis=0, tiled=True),
        lax.all_gather(shards[7], "fsdp", axis=0, tiled=True),
        lax.all_gather(shards[8], "fsdp", axis=0, tiled=True),
        lax.all_gather(shards[9], "fsdp", axis=0, tiled=True),
        lax.all_gather(shards[10], "fsdp", axis=0, tiled=True),
        lax.all_gather(shards[11], "fsdp", axis=0, tiled=True),
        lax.all_gather(shards[12], "fsdp", axis=0, tiled=True),
    )


def share(grads):
    return (
        lax.psum_scatter(grads[0], "fsdp", scatter_dimension=0, tiled=True),
        lax.psum_scatter(grads[1], "fsdp", scatter_dimension=0, tiled=True),
        lax.psum_scatter(grads[2], "fsdp", scatter_dimension=0, tiled=True),
        lax.psum_scatter(grads[3], "fsdp", scatter_dimension=0, tiled=True),
        lax.psum_scatter(grads[4], "fsdp", scatter_dimension=0, tiled=True),
        lax.psum_scatter(grads[5], "fsdp", scatter_dimension=0, tiled=True),
        lax.psum_scatter(grads[6], "fsdp", scatter_dimension=0, tiled=True),
        lax.psum_scatter(grads[7], "fsdp", scatter_dimension=0, tiled=True),
        lax.psum_scatter(grads[8], "fsdp", scatter_dimension=0, tiled=True),
        lax.psum_scatter(grads[9], "fsdp", scatter_dimension=0, tiled=True),
        lax.psum_scatter(grads[10], "fsdp", scatter_dimension=0, tiled=True),
        lax.psum_scatter(grads[11], "fsdp", scatter_dimension=0, tiled=True),
        lax.psum_scatter(grads[12], "fsdp", scatter_dimension=0, tiled=True),
    )


def on_device(
    layer_input,
    segments,
    ln1_gain,
    ln1_bias,
    w_qkv,
    q_bias,
    v_bias,
    w_attn_out,
    b_attn_out,
    ln2_gain,
    ln2_bias,
    w_up,
    b_up,
    w_down,
    b_down,
    cotangent,
):
    shards = (
        ln1_gain,
        ln1_bias,
        w_qkv,
        q_bias,
        v_bias,
        w_attn_out,
        b_attn_out,
        ln2_gain,
        ln2_bias,
        w_up,
        b_up,
        w_down,
        b_down,
    )
    micro = layer_input.shape[0]
    count_rows = layer_input.shape[2]
    length = segments.shape[2]
    positions = stored_positions(length, lax.axis_size("ctx"))
    start = lax.axis_index("ctx") * count_rows
    outputs = []
    input_grads = []
    shared = None
    for number in range(micro):
        weights = fetch(shards)
        output, grad_input, grads = layer_pass(
            layer_input[number, 0],
            cotangent[number, 0],
            segments[number, 0],
            weights,
            positions,
            start,
        )
        summed = share(grads)
        shared = summed if shared is None else jax.tree.map(jnp.add, shared, summed)
        outputs.append(output)
        input_grads.append(grad_input)
    final = lax.psum(
        (
            shared[0],
            shared[1],
            shared[2],
            shared[3],
            shared[4],
            shared[5],
            shared[6],
            shared[7],
            shared[8],
            shared[9],
            shared[10],
            shared[11],
            shared[12],
        ),
        "ctx",
    )
    activations = jnp.stack(outputs)[:, None]
    input_grad = jnp.stack(input_grads)[:, None]
    return (
        activations,
        input_grad,
        final[0],
        final[1],
        final[2],
        final[3],
        final[4],
        final[5],
        final[6],
        final[7],
        final[8],
        final[9],
        final[10],
        final[11],
        final[12],
    )


D = 768
HD = 64
BLK = 256
NEG = -1e30
F32 = jnp.float32
BF16 = jnp.bfloat16


def dot(lhs, rhs, lhs_dim, rhs_dim):
    return lax.dot_general(
        lhs, rhs, (((lhs_dim,), (rhs_dim,)), ((), ())), preferred_element_type=F32
    )


def norm(v):
    center = v - jnp.mean(v, -1, keepdims=True)
    inverse = lax.rsqrt(jnp.mean(center * center, -1, keepdims=True) + 1e-05)
    return center * inverse, inverse


def colsum(v):
    return jnp.sum(v, 0, keepdims=True)


def loop(count, body):
    def step(index, carry):
        body(index)
        return carry

    lax.fori_loop(0, count, step, 0)


def lanes(index, size):
    return pl.ds(pl.multiple_of(index * size, size), size)


def attention_masks(seg_ref, bias_ref, mine):
    key = lax.broadcasted_iota(jnp.int32, (BLK, BLK), 0)
    query = lax.broadcasted_iota(jnp.int32, (BLK, BLK), 1)
    causal = key <= query
    for micro in range(2):

        def row(start):
            piece = seg_ref[micro : micro + 1, pl.ds(pl.multiple_of(start, BLK), BLK)]
            return jnp.broadcast_to(piece.astype(F32), (BLK, BLK))

        solo = row(mine * 2 * BLK + mine * BLK)
        wide = row(mine * 2 * BLK + (1 - mine) * BLK)
        extra = row((1 - mine) * 3 * BLK)
        bias_ref[micro, 0:BLK] = jnp.where((solo.T == solo) & causal, 0.0, NEG)
        bias_ref[micro, BLK : 2 * BLK] = jnp.where(extra.T == wide, 0.0, NEG)
        bias_ref[micro, 2 * BLK :] = jnp.where((wide.T == wide) & causal, 0.0, NEG)


def attention_rows(micro, mine):
    solo = pl.ds(pl.multiple_of(micro * 2 * BLK + mine * BLK, BLK), BLK)
    wide = pl.ds(pl.multiple_of(micro * 2 * BLK + (1 - mine) * BLK, BLK), BLK)
    extra = pl.ds(pl.multiple_of(1024 + micro * BLK, BLK), BLK)
    return solo, wide, extra


def halves(value):
    left = lax.broadcasted_iota(jnp.int32, value.shape, 1) < HD
    zero = jnp.zeros_like(value)
    return jnp.where(left, value, zero), jnp.where(left, zero, value)


def softmax_columns(tiles):
    peak = tiles[0].max(0, keepdims=True)
    for tile in tiles[1:]:
        peak = jnp.maximum(peak, tile.max(0, keepdims=True))
    terms = [jnp.exp(tile - peak) for tile in tiles]
    total = colsum(terms[0])
    for term in terms[1:]:
        total = total + colsum(term)
    scale = 1.0 / total
    return [(term * scale).astype(BF16) for term in terms]


def attention_forward(index, refs, mine):
    q_ref, k_ref, v_ref, o_ref, p_ref, bias_ref = refs
    micro = index // 6
    pair = lanes(index % 6, 128)
    solo, wide, extra = attention_rows(micro, mine)
    k_s, k_x, k_e = k_ref[solo, pair], k_ref[wide, pair], k_ref[extra, pair]
    vt_s, vt_x, vt_e = v_ref[solo, pair].T, v_ref[wide, pair].T, v_ref[extra, pair].T
    q_s, q_x = halves(q_ref[solo, pair]), halves(q_ref[wide, pair])
    outs_s, outs_x = [], []
    for head in range(2):
        rows = slice(head * HD, head * HD + HD)
        (p_s,) = softmax_columns([dot(k_s, q_s[head], 1, 1) + bias_ref[micro, 0:BLK]])
        p_e, p_x = softmax_columns(
            [
                dot(k_e, q_x[head], 1, 1) + bias_ref[micro, BLK : 2 * BLK],
                dot(k_x, q_x[head], 1, 1) + bias_ref[micro, 2 * BLK :],
            ]
        )
        p_ref[index, head, 0:BLK] = p_s
        p_ref[index, head, BLK : 2 * BLK] = p_e
        p_ref[index, head, 2 * BLK :] = p_x
        outs_s.append(dot(vt_s[rows], p_s, 1, 0))
        outs_x.append(dot(vt_e[rows], p_e, 1, 0) + dot(vt_x[rows], p_x, 1, 0))
    o_ref[solo, pair] = jnp.concatenate(outs_s, 0).T.astype(BF16)
    o_ref[wide, pair] = jnp.concatenate(outs_x, 0).T.astype(BF16)


def attention_backward(index, refs, mine):
    q_ref, k_ref, v_ref, go_ref, p_ref = refs
    micro = index // 6
    pair = lanes(index % 6, 128)
    solo, wide, extra = attention_rows(micro, mine)
    k_s, k_x, k_e = k_ref[solo, pair], k_ref[wide, pair], k_ref[extra, pair]
    v_s, v_x, v_e = v_ref[solo, pair], v_ref[wide, pair], v_ref[extra, pair]
    kt_s, kt_x, kt_e = k_s.T, k_x.T, k_e.T
    q_s, q_x = halves(q_ref[solo, pair]), halves(q_ref[wide, pair])
    go_s, go_x = halves(go_ref[solo, pair]), halves(go_ref[wide, pair])
    p_all, g_all, outs_s, outs_x = [], [], [], []
    for head in range(2):
        rows = slice(head * HD, head * HD + HD)
        p_s, p_e, p_x = (p_ref[index, head, BLK * t : BLK * t + BLK] for t in range(3))
        f_s, f_e, f_x = p_s.astype(F32), p_e.astype(F32), p_x.astype(F32)
        t_s = f_s * dot(v_s, go_s[head], 1, 1)
        t_e = f_e * dot(v_e, go_x[head], 1, 1)
        t_x = f_x * dot(v_x, go_x[head], 1, 1)
        d_s = colsum(t_s)
        d_x = colsum(t_e) + colsum(t_x)
        g_s = (t_s - f_s * d_s).astype(BF16)
        g_e = (t_e - f_e * d_x).astype(BF16)
        g_x = (t_x - f_x * d_x).astype(BF16)
        outs_s.append(dot(kt_s[rows], g_s, 1, 0))
        outs_x.append(dot(kt_e[rows], g_e, 1, 0) + dot(kt_x[rows], g_x, 1, 0))
        p_all.append((p_s, p_e, p_x))
        g_all.append((g_s, g_e, g_x))

    def both(tiles, which, right):
        return dot(jnp.concatenate([tiles[0][which], tiles[1][which]], 1), right, 1, 0).astype(BF16)

    go_s, go_x = jnp.concatenate(go_s, 0), jnp.concatenate(go_x, 0)
    q_s, q_x = jnp.concatenate(q_s, 0), jnp.concatenate(q_x, 0)
    v_ref[solo, pair] = both(p_all, 0, go_s)
    v_ref[extra, pair] = both(p_all, 1, go_x)
    v_ref[wide, pair] = both(p_all, 2, go_x)
    k_ref[solo, pair] = both(g_all, 0, q_s)
    k_ref[extra, pair] = both(g_all, 1, q_x)
    k_ref[wide, pair] = both(g_all, 2, q_x)
    q_ref[solo, pair] = (jnp.concatenate(outs_s, 0).T * 0.125).astype(BF16)
    q_ref[wide, pair] = (jnp.concatenate(outs_x, 0).T * 0.125).astype(BF16)


def layer_kernel(
    x_hbm, xe_hbm, cot_hbm, seg_ref, w_hbm, vec_ref, act_hbm, g1_hbm, gr_hbm, g1e_hbm, g_hbm, vg_hbm,
    w_ref, x_ref, cot_ref, q_ref, k_ref, v_ref, o_ref, p_ref, bias_ref, acc_ref, n2_ref, a2_ref, rs2_ref,
    g2_ref, a1_ref, a3_ref, gu_ref, vg_ref, bup_ref, sem,
):
    mine = lax.axis_index("ctx")
    for i, (src, dst) in enumerate(
        ((x_hbm, x_ref.at[0:1024]), (xe_hbm, x_ref.at[1024:1536]), (cot_hbm, cot_ref), (w_hbm, w_ref))
    ):
        pltpu.make_async_copy(src, dst, sem.at[i]).start()
    for i, (src, dst) in enumerate(
        ((x_hbm, x_ref.at[0:1024]), (xe_hbm, x_ref.at[1024:1536]), (cot_hbm, cot_ref), (w_hbm, w_ref))
    ):
        pltpu.make_async_copy(src, dst, sem.at[i]).wait()

    def weight(index):
        return w_ref[index].reshape(D, D)

    def vec(row):
        return vec_ref[row : row + 1, :].astype(F32)

    vg_ref[...] = jnp.zeros_like(vg_ref)

    def add_vec(row, value):
        vg_ref[row : row + 1, :] += value

    def first_norm(r):
        rows = pl.ds(r * BLK, BLK)
        normed, _ = norm(x_ref[rows, :].astype(F32))
        a1_ref[rows, :] = (normed * vec(0) + vec(1)).astype(BF16)

    loop(6, first_norm)
    attention_masks(seg_ref, bias_ref, mine)
    k_ref[...] = dot(a1_ref[...], weight(1), 1, 0).astype(BF16)
    v_ref[...] = (dot(a1_ref[...], weight(2), 1, 0) + vec(3)).astype(BF16)
    q_ref[...] = ((dot(a1_ref[0:1024, :], weight(0), 1, 0) + vec(2)).astype(BF16) * 0.125).astype(BF16)
    loop(12, lambda i: attention_forward(i, (q_ref, k_ref, v_ref, o_ref, p_ref, bias_ref), mine))

    acc_ref[...] = dot(o_ref[...], weight(3), 1, 0)

    def second_norm(r):
        rows = pl.ds(r * BLK, BLK)
        resid = acc_ref[rows, :] + x_ref[rows, :].astype(F32) + vec(4)
        normed, inverse = norm(resid)
        acc_ref[rows, :] = resid + vec(7)
        n2_ref[rows, :] = normed.astype(BF16)
        a2_ref[rows, :] = (normed * vec(5) + vec(6)).astype(BF16)
        rs2_ref[rows, :] = jnp.broadcast_to(inverse, (BLK, 128))
        add_vec(7, colsum(cot_ref[rows, :].astype(F32)))
        g2_ref[rows, :] = jnp.zeros((BLK, D), F32)

    loop(4, second_norm)

    def feed(j):
        up, down = 4 + j, 8 + j
        bias = bup_ref[j, 0:1]

        def part(r):
            rows = pl.ds(r * 512, 512)
            u = dot(a2_ref[rows, :], weight(up), 1, 0) + bias
            back = dot(cot_ref[rows, :], weight(down), 1, 1)
            square = u * u
            th = jnp.tanh(u * (0.7978845608028654 + 0.035677408136300125 * square))
            half = 0.5 + 0.5 * th
            a3_ref[rows, :] = (u * half).astype(BF16)
            slope = half + (half * (1.0 - th)) * (u * (0.7978845608028654 + 0.10703222440890037 * square))
            gu = (back * slope).astype(BF16)
            gu_ref[rows, :] = gu
            bup_ref[j, 1:2] += colsum(gu.astype(F32))

        loop(2, part)
        acc_ref[...] += dot(a3_ref[...], weight(down), 1, 0)
        g2_ref[...] += dot(gu_ref[...], weight(up), 1, 1)
        w_ref[down] = dot(a3_ref[...], cot_ref[...], 0, 0).astype(BF16).reshape(4, 4, 48, D)
        w_ref[up] = dot(a2_ref[...], gu_ref[...], 0, 0).astype(BF16).reshape(4, 4, 48, D)

    for j in range(4):
        bup_ref[j, 0:1] = vec(8 + j)
        bup_ref[j, 1:2] = jnp.zeros((1, D), F32)
    loop(4, feed)
    for j in range(4):
        vg_ref[8 + j : 9 + j, :] = bup_ref[j, 1:2]

    def second_back(r):
        rows = pl.ds(r * BLK, BLK)
        a3_ref[rows, :] = acc_ref[rows, :].astype(BF16)
        g2 = g2_ref[rows, :]
        normed = n2_ref[rows, :].astype(F32)
        add_vec(5, colsum(g2 * normed))
        add_vec(6, colsum(g2))
        t = g2 * vec(5)
        first = jnp.mean(t, -1, keepdims=True)
        second = jnp.mean(t * normed, -1, keepdims=True)
        grad = cot_ref[rows, :].astype(F32) + rs2_ref[rows, 0:1] * (t - first - normed * second)
        g2_ref[rows, :] = grad
        lowered = grad.astype(BF16)
        a2_ref[rows, :] = lowered
        add_vec(4, colsum(lowered.astype(F32)))

    loop(4, second_back)
    out_copy = pltpu.make_async_copy(a3_ref, act_hbm, sem.at[0])
    out_copy.start()
    gu_ref[...] = dot(a2_ref[...], weight(3), 1, 1).astype(BF16)
    w_ref[3] = dot(o_ref[...], a2_ref[...], 0, 0).astype(BF16).reshape(4, 4, 48, D)
    loop(12, lambda i: attention_backward(i, (q_ref, k_ref, v_ref, gu_ref, p_ref), mine))

    add_vec(2, colsum(q_ref[...].astype(F32)))
    add_vec(3, colsum(v_ref[...].astype(F32)))
    out_copy.wait()
    g1e = dot(k_ref[1024:1536, :], weight(1), 1, 1) + dot(v_ref[1024:1536, :], weight(2), 1, 1)
    a3_ref[0:512, :] = g1e.astype(BF16)
    acc_ref[...] = dot(q_ref[...], weight(0), 1, 1)
    acc_ref[...] += dot(k_ref[0:1024, :], weight(1), 1, 1)
    acc_ref[...] += dot(v_ref[0:1024, :], weight(2), 1, 1)
    w_ref[0] = dot(a1_ref[0:1024, :], q_ref[...], 0, 0).astype(BF16).reshape(4, 4, 48, D)
    w_ref[1] = dot(a1_ref[...], k_ref[...], 0, 0).astype(BF16).reshape(4, 4, 48, D)
    w_ref[2] = dot(a1_ref[...], v_ref[...], 0, 0).astype(BF16).reshape(4, 4, 48, D)

    def extra_back(r):
        rows = pl.ds(1024 + r * BLK, BLK)
        normed, _ = norm(x_ref[rows, :].astype(F32))
        g1 = a3_ref[pl.ds(r * BLK, BLK), :].astype(F32)
        add_vec(0, colsum(g1 * normed))
        add_vec(1, colsum(g1))

    loop(2, extra_back)

    def first_back(r):
        rows = pl.ds(r * BLK, BLK)
        normed, inverse = norm(x_ref[rows, :].astype(F32))
        g1 = acc_ref[rows, :]
        add_vec(0, colsum(g1 * normed))
        add_vec(1, colsum(g1))

    loop(4, first_back)
    pairs = ((acc_ref, g1_hbm), (g2_ref, gr_hbm), (a3_ref.at[0:512], g1e_hbm), (w_ref, g_hbm), (vg_ref, vg_hbm))
    for i, (src, dst) in enumerate(pairs):
        pltpu.make_async_copy(src, dst, sem.at[i]).start()
    for i, (src, dst) in enumerate(pairs):
        pltpu.make_async_copy(src, dst, sem.at[i]).wait()


def fast_device(
    layer_input, segments, ln1_gain, ln1_bias, w_qkv, q_bias, v_bias, w_attn_out, b_attn_out,
    ln2_gain, ln2_bias, w_up, b_up, w_down, b_down, cotangent,
):
    mine = lax.axis_index("ctx")
    x = layer_input.reshape(1024, D)
    cot = cotangent.reshape(1024, D)
    seg = segments.reshape(2, 1024)
    own = lax.dynamic_slice_in_dim(x.reshape(2, 512, D), mine * BLK, BLK, 1)
    extra = lax.ppermute(own, "ctx", ((0, 1), (1, 0))).reshape(512, D)

    def gather(v):
        return lax.all_gather(v, "fsdp", axis=0, tiled=True)

    qkv, up = gather(w_qkv), gather(w_up)
    blocks = [qkv[:, D * i : D * i + D] for i in range(3)] + [gather(w_attn_out)]
    blocks += [up[:, D * i : D * i + D] for i in range(4)]
    w = jnp.concatenate([jnp.stack(blocks), gather(w_down).reshape(4, D, D)]).reshape(12, 4, 4, 48, D)
    rows = [ln1_gain, ln1_bias, q_bias, v_bias, b_attn_out, ln2_gain, ln2_bias, b_down]
    vec = jnp.concatenate(
        [jnp.stack([gather(v) for v in rows]), gather(b_up).reshape(4, D), jnp.zeros((4, D), BF16)]
    )
    big = lambda *shape, dtype=BF16: jax.ShapeDtypeStruct(shape, dtype)
    hbm = pl.BlockSpec(memory_space=pltpu.HBM)
    vmem = pl.BlockSpec(memory_space=pltpu.VMEM)
    act, g1, gr, g1e, g, vg = pl.pallas_call(
        layer_kernel,
        out_shape=(
            big(1024, D), big(1024, D, dtype=F32), big(1024, D, dtype=F32), big(512, D),
            big(12, 4, 4, 48, D), big(16, D, dtype=F32),
        ),
        in_specs=[hbm, hbm, hbm, vmem, hbm, vmem],
        out_specs=(hbm,) * 6,
        scratch_shapes=[
            pltpu.VMEM((12, 4, 4, 48, D), BF16),
            pltpu.VMEM((1536, D), BF16),
            pltpu.VMEM((1024, D), BF16),
            pltpu.VMEM((1024, D), BF16),
            pltpu.VMEM((1536, D), BF16),
            pltpu.VMEM((1536, D), BF16),
            pltpu.VMEM((1024, D), BF16),
            pltpu.VMEM((12, 2, 3 * BLK, BLK), BF16),
            pltpu.VMEM((2, 3 * BLK, BLK), F32),
            pltpu.VMEM((1024, D), F32),
            pltpu.VMEM((1024, D), BF16),
            pltpu.VMEM((1024, D), BF16),
            pltpu.VMEM((1024, 128), F32),
            pltpu.VMEM((1024, D), F32),
            pltpu.VMEM((1536, D), BF16),
            pltpu.VMEM((1024, D), BF16),
            pltpu.VMEM((1024, D), BF16),
            pltpu.VMEM((16, D), F32),
            pltpu.VMEM((4, 8, D), F32),
            pltpu.SemaphoreType.DMA((8,)),
        ],
        compiler_params=pltpu.CompilerParams(vmem_limit_bytes=63_000_000),
        name="layer",
    )(x, extra, cot, seg, w, vec)
    back = lax.ppermute(g1e.astype(F32), "ctx", ((0, 1), (1, 0))).reshape(2, BLK, D)
    g1 = g1.reshape(2, 512, D)
    mid = lax.dynamic_slice_in_dim(g1, mine * BLK, BLK, 1) + back
    g1 = lax.dynamic_update_slice_in_dim(g1, mid, mine * BLK, 1).reshape(1024, D)
    normed, inverse = normalize_parts(x.astype(F32))
    gx = (gr + normalize_back(g1 * vec[0].astype(F32), normed, inverse)).astype(BF16)
    g = g.astype(F32).reshape(12, D, D)

    def scatter(v):
        return lax.psum(lax.psum_scatter(v, "fsdp", scatter_dimension=0, tiled=True), "ctx")

    g_qkv = scatter(jnp.concatenate([g[0], g[1], g[2]], 1))
    g_out = scatter(g[3])
    g_up = scatter(jnp.concatenate([g[4], g[5], g[6], g[7]], 1))
    g_down = scatter(g[8:].reshape(4 * D, D))
    sums = lax.psum(vg, ("ctx", "fsdp"))
    f = lax.axis_index("fsdp")
    part = lambda i: lax.dynamic_slice_in_dim(sums[i], f * 48, 48)
    g_bup = lax.dynamic_slice_in_dim(sums[8:12].reshape(4 * D), f * 192, 192)
    return (
        act.reshape(2, 1, 512, D), gx.reshape(2, 1, 512, D), part(0), part(1), g_qkv, part(2), part(3),
        g_out, part(4), part(5), part(6), g_up, g_bup, g_down, part(7),
    )


def solution(mesh):
    in_specs = (
        P(None, "fsdp", "ctx", None),
        P(None, "fsdp", None),
        P("fsdp"),
        P("fsdp"),
        P("fsdp", None),
        P("fsdp"),
        P("fsdp"),
        P("fsdp", None),
        P("fsdp"),
        P("fsdp"),
        P("fsdp"),
        P("fsdp", None),
        P("fsdp"),
        P("fsdp", None),
        P("fsdp"),
        P(None, "fsdp", "ctx", None),
    )
    out_specs = (
        P(None, "fsdp", "ctx", None),
        P(None, "fsdp", "ctx", None),
        P("fsdp"),
        P("fsdp"),
        P("fsdp", None),
        P("fsdp"),
        P("fsdp"),
        P("fsdp", None),
        P("fsdp"),
        P("fsdp"),
        P("fsdp"),
        P("fsdp", None),
        P("fsdp"),
        P("fsdp", None),
        P("fsdp"),
    )
    fast = mesh.shape["ctx"] == 2 and mesh.shape["fsdp"] == 16
    return jax.shard_map(
        fast_device if fast else on_device, mesh=mesh, in_specs=in_specs, out_specs=out_specs, check_vma=False
    )
```

```python
import jax
import jax.numpy as jnp
from jax import lax
from jax.experimental import pallas as pl
from jax.experimental.pallas import tpu as pltpu
from jax.sharding import PartitionSpec as P

H = 12


def stored_positions(length, groups):
    block_size = length // (2 * groups)
    stored = jnp.arange(length, dtype=jnp.int32)
    holder = stored // (2 * block_size)
    within = stored % (2 * block_size)
    second = within // block_size
    offset = within % block_size
    block_index = jnp.where(second == 0, holder, 2 * groups - 1 - holder)
    return block_index * block_size + offset


def normalize_parts(values):
    center = jnp.mean(values, -1, keepdims=True)
    centered = values - center
    inverse = lax.rsqrt(jnp.mean(centered * centered, -1, keepdims=True) + 1e-05)
    return (centered * inverse, inverse)


def normalize_back(grad_normed, normed, inverse):
    first = jnp.mean(grad_normed, -1, keepdims=True)
    second = jnp.mean(grad_normed * normed, -1, keepdims=True)
    return inverse * (grad_normed - first - normed * second)


def tile_allowed(query_pos, query_seg, key_pos, key_seg):
    return (key_pos[None, :] <= query_pos[:, None]) & (key_seg[None, :] == query_seg[:, None])


def tile_scores(query, keys_tile, allowed):
    scores = (
        jnp.einsum("qhd,khd->hqk", query, keys_tile, preferred_element_type=jnp.float32) * 0.125
    )
    return jnp.where(allowed[None], scores, -1e30)


def online_softmax(query, query_pos, query_seg, tiles):
    heads = query.shape[1]
    count_rows = query.shape[0]

    def advance(carry, tile):
        keys_tile, values_tile, key_pos, key_seg = tile
        allowed = tile_allowed(query_pos, query_seg, key_pos, key_seg)

        def compute(state):
            peak, total, accum = state
            scores = tile_scores(query, keys_tile, allowed)
            new_peak = jnp.maximum(peak, jnp.max(scores, -1))
            terms = jnp.where(allowed[None], jnp.exp(scores - new_peak[..., None]), 0.0)
            factor = jnp.exp(peak - new_peak)
            upper = terms.astype(jnp.bfloat16)
            lower = (terms - upper.astype(jnp.float32)).astype(jnp.bfloat16)
            added = jnp.einsum(
                "hqk,khd->qhd", upper, values_tile, preferred_element_type=jnp.float32
            )
            added = added + jnp.einsum(
                "hqk,khd->qhd", lower, values_tile, preferred_element_type=jnp.float32
            )
            accum = accum * jnp.transpose(factor)[..., None] + added
            return (new_peak, total * factor + jnp.sum(terms, -1), accum)

        return (compute(carry), None)

    start_state = (
        jnp.full((heads, count_rows), -1e30, jnp.float32),
        jnp.zeros((heads, count_rows), jnp.float32),
        jnp.zeros(query.shape, jnp.float32),
    )
    (peak, total, accum), unused = lax.scan(advance, start_state, tiles)
    exact = accum / jnp.transpose(total)[..., None]
    return (peak + jnp.log(total), exact)


def attention_out(query, log_total, query_pos, query_seg, tiles):

    def advance(carry, tile):
        keys_tile, values_tile, key_pos, key_seg = tile
        allowed = tile_allowed(query_pos, query_seg, key_pos, key_seg)

        def compute(summed):
            scores = tile_scores(query, keys_tile, allowed)
            probs = jnp.where(allowed[None], jnp.exp(scores - log_total[..., None]), 0.0)
            lowered = probs.astype(jnp.bfloat16)
            return summed + jnp.einsum(
                "hqk,khd->qhd", lowered, values_tile, preferred_element_type=jnp.float32
            )

        return (compute(carry), None)

    summed, unused = lax.scan(advance, jnp.zeros(query.shape, jnp.float32), tiles)
    return summed


def attention_back(query, log_total, grad_attended, delta, query_pos, query_seg, tiles):

    def advance(grad_query, tile):
        keys_tile, values_tile, key_pos, key_seg = tile
        allowed = tile_allowed(query_pos, query_seg, key_pos, key_seg)

        def compute(carry_query):
            scores = tile_scores(query, keys_tile, allowed)
            probs = jnp.where(allowed[None], jnp.exp(scores - log_total[..., None]), 0.0)
            lowered = probs.astype(jnp.bfloat16)
            grad_values = jnp.einsum(
                "hqk,qhd->khd", lowered, grad_attended, preferred_element_type=jnp.float32
            )
            grad_probs = jnp.einsum(
                "qhd,khd->hqk", grad_attended, values_tile, preferred_element_type=jnp.float32
            )
            grad_scores = (probs * (grad_probs - delta[..., None])).astype(jnp.bfloat16)
            new_query = carry_query + 0.125 * jnp.einsum(
                "hqk,khd->qhd", grad_scores, keys_tile, preferred_element_type=jnp.float32
            )
            grad_keys = 0.125 * jnp.einsum(
                "hqk,qhd->khd", grad_scores, query, preferred_element_type=jnp.float32
            )
            return (new_query, grad_keys, grad_values)

        new_query, grad_keys, grad_values = compute(grad_query)
        return (new_query, (grad_keys, grad_values))

    grad_query, (grad_keys, grad_values) = lax.scan(
        advance, jnp.zeros(query.shape, jnp.float32), tiles
    )
    return (grad_query, grad_keys, grad_values)


def column_sums(values):
    return jnp.sum(values.astype(jnp.float32), 0)


def layer_pass(inputs, cots, seg_row, weights, positions, start):
    (
        gain_one,
        shift_one,
        proj_mixed,
        bias_query,
        bias_value,
        proj_out,
        bias_out,
        gain_two,
        shift_two,
        proj_up,
        bias_up,
        proj_down,
        bias_down,
    ) = weights
    count_rows = inputs.shape[0]
    width = inputs.shape[1]
    heads = H
    head_size = width // heads
    length = seg_row.shape[0]
    query_pos = lax.dynamic_slice_in_dim(positions, start, count_rows)
    query_seg = lax.dynamic_slice_in_dim(seg_row, start, count_rows)
    values_in = inputs.astype(jnp.float32)
    normed_one, inverse_one = normalize_parts(values_in)
    lowered_one = (
        normed_one * gain_one.astype(jnp.float32) + shift_one.astype(jnp.float32)
    ).astype(jnp.bfloat16)
    mixed_bias = jnp.concatenate(
        [
            bias_query.astype(jnp.float32),
            jnp.zeros((width,), jnp.float32),
            bias_value.astype(jnp.float32),
        ]
    )
    mixed = (
        jnp.dot(lowered_one, proj_mixed, preferred_element_type=jnp.float32) + mixed_bias
    ).astype(jnp.bfloat16)
    query = mixed[:, :width].reshape(count_rows, heads, head_size)
    keys_values = lax.all_gather(mixed[:, width:], "ctx", axis=0, tiled=True)
    block = min(512, length)
    count = length // block
    tiles = (
        keys_values[:, :width].reshape(count, block, heads, head_size),
        keys_values[:, width:].reshape(count, block, heads, head_size),
        positions.reshape(count, block),
        seg_row.reshape(count, block),
    )
    log_total, exact = online_softmax(query, query_pos, query_seg, tiles)
    summed = attention_out(query, log_total, query_pos, query_seg, tiles)
    attended = summed.reshape(count_rows, width).astype(jnp.bfloat16)
    branch = jnp.dot(attended, proj_out, preferred_element_type=jnp.float32) + bias_out.astype(
        jnp.float32
    )
    resid = values_in + branch
    normed_two, inverse_two = normalize_parts(resid)
    lowered_two = (
        normed_two * gain_two.astype(jnp.float32) + shift_two.astype(jnp.float32)
    ).astype(jnp.bfloat16)
    hidden = jnp.dot(lowered_two, proj_up, preferred_element_type=jnp.float32) + bias_up.astype(
        jnp.float32
    )

    def smooth(pre_active):
        return jax.nn.gelu(pre_active, approximate=True)

    active_full, gelu_back = jax.vjp(smooth, hidden)
    active = active_full.astype(jnp.bfloat16)
    down = jnp.dot(active, proj_down, preferred_element_type=jnp.float32) + bias_down.astype(
        jnp.float32
    )
    output = (resid + down).astype(jnp.bfloat16)
    grad_out = cots.astype(jnp.float32)
    grad_bias_down = column_sums(cots)
    grad_proj_down = jnp.einsum("tf,td->fd", active, cots, preferred_element_type=jnp.float32)
    grad_active = jnp.einsum("td,fd->tf", cots, proj_down, preferred_element_type=jnp.float32)
    grad_hidden = gelu_back(grad_active)[0].astype(jnp.bfloat16)
    grad_bias_up = column_sums(grad_hidden)
    grad_proj_up = jnp.einsum(
        "td,tf->df", lowered_two, grad_hidden, preferred_element_type=jnp.float32
    )
    grad_lowered_two = jnp.einsum(
        "tf,df->td", grad_hidden, proj_up, preferred_element_type=jnp.float32
    )
    grad_gain_two = jnp.sum(grad_lowered_two * normed_two, 0)
    grad_shift_two = jnp.sum(grad_lowered_two, 0)
    grad_resid = grad_out + normalize_back(
        grad_lowered_two * gain_two.astype(jnp.float32), normed_two, inverse_two
    )
    grad_branch = grad_resid.astype(jnp.bfloat16)
    grad_bias_out = column_sums(grad_branch)
    grad_proj_out = jnp.einsum(
        "td,te->de", attended, grad_branch, preferred_element_type=jnp.float32
    )
    grad_attended = jnp.einsum(
        "te,de->td", grad_branch, proj_out, preferred_element_type=jnp.float32
    ).astype(jnp.bfloat16)
    grad_attended = grad_attended.reshape(count_rows, heads, head_size)
    delta = jnp.einsum("qhd,qhd->hq", grad_attended.astype(jnp.float32), exact)
    grad_query, grad_keys, grad_values = attention_back(
        query, log_total, grad_attended, delta, query_pos, query_seg, tiles
    )
    grad_pairs = jnp.concatenate(
        [grad_keys.reshape(length, width), grad_values.reshape(length, width)], 1
    )
    grad_pairs_local = lax.psum_scatter(grad_pairs, "ctx", scatter_dimension=0, tiled=True)
    grad_mixed = jnp.concatenate(
        [grad_query.reshape(count_rows, width), grad_pairs_local], 1
    ).astype(jnp.bfloat16)
    grad_bias_query = column_sums(grad_mixed[:, :width])
    grad_bias_value = column_sums(grad_mixed[:, 2 * width :])
    grad_proj_mixed = jnp.einsum(
        "td,te->de", lowered_one, grad_mixed, preferred_element_type=jnp.float32
    )
    grad_lowered_one = jnp.einsum(
        "te,de->td", grad_mixed, proj_mixed, preferred_element_type=jnp.float32
    )
    grad_gain_one = jnp.sum(grad_lowered_one * normed_one, 0)
    grad_shift_one = jnp.sum(grad_lowered_one, 0)
    grad_input = grad_resid + normalize_back(
        grad_lowered_one * gain_one.astype(jnp.float32), normed_one, inverse_one
    )
    grads = (
        grad_gain_one,
        grad_shift_one,
        grad_proj_mixed,
        grad_bias_query,
        grad_bias_value,
        grad_proj_out,
        grad_bias_out,
        grad_gain_two,
        grad_shift_two,
        grad_proj_up,
        grad_bias_up,
        grad_proj_down,
        grad_bias_down,
    )
    return (output, grad_input.astype(jnp.bfloat16), grads)


def fetch(shards):
    return (
        lax.all_gather(shards[0], "fsdp", axis=0, tiled=True),
        lax.all_gather(shards[1], "fsdp", axis=0, tiled=True),
        lax.all_gather(shards[2], "fsdp", axis=0, tiled=True),
        lax.all_gather(shards[3], "fsdp", axis=0, tiled=True),
        lax.all_gather(shards[4], "fsdp", axis=0, tiled=True),
        lax.all_gather(shards[5], "fsdp", axis=0, tiled=True),
        lax.all_gather(shards[6], "fsdp", axis=0, tiled=True),
        lax.all_gather(shards[7], "fsdp", axis=0, tiled=True),
        lax.all_gather(shards[8], "fsdp", axis=0, tiled=True),
        lax.all_gather(shards[9], "fsdp", axis=0, tiled=True),
        lax.all_gather(shards[10], "fsdp", axis=0, tiled=True),
        lax.all_gather(shards[11], "fsdp", axis=0, tiled=True),
        lax.all_gather(shards[12], "fsdp", axis=0, tiled=True),
    )


def share(grads):
    return (
        lax.psum_scatter(grads[0], "fsdp", scatter_dimension=0, tiled=True),
        lax.psum_scatter(grads[1], "fsdp", scatter_dimension=0, tiled=True),
        lax.psum_scatter(grads[2], "fsdp", scatter_dimension=0, tiled=True),
        lax.psum_scatter(grads[3], "fsdp", scatter_dimension=0, tiled=True),
        lax.psum_scatter(grads[4], "fsdp", scatter_dimension=0, tiled=True),
        lax.psum_scatter(grads[5], "fsdp", scatter_dimension=0, tiled=True),
        lax.psum_scatter(grads[6], "fsdp", scatter_dimension=0, tiled=True),
        lax.psum_scatter(grads[7], "fsdp", scatter_dimension=0, tiled=True),
        lax.psum_scatter(grads[8], "fsdp", scatter_dimension=0, tiled=True),
        lax.psum_scatter(grads[9], "fsdp", scatter_dimension=0, tiled=True),
        lax.psum_scatter(grads[10], "fsdp", scatter_dimension=0, tiled=True),
        lax.psum_scatter(grads[11], "fsdp", scatter_dimension=0, tiled=True),
        lax.psum_scatter(grads[12], "fsdp", scatter_dimension=0, tiled=True),
    )


def on_device(
    layer_input,
    segments,
    ln1_gain,
    ln1_bias,
    w_qkv,
    q_bias,
    v_bias,
    w_attn_out,
    b_attn_out,
    ln2_gain,
    ln2_bias,
    w_up,
    b_up,
    w_down,
    b_down,
    cotangent,
):
    shards = (
        ln1_gain,
        ln1_bias,
        w_qkv,
        q_bias,
        v_bias,
        w_attn_out,
        b_attn_out,
        ln2_gain,
        ln2_bias,
        w_up,
        b_up,
        w_down,
        b_down,
    )
    micro = layer_input.shape[0]
    count_rows = layer_input.shape[2]
    length = segments.shape[2]
    positions = stored_positions(length, lax.axis_size("ctx"))
    start = lax.axis_index("ctx") * count_rows
    outputs = []
    input_grads = []
    shared = None
    for number in range(micro):
        weights = fetch(shards)
        output, grad_input, grads = layer_pass(
            layer_input[number, 0],
            cotangent[number, 0],
            segments[number, 0],
            weights,
            positions,
            start,
        )
        summed = share(grads)
        shared = summed if shared is None else jax.tree.map(jnp.add, shared, summed)
        outputs.append(output)
        input_grads.append(grad_input)
    final = lax.psum(
        (
            shared[0],
            shared[1],
            shared[2],
            shared[3],
            shared[4],
            shared[5],
            shared[6],
            shared[7],
            shared[8],
            shared[9],
            shared[10],
            shared[11],
            shared[12],
        ),
        "ctx",
    )
    activations = jnp.stack(outputs)[:, None]
    input_grad = jnp.stack(input_grads)[:, None]
    return (
        activations,
        input_grad,
        final[0],
        final[1],
        final[2],
        final[3],
        final[4],
        final[5],
        final[6],
        final[7],
        final[8],
        final[9],
        final[10],
        final[11],
        final[12],
    )


D = 768
HD = 64
BLK = 256
NEG = -1e30
F32 = jnp.float32
BF16 = jnp.bfloat16


def dot(lhs, rhs, lhs_dim, rhs_dim):
    return lax.dot_general(
        lhs, rhs, (((lhs_dim,), (rhs_dim,)), ((), ())), preferred_element_type=F32
    )


def norm(v):
    center = v - jnp.mean(v, -1, keepdims=True)
    inverse = lax.rsqrt(jnp.mean(center * center, -1, keepdims=True) + 1e-05)
    return center * inverse, inverse


def colsum(v):
    return jnp.sum(v, 0, keepdims=True)


def loop(count, body):
    def step(index, carry):
        body(index)
        return carry

    lax.fori_loop(0, count, step, 0)


def lanes(index, size):
    return pl.ds(pl.multiple_of(index * size, size), size)


def attention_masks(seg_ref, bias_ref, mine):
    key = lax.broadcasted_iota(jnp.int32, (BLK, BLK), 0)
    query = lax.broadcasted_iota(jnp.int32, (BLK, BLK), 1)
    causal = key <= query
    for micro in range(2):

        def row(start):
            piece = seg_ref[micro : micro + 1, pl.ds(pl.multiple_of(start, BLK), BLK)]
            return jnp.broadcast_to(piece.astype(F32), (BLK, BLK))

        solo = row(mine * 2 * BLK + mine * BLK)
        wide = row(mine * 2 * BLK + (1 - mine) * BLK)
        extra = row((1 - mine) * 3 * BLK)
        rows = slice(micro * BLK, micro * BLK + BLK)
        tiles = ((solo.T == solo) & causal, extra.T == wide, (wide.T == wide) & causal)
        for t, allowed in enumerate(tiles):
            bias_ref[rows, t * BLK : t * BLK + BLK] = jnp.where(allowed, 0.0, NEG).astype(BF16)


def attention_rows(micro, mine):
    solo = pl.ds(pl.multiple_of(micro * 2 * BLK + mine * BLK, BLK), BLK)
    wide = pl.ds(pl.multiple_of(micro * 2 * BLK + (1 - mine) * BLK, BLK), BLK)
    extra = pl.ds(pl.multiple_of(1024 + micro * BLK, BLK), BLK)
    return solo, wide, extra


def halves(value):
    left = lax.broadcasted_iota(jnp.int32, value.shape, 1) < HD
    zero = jnp.zeros_like(value)
    return jnp.where(left, value, zero), jnp.where(left, zero, value)


def softmax_columns(tiles):
    peak = tiles[0].max(0, keepdims=True)
    for tile in tiles[1:]:
        peak = jnp.maximum(peak, tile.max(0, keepdims=True))
    terms = [jnp.exp(tile - peak) for tile in tiles]
    total = colsum(terms[0])
    for term in terms[1:]:
        total = total + colsum(term)
    scale = 1.0 / total
    return [(term * scale).astype(BF16) for term in terms]


def attention_forward(index, refs, mine):
    q_ref, k_ref, v_ref, o_ref, p_ref, bias_ref = refs
    micro = index // 6
    pair = lanes(index % 6, 128)
    solo, wide, extra = attention_rows(micro, mine)
    k_s, k_x, k_e = k_ref[solo, pair], k_ref[wide, pair], k_ref[extra, pair]
    vt_s, vt_x, vt_e = v_ref[solo, pair].T, v_ref[wide, pair].T, v_ref[extra, pair].T
    q_s, q_x = halves(q_ref[solo, pair]), halves(q_ref[wide, pair])
    outs_s, outs_x = [], []

    def bias(t):
        rows = pl.ds(pl.multiple_of(micro * BLK, BLK), BLK)
        return bias_ref[rows, t * BLK : t * BLK + BLK].astype(F32)

    for head in range(2):
        rows = slice(head * HD, head * HD + HD)
        (p_s,) = softmax_columns([dot(k_s, q_s[head], 1, 1) + bias(0)])
        p_e, p_x = softmax_columns(
            [
                dot(k_e, q_x[head], 1, 1) + bias(1),
                dot(k_x, q_x[head], 1, 1) + bias(2),
            ]
        )
        p_ref[index, head, 0:BLK] = p_s
        p_ref[index, head, BLK : 2 * BLK] = p_e
        p_ref[index, head, 2 * BLK :] = p_x
        outs_s.append(dot(vt_s[rows], p_s, 1, 0))
        outs_x.append(dot(vt_e[rows], p_e, 1, 0) + dot(vt_x[rows], p_x, 1, 0))
    o_ref[solo, pair] = jnp.concatenate(outs_s, 0).T.astype(BF16)
    o_ref[wide, pair] = jnp.concatenate(outs_x, 0).T.astype(BF16)


def attention_backward(index, refs, mine):
    q_ref, k_ref, v_ref, go_ref, p_ref = refs
    micro = index // 6
    pair = lanes(index % 6, 128)
    solo, wide, extra = attention_rows(micro, mine)
    k_s, k_x, k_e = k_ref[solo, pair], k_ref[wide, pair], k_ref[extra, pair]
    v_s, v_x, v_e = v_ref[solo, pair], v_ref[wide, pair], v_ref[extra, pair]
    kt_s, kt_x, kt_e = k_s.T, k_x.T, k_e.T
    q_s, q_x = halves(q_ref[solo, pair]), halves(q_ref[wide, pair])
    go_s, go_x = halves(go_ref[solo, pair]), halves(go_ref[wide, pair])
    p_all, g_all, outs_s, outs_x = [], [], [], []
    for head in range(2):
        rows = slice(head * HD, head * HD + HD)
        p_s, p_e, p_x = (p_ref[index, head, BLK * t : BLK * t + BLK] for t in range(3))
        f_s, f_e, f_x = p_s.astype(F32), p_e.astype(F32), p_x.astype(F32)
        t_s = f_s * dot(v_s, go_s[head], 1, 1)
        t_e = f_e * dot(v_e, go_x[head], 1, 1)
        t_x = f_x * dot(v_x, go_x[head], 1, 1)
        d_s = colsum(t_s)
        d_x = colsum(t_e) + colsum(t_x)
        g_s = (t_s - f_s * d_s).astype(BF16)
        g_e = (t_e - f_e * d_x).astype(BF16)
        g_x = (t_x - f_x * d_x).astype(BF16)
        outs_s.append(dot(kt_s[rows], g_s, 1, 0))
        outs_x.append(dot(kt_e[rows], g_e, 1, 0) + dot(kt_x[rows], g_x, 1, 0))
        p_all.append((p_s, p_e, p_x))
        g_all.append((g_s, g_e, g_x))

    def both(tiles, which, right):
        return dot(jnp.concatenate([tiles[0][which], tiles[1][which]], 1), right, 1, 0).astype(BF16)

    go_s, go_x = jnp.concatenate(go_s, 0), jnp.concatenate(go_x, 0)
    q_s, q_x = jnp.concatenate(q_s, 0), jnp.concatenate(q_x, 0)
    v_ref[solo, pair] = both(p_all, 0, go_s)
    v_ref[extra, pair] = both(p_all, 1, go_x)
    v_ref[wide, pair] = both(p_all, 2, go_x)
    k_ref[solo, pair] = both(g_all, 0, q_s)
    k_ref[extra, pair] = both(g_all, 1, q_x)
    k_ref[wide, pair] = both(g_all, 2, q_x)
    q_ref[solo, pair] = (jnp.concatenate(outs_s, 0).T * 0.125).astype(BF16)
    q_ref[wide, pair] = (jnp.concatenate(outs_x, 0).T * 0.125).astype(BF16)


MESH = pl.DeviceIdType.MESH
HALF = D // 2


class Place:
    def __init__(self):
        self.c = lax.axis_index("ctx")
        f = lax.axis_index("fsdp")
        self.z, self.y, self.k = f // 4, (f // 2) % 2, f % 2
        self.sibling = self.at(self.c, self.z, self.y, 1 - self.k)
        self.beside = self.at(1 - self.c, self.z, self.y, self.k)
        self.across = self.at(self.c, self.z, 1 - self.y, self.k)

    def at(self, c, z, y, k):
        return (c, z * 4 + y * 2 + k)

    def level(self, step):
        return lax.rem(self.z + step, 4)

    def along(self, step):
        return self.at(self.c, self.level(step), self.y, self.k)

    def pick(self, first, second):
        return first + self.k * (second - first)

    def turn(self, core):
        side = self.k if core == 0 else 1 - self.k
        c = self.c + (1 - side) * (1 - 2 * self.c)
        y = self.y + side * (1 - 2 * self.y)
        return self.at(c, self.z, y, self.k)


def half(index):
    return pl.ds(pl.multiple_of(index * HALF, 128), HALF)


def send(source, target, sends, recvs, device):
    return pltpu.make_async_remote_copy(
        src_ref=source, dst_ref=target, send_sem=sends, recv_sem=recvs, device_id=device, device_id_type=MESH
    )


def begin(copies):
    for copy in copies:
        copy.start()


def landed(copies):
    for copy in copies:
        copy.wait_recv()


def gone(copies):
    for copy in copies:
        copy.wait_send()


class Gather:
    def __init__(self, place, sources, w_ref, d_ref, vec_ref, sends, recvs, local):
        self.p, self.sources = place, sources
        self.w, self.d, self.v = w_ref, d_ref, vec_ref
        self.sends, self.recvs, self.local = sends, recvs, local

    def whole(self, piece):
        return self.v if piece is None else self.w.at[piece]

    def row(self, piece):
        return 12 if piece is None else piece

    def own(self, piece):
        if piece is None:
            return self.sources[3]
        if piece < 3:
            return self.sources[0].at[:, piece * D : piece * D + D]
        if piece == 3:
            return self.sources[1]
        return self.sources[2].at[:, (piece - 4) * D : (piece - 3) * D]

    def own_half(self, piece):
        cols = half(self.p.c)
        if piece is None:
            return self.sources[3].at[:, cols]
        if piece == 3:
            return self.sources[1].at[:, cols]
        base, first = (self.sources[0], 0) if piece < 3 else (self.sources[2], 4)
        return base.at[:, pl.ds(pl.multiple_of((piece - first) * D + self.p.c * HALF, 128), HALF)]

    def keep(self, piece):
        p = self.p
        return pltpu.make_async_copy(
            self.own(piece), self.whole(piece).at[p.z, p.y, p.k], self.local.at[self.row(piece)]
        )

    def keep_down(self):
        p = self.p
        return pltpu.make_async_copy(self.sources[4], self.d.at[p.z, p.y, p.k], self.local.at[8])

    def z_copy(self, piece, step, level):
        p, row = self.p, self.row(piece)
        return send(
            self.own_half(piece),
            self.whole(piece).at[level, p.y, p.k, :, half(p.c)],
            self.sends.at[row, step - 1],
            self.recvs.at[row, step - 1],
            p.along(step),
        )

    def z_down(self, step, level, sem):
        p = self.p
        return send(
            self.sources[4].at[:, half(p.c)],
            self.d.at[level, p.y, p.k, :, half(p.c)],
            self.sends.at[13, sem],
            self.recvs.at[13, sem],
            p.along(step),
        )

    def start(self, pieces):
        for piece in pieces:
            self.keep(piece).start()
            for step in (1, 2, 3):
                self.z_copy(piece, step, self.p.z).start()

    def start_down(self):
        self.keep_down().start()
        for step in (1, 2, 3):
            self.z_down(step, self.p.z, step - 1).start()

    def copies(self, piece):
        p, row = self.p, self.row(piece)
        whole = self.whole(piece)

        def to(part, column, device):
            return send(part, part, self.sends.at[row, column], self.recvs.at[row, column], device)

        def beside():
            return [
                to(whole.at[p.level(step), p.y, p.k, :, half(p.c)], 2 + step, p.beside) for step in (1, 2, 3)
            ]

        def across():
            return [to(whole.at[:, p.y, p.k, :, half(p.c)], 6, p.across)]

        def forward():
            part = whole.at[:, p.pick(1 - p.y, p.y), p.k, :, half(p.pick(p.c, 1 - p.c))]
            return [to(part, 7, p.turn(0))]

        def sibling():
            return [to(whole.at[:, :, p.k], 8, p.sibling)]

        return beside, across, forward, sibling

    def copies_down(self, j):
        p, row = self.p, 8 + j

        def to(part, column, device):
            return send(part, part, self.sends.at[row, column], self.recvs.at[row, column], device)

        def beside():
            return [to(self.d.at[j, p.y, p.k, :, half(p.c)], 3, p.beside)]

        def across():
            return [to(self.d.at[j, p.y, p.k, :, half(p.c)], 6, p.across)]

        def forward():
            part = self.d.at[j, p.pick(1 - p.y, p.y), p.k, :, half(p.pick(p.c, 1 - p.c))]
            return [to(part, 7, p.turn(0))]

        def sibling():
            return [to(self.d.at[j, :, p.k], 8, p.sibling)]

        return beside, across, forward, sibling

    def stage(self, number, piece):
        if isinstance(piece, tuple):
            return self.stage_down(number, piece[1])
        beside, across, forward, sibling = self.copies(piece)
        if number == 2:
            self.keep_wait(piece)
            for step in (1, 2, 3):
                self.z_wait(piece, step)
            begin(beside() + across())
        elif number == 3:
            landed(beside() + across())
            begin(forward())
        elif number == 4:
            landed(forward())
            begin(sibling())
        elif number == 5:
            landed(sibling())
        else:
            gone(beside() + across() + forward() + sibling())

    def keep_wait(self, piece):
        p = self.p
        part = self.whole(piece).at[p.z, p.y, p.k]
        pltpu.make_async_copy(part, part, self.local.at[self.row(piece)]).wait()

    def z_wait(self, piece, step):
        p, row = self.p, self.row(piece)
        part = self.whole(piece).at[p.level(4 - step), p.y, p.k, :, half(p.c)]
        send(part, part, self.sends.at[row, step - 1], self.recvs.at[row, step - 1], p.along(step)).wait_recv()

    def stage_down(self, number, j):
        p = self.p
        beside, across, forward, sibling = self.copies_down(j)
        away = p.z != j
        if number == 2:

            @pl.when(away)
            def _():
                step = lax.rem(p.z - j + 4, 4)
                part = self.d.at[j, p.y, p.k, :, half(p.c)]
                landed([send(part, part, self.sends.at[13, step - 1], self.recvs.at[13, step - 1], p.along(1))])
                begin(beside())

            @pl.when(p.z == j)
            def _():
                self.keep_down().wait()

            begin(across())
        elif number == 3:

            @pl.when(away)
            def _():
                landed(beside())

            landed(across())
            begin(forward())
        elif number == 4:
            landed(forward())
            begin(sibling())
        elif number == 5:
            landed(sibling())
        else:

            @pl.when(away)
            def _():
                gone(beside())

            gone(across() + forward() + sibling())

    def finish(self):
        for piece in (None, *range(8)):
            for step in (1, 2, 3):
                self.z_copy(piece, step, self.p.z).wait_send()
        for step in (1, 2, 3):
            self.z_down(step, self.p.z, step - 1).wait_send()


class Scatter:
    def __init__(self, place, w_ref, d_ref, rings, fin_ref, find_ref, sends, recvs):
        self.p, self.w, self.d = place, w_ref, d_ref
        self.rings, self.fin, self.find = rings, fin_ref, find_ref
        self.sends, self.recvs = sends, recvs

    def part(self, block, y, col):
        if isinstance(block, tuple):
            return self.d.at[block[1], y, self.p.k, :, half(col)]
        return self.w.at[block, :, y, self.p.k, :, half(col)]

    def row(self, block):
        return 8 + block[1] if isinstance(block, tuple) else block

    def ring(self, block, which, slot):
        return self.rings[2 * which + (1 if isinstance(block, tuple) else 0)].at[slot]

    def sem(self, block, column):
        row = self.row(block)
        return self.sends.at[row, column], self.recvs.at[row, column]

    def to_sibling(self, block, slot):
        p = self.p
        part = self.d.at[block[1], :, 1 - p.k] if isinstance(block, tuple) else self.w.at[block, :, :, 1 - p.k]
        return send(part, self.ring(block, 0, slot), *self.sem(block, 0), p.sibling)

    def first(self, block, slot, i):
        p = self.p
        part = self.part(block, p.pick(i, 1 - p.y), p.pick(1 - p.c, i))
        ring = self.ring(block, 1, slot)
        ring = ring.at[i] if isinstance(block, tuple) else ring.at[:, i]
        return send(part, ring, *self.sem(block, 1 + i), p.turn(0))

    def second(self, block, slot):
        p = self.p
        part = self.part(block, p.pick(1 - p.y, p.y), p.pick(p.c, 1 - p.c))
        return send(part, self.ring(block, 2, slot), *self.sem(block, 3), p.turn(1))

    def third(self, block, slot, step):
        p = self.p
        part = self.w.at[block, p.level(step), p.y, p.k, :, half(p.c)]
        return send(part, self.rings[6].at[slot, step - 1], *self.sem(block, 3 + step), p.along(step))

    def third_down(self, j, step):
        p = self.p
        part = self.part(("d", j), p.y, p.c)
        return send(part, self.rings[7].at[step - 1], *self.sem(("d", j), 3 + step), p.at(p.c, j, p.y, p.k))

    def last(self, block):
        p = self.p
        part = self.find.at[:, half(p.c)] if isinstance(block, tuple) else self.fin.at[block, :, half(p.c)]
        return send(part, part, *self.sem(block, 7), p.beside)

    def stage(self, number, block, slot):
        p = self.p
        down = isinstance(block, tuple)
        if number == 0:
            self.to_sibling(block, slot).start()
        elif number == 1:
            self.to_sibling(block, slot).wait_recv()
            mine = self.d.at[block[1], :, p.k] if down else self.w.at[block, :, :, p.k]
            mine[...] = mine[...] + self.ring(block, 0, slot)[...]
            for i in (0, 1):
                self.first(block, slot, i).start()
        elif number == 2:
            for i in (0, 1):
                self.first(block, slot, i).wait_recv()
                mine = self.part(block, p.pick(i, p.y), p.pick(p.c, i))
                ring = self.ring(block, 1, slot)
                mine[...] = mine[...] + (ring[i] if down else ring[:, i])
            self.second(block, slot).start()
        elif number == 3:
            self.second(block, slot).wait_recv()
            mine = self.part(block, p.y, p.c)
            mine[...] = mine[...] + self.ring(block, 2, slot)[...]
            if down:
                j = block[1]

                @pl.when(p.z != j)
                def _():
                    step = lax.rem(j - p.z + 4, 4)
                    self.third_down(j, step).start()
            else:
                for step in (1, 2, 3):
                    self.third(block, slot, step).start()
        elif number == 4:
            if down:
                j = block[1]

                @pl.when(p.z == j)
                def _():
                    total = self.part(block, p.y, p.c)[...].astype(F32)
                    for step in (1, 2, 3):
                        self.third_down(j, step).wait_recv()
                        total = total + self.rings[7][step - 1].astype(F32)
                    self.find[:, half(p.c)] = total.astype(BF16)
                    self.last(block).start()
            else:
                total = self.w[block, p.z, p.y, p.k, :, half(p.c)].astype(F32)
                for step in (1, 2, 3):
                    self.third(block, slot, step).wait_recv()
                    total = total + self.rings[6][slot, step - 1].astype(F32)
                self.fin[block, :, half(p.c)] = total.astype(BF16)
                self.last(block).start()
        elif number == 5:
            if down:

                @pl.when(p.z == block[1])
                def _():
                    self.last(block).wait_recv()
            else:
                self.last(block).wait_recv()

    def finish(self, block, slot):
        p = self.p
        self.to_sibling(block, slot).wait_send()
        for i in (0, 1):
            self.first(block, slot, i).wait_send()
        self.second(block, slot).wait_send()
        if isinstance(block, tuple):
            j = block[1]

            @pl.when(p.z != j)
            def _():
                self.third_down(j, lax.rem(j - p.z + 4, 4)).wait_send()

            @pl.when(p.z == j)
            def _():
                self.last(block).wait_send()
        else:
            for step in (1, 2, 3):
                self.third(block, slot, step).wait_send()
            self.last(block).wait_send()


def layer_kernel(
    x_hbm, cot_hbm, seg_ref, qkv_hbm, out_hbm, up_hbm, vec_hbm, down_hbm,
    act_hbm, gx_hbm, fin_hbm, find_hbm, vg_hbm,
    w_ref, d_ref, vecs_ref, vec_ref, x_ref, cot_ref, q_ref, k_ref, v_ref, o_ref, p_ref, bias_ref,
    acc_ref, n2_ref, a2_ref, rs2_ref, g2_ref, a1_ref, gu_ref, vg_ref, bup_ref,
    ring0, ring1, ring2, ring3, ring4, ring5, ring6, ring7, fin_ref, find_ref, vr_ref,
    ag_send, ag_recv, ag_local, rs_send, rs_recv, v_send, v_recv, x_send, x_recv, sem,
):
    place = Place()
    mine = place.c
    a3_ref = x_ref.at[0:1024]
    gather = Gather(
        place, (qkv_hbm, out_hbm, up_hbm, vec_hbm, down_hbm), w_ref, d_ref, vecs_ref, ag_send, ag_recv, ag_local
    )
    scatter = Scatter(
        place, w_ref, d_ref, (ring0, ring1, ring2, ring3, ring4, ring5, ring6, ring7), fin_ref, find_ref, rs_send, rs_recv
    )
    barrier = pltpu.get_barrier_semaphore()
    for device in (place.sibling, place.beside, place.across, place.along(1), place.along(2), place.along(3)):
        pl.semaphore_signal(barrier, 1, device_id=device, device_id_type=MESH)
    load_x = pltpu.make_async_copy(x_hbm, x_ref.at[0:1024], sem.at[0])
    load_cot = pltpu.make_async_copy(cot_hbm, cot_ref, sem.at[1])
    load_x.start()
    load_cot.start()
    pl.semaphore_wait(barrier, 6)

    def rows_out(micro):
        return pl.ds(pl.multiple_of(micro * 512 + mine * BLK, BLK), BLK)

    give = [
        send(
            x_hbm.at[rows_out(micro)],
            x_ref.at[1024 + micro * BLK : 1024 + micro * BLK + BLK],
            x_send.at[micro],
            x_recv.at[micro],
            place.beside,
        )
        for micro in range(2)
    ]
    gather.start((None, 1))
    give[0].start()
    give[1].start()
    gather.start((2, 0, 3))

    order = [None, 1, 2, 0, 3, 4, ("d", 0), 5, ("d", 1), 6, ("d", 2), 7, ("d", 3)]

    def tick(t):
        for stage in (5, 4, 3, 2):
            at = t - (stage - 2)
            if 0 <= at < len(order):
                gather.stage(stage, order[at])

    def weight(index):
        return w_ref[index].reshape(D, D)

    def weight_down(index):
        return d_ref[index].reshape(D, D)

    def vec(row):
        return vec_ref[row : row + 1, :]

    def add_vec(row, value):
        vg_ref[row : row + 1, :] += value

    tick(0)
    gather.start((4, 5, 6, 7))
    gather.start_down()
    vg_ref[...] = jnp.zeros_like(vg_ref)
    attention_masks(seg_ref, bias_ref, mine)
    tick(1)
    load_x.wait()
    tick(2)
    tick(3)
    total = vecs_ref[0, 0, 0].astype(F32)
    for shard in range(1, 16):
        total = total + vecs_ref[shard // 4, (shard // 2) % 2, shard % 2].astype(F32)
    vec_ref[...] = total

    def first_norm(r):
        rows = pl.ds(r * BLK, BLK)
        normed, _ = norm(x_ref[rows, :].astype(F32))
        a1_ref[rows, :] = (normed * vec(0) + vec(1)).astype(BF16)

    loop(4, first_norm)
    give[0].wait_recv()
    give[1].wait_recv()
    loop(2, lambda r: first_norm(4 + r))
    tick(4)
    k_ref[...] = dot(a1_ref[...], weight(1), 1, 0).astype(BF16)
    tick(5)
    v_ref[...] = (dot(a1_ref[...], weight(2), 1, 0) + vec(3)).astype(BF16)
    tick(6)
    q_ref[...] = ((dot(a1_ref[0:1024, :], weight(0), 1, 0) + vec(2)).astype(BF16) * 0.125).astype(BF16)

    def forward(i):
        attention_forward(i, (q_ref, k_ref, v_ref, o_ref, p_ref, bias_ref), mine)
        for t, at in ((7, 3), (8, 7), (9, 11)):

            @pl.when(i == at)
            def _():
                tick(t)

    loop(12, forward)

    acc_ref[...] = dot(o_ref[...], weight(3), 1, 0)
    load_cot.wait()

    def second_norm(r):
        rows = pl.ds(r * BLK, BLK)
        resid = acc_ref[rows, :] + x_ref[rows, :].astype(F32) + vec(4)
        normed, inverse = norm(resid)
        acc_ref[rows, :] = resid + vec(7)
        n2_ref[rows, :] = normed.astype(BF16)
        a2_ref[rows, :] = (normed * vec(5) + vec(6)).astype(BF16)
        rs2_ref[rows, :] = jnp.broadcast_to(inverse, (BLK, 128))
        add_vec(7, colsum(cot_ref[rows, :].astype(F32)))
        g2_ref[rows, :] = jnp.zeros((BLK, D), F32)

    loop(4, second_norm)
    for j in range(4):
        bup_ref[j, 0:1] = vec(8 + j)
        bup_ref[j, 1:2] = jnp.zeros((1, D), F32)

    def feed(j):
        up = 4 + j
        bias = bup_ref[j, 0:1]

        def part(r):
            rows = pl.ds(r * 512, 512)
            u = dot(a2_ref[rows, :], weight(up), 1, 0) + bias
            back = dot(cot_ref[rows, :], weight_down(j), 1, 1)
            square = u * u
            th = jnp.tanh(u * (0.7978845608028654 + 0.035677408136300125 * square))
            half_up = 0.5 + 0.5 * th
            a3_ref[rows, :] = (u * half_up).astype(BF16)
            slope = half_up + (half_up * (1.0 - th)) * (u * (0.7978845608028654 + 0.10703222440890037 * square))
            gu = (back * slope).astype(BF16)
            gu_ref[rows, :] = gu
            bup_ref[j, 1:2] += colsum(gu.astype(F32))

        loop(2, part)

        @pl.when(j < 3)
        def _():
            gather.stage(5, 5 + j)
            gather.stage(4, ("d", j + 1))

        @pl.when(j < 2)
        def _():
            gather.stage(3, 6 + j)
            gather.stage(2, ("d", j + 2))

        @pl.when(j >= 1)
        def _():
            scatter.stage(1, 3 + j, (j - 1) % 4)
            scatter.stage(1, ("d", j - 1), (j - 1) % 2)

        acc_ref[...] += dot(a3_ref[...], weight_down(j), 1, 0)
        g2_ref[...] += dot(gu_ref[...], weight(up), 1, 1)

        @pl.when(j < 3)
        def _():
            gather.stage(5, ("d", j + 1))

        @pl.when(j < 2)
        def _():
            gather.stage(4, 6 + j)
            gather.stage(3, ("d", j + 2))

        @pl.when(j < 1)
        def _():
            gather.stage(2, 7 + j)

        @pl.when(j >= 1)
        def _():
            scatter.stage(2, 3 + j, (j - 1) % 4)
            scatter.stage(2, ("d", j - 1), (j - 1) % 2)

        gather.stage(6, up)
        w_ref[up] = dot(a2_ref[...], gu_ref[...], 0, 0).astype(BF16).reshape(4, 2, 2, 48, D)
        scatter.stage(0, up, j % 4)

        @pl.when(j >= 1)
        def _():
            scatter.stage(3, 3 + j, (j - 1) % 4)
            scatter.stage(3, ("d", j - 1), (j - 1) % 2)

        gather.stage(6, ("d", j))
        d_ref[j] = dot(a3_ref[...], cot_ref[...], 0, 0).astype(BF16).reshape(2, 2, 192, D)
        scatter.stage(0, ("d", j), j % 2)

        @pl.when(j >= 1)
        def _():
            scatter.stage(4, 3 + j, (j - 1) % 4)
            scatter.stage(4, ("d", j - 1), (j - 1) % 2)

    loop(4, feed)
    for j in range(4):
        vg_ref[8 + j : 9 + j, :] = bup_ref[j, 1:2]

    def second_back(r):
        rows = pl.ds(r * BLK, BLK)
        a3_ref[rows, :] = acc_ref[rows, :].astype(BF16)
        g2 = g2_ref[rows, :]
        normed = n2_ref[rows, :].astype(F32)
        add_vec(5, colsum(g2 * normed))
        add_vec(6, colsum(g2))
        t = g2 * vec(5)
        first = jnp.mean(t, -1, keepdims=True)
        second = jnp.mean(t * normed, -1, keepdims=True)
        grad = cot_ref[rows, :].astype(F32) + rs2_ref[rows, 0:1] * (t - first - normed * second)
        g2_ref[rows, :] = grad
        lowered = grad.astype(BF16)
        a2_ref[rows, :] = lowered
        add_vec(4, colsum(lowered.astype(F32)))

    loop(4, second_back)
    out_copy = pltpu.make_async_copy(a3_ref, act_hbm, sem.at[0])
    out_copy.start()
    last = [(7, 3), (("d", 3), 1)]
    for block, slot in last:
        scatter.stage(1, block, slot)
    gu_ref[...] = dot(a2_ref[...], weight(3), 1, 1).astype(BF16)
    gather.stage(6, 3)
    w_ref[3] = dot(o_ref[...], a2_ref[...], 0, 0).astype(BF16).reshape(4, 2, 2, 48, D)
    scatter.stage(0, 3, 0)
    for block, slot in last:
        scatter.stage(2, block, slot)

    def backward(i):
        attention_backward(i, (q_ref, k_ref, v_ref, gu_ref, p_ref), mine)

        @pl.when(i == 2)
        def _():
            scatter.stage(1, 3, 0)
            for block, slot in last:
                scatter.stage(3, block, slot)

        @pl.when(i == 5)
        def _():
            out_copy.wait()
            load_x.start()
            scatter.stage(2, 3, 0)
            for block, slot in last:
                scatter.stage(4, block, slot)

        @pl.when(i == 8)
        def _():
            scatter.stage(3, 3, 0)

        @pl.when(i == 11)
        def _():
            scatter.stage(4, 3, 0)

    loop(12, backward)

    gather.stage(6, 0)
    gather.stage(6, 1)
    gather.stage(6, 2)
    a2_ref[0:512, :] = (
        dot(k_ref[1024:1536, :], weight(1), 1, 1) + dot(v_ref[1024:1536, :], weight(2), 1, 1)
    ).astype(BF16)
    give_back = send(a2_ref.at[0:512], bias_ref, x_send.at[2], x_recv.at[2], place.beside)
    give_back.start()
    acc_ref[...] = dot(v_ref[0:1024, :], weight(2), 1, 1)
    w_ref[2] = dot(a1_ref[...], v_ref[...], 0, 0).astype(BF16).reshape(4, 2, 2, 48, D)
    scatter.stage(0, 2, 1)
    acc_ref[...] += dot(k_ref[0:1024, :], weight(1), 1, 1)
    w_ref[1] = dot(a1_ref[...], k_ref[...], 0, 0).astype(BF16).reshape(4, 2, 2, 48, D)
    scatter.stage(1, 2, 1)
    scatter.stage(0, 1, 2)
    acc_ref[...] += dot(q_ref[...], weight(0), 1, 1)
    w_ref[0] = dot(a1_ref[0:1024, :], q_ref[...], 0, 0).astype(BF16).reshape(4, 2, 2, 48, D)
    scatter.stage(2, 2, 1)
    scatter.stage(1, 1, 2)
    scatter.stage(0, 0, 3)

    add_vec(2, colsum(q_ref[...].astype(F32)))
    add_vec(3, colsum(v_ref[...].astype(F32)))

    def extra_back(r):
        rows = pl.ds(1024 + r * BLK, BLK)
        normed, _ = norm(x_ref[rows, :].astype(F32))
        g1 = a2_ref[pl.ds(r * BLK, BLK), :].astype(F32)
        add_vec(0, colsum(g1 * normed))
        add_vec(1, colsum(g1))

    loop(2, extra_back)

    def first_sums(r):
        rows = pl.ds(r * BLK, BLK)
        normed, inverse = norm(x_ref[rows, :].astype(F32))
        g1 = acc_ref[rows, :]
        add_vec(0, colsum(g1 * normed))
        add_vec(1, colsum(g1))

    load_x.wait()
    loop(4, first_sums)
    def exchange(index, slot, device):
        return send(vg_ref, vr_ref.at[slot], v_send.at[index], v_recv.at[index], device)

    def add_up(indices):
        for index, device in indices:
            exchange(index, index, device).start()
        for index, device in indices:
            exchange(index, index, device).wait()
        value = vg_ref[...]
        for index, device in indices:
            value = value + vr_ref[index]
        vg_ref[...] = value

    add_up([(0, place.sibling)])
    scatter.stage(3, 2, 1)
    scatter.stage(2, 1, 2)
    scatter.stage(1, 0, 3)
    give_back.wait_recv()

    def first_back(r):
        rows = pl.ds(r * BLK, BLK)
        normed, inverse = norm(x_ref[rows, :].astype(F32))
        t = acc_ref[rows, :] * vec(0)
        first = jnp.mean(t, -1, keepdims=True)
        second = jnp.mean(t * normed, -1, keepdims=True)
        gu_ref[rows, :] = (g2_ref[rows, :] + inverse * (t - first - normed * second)).astype(BF16)

    for micro in range(2):
        acc_ref[rows_out(micro), :] += bias_ref[micro * BLK : micro * BLK + BLK, :].astype(F32)
    loop(4, first_back)
    gx_copy = pltpu.make_async_copy(gu_ref, gx_hbm, sem.at[1])
    gx_copy.start()
    add_up([(1, place.beside)])
    scatter.stage(4, 2, 1)
    scatter.stage(3, 1, 2)
    scatter.stage(2, 0, 3)
    add_up([(2, place.across)])
    scatter.stage(4, 1, 2)
    scatter.stage(3, 0, 3)
    add_up([(3, place.along(1)), (4, place.along(2)), (5, place.along(3))])
    scatter.stage(4, 0, 3)
    blocks = [(4 + j, j) for j in range(4)] + [(("d", j), j % 2) for j in range(4)] + [(3, 0), (2, 1), (1, 2), (0, 3)]
    for block, slot in blocks:
        scatter.stage(5, block, slot)
    ends = [
        pltpu.make_async_copy(source, target, sem.at[2 + i])
        for i, (source, target) in enumerate(((fin_ref, fin_hbm), (find_ref, find_hbm), (vg_ref, vg_hbm)))
    ]
    for copy in ends:
        copy.start()
    for block, slot in blocks:
        scatter.finish(block, slot)
    gather.stage(6, None)
    gather.finish()
    give[0].wait_send()
    give[1].wait_send()
    give_back.wait_send()
    gx_copy.wait()
    for copy in ends:
        copy.wait()


def fast_device(
    layer_input, segments, ln1_gain, ln1_bias, w_qkv, q_bias, v_bias, w_attn_out, b_attn_out,
    ln2_gain, ln2_bias, w_up, b_up, w_down, b_down, cotangent,
):
    f = lax.axis_index("fsdp")
    rows = jnp.stack([ln1_gain, ln1_bias, q_bias, v_bias, b_attn_out, ln2_gain, ln2_bias, b_down])
    vec = lax.dynamic_update_slice(jnp.zeros((16, D), BF16), rows, (0, f * 48))
    vec = lax.dynamic_update_slice(vec, b_up[None], (8 + f // 4, (f % 4) * 192))
    big = lambda *shape, dtype=BF16: jax.ShapeDtypeStruct(shape, dtype)
    hbm = pl.BlockSpec(memory_space=pltpu.HBM)
    vmem = pl.BlockSpec(memory_space=pltpu.VMEM)
    act, gx, fin, find, sums = pl.pallas_call(
        layer_kernel,
        out_shape=(
            big(1024, D), big(1024, D), big(8, 48, D), big(192, D), big(16, D, dtype=F32),
        ),
        in_specs=[hbm, hbm, vmem, hbm, hbm, hbm, hbm, hbm],
        out_specs=(hbm,) * 5,
        scratch_shapes=[
            pltpu.VMEM((8, 4, 2, 2, 48, D), BF16),
            pltpu.VMEM((4, 2, 2, 192, D), BF16),
            pltpu.VMEM((4, 2, 2, 16, D), BF16),
            pltpu.VMEM((16, D), F32),
            pltpu.VMEM((1536, D), BF16),
            pltpu.VMEM((1024, D), BF16),
            pltpu.VMEM((1024, D), BF16),
            pltpu.VMEM((1536, D), BF16),
            pltpu.VMEM((1536, D), BF16),
            pltpu.VMEM((1024, D), BF16),
            pltpu.VMEM((12, 2, 3 * BLK, BLK), BF16),
            pltpu.VMEM((2 * BLK, 3 * BLK), BF16),
            pltpu.VMEM((1024, D), F32),
            pltpu.VMEM((1024, D), BF16),
            pltpu.VMEM((1024, D), BF16),
            pltpu.VMEM((1024, 128), F32),
            pltpu.VMEM((1024, D), F32),
            pltpu.VMEM((1536, D), BF16),
            pltpu.VMEM((1024, D), BF16),
            pltpu.VMEM((16, D), F32),
            pltpu.VMEM((4, 8, D), F32),
            pltpu.VMEM((4, 4, 2, 48, D), BF16),
            pltpu.VMEM((2, 2, 192, D), BF16),
            pltpu.VMEM((4, 4, 2, 48, HALF), BF16),
            pltpu.VMEM((2, 2, 192, HALF), BF16),
            pltpu.VMEM((4, 4, 48, HALF), BF16),
            pltpu.VMEM((2, 192, HALF), BF16),
            pltpu.VMEM((4, 3, 48, HALF), BF16),
            pltpu.VMEM((3, 192, HALF), BF16),
            pltpu.VMEM((8, 48, D), BF16),
            pltpu.VMEM((192, D), BF16),
            pltpu.VMEM((6, 16, D), F32),
            pltpu.SemaphoreType.DMA((14, 9)),
            pltpu.SemaphoreType.DMA((14, 9)),
            pltpu.SemaphoreType.DMA((13,)),
            pltpu.SemaphoreType.DMA((12, 8)),
            pltpu.SemaphoreType.DMA((12, 8)),
            pltpu.SemaphoreType.DMA((6,)),
            pltpu.SemaphoreType.DMA((6,)),
            pltpu.SemaphoreType.DMA((3,)),
            pltpu.SemaphoreType.DMA((3,)),
            pltpu.SemaphoreType.DMA((5,)),
        ],
        compiler_params=pltpu.CompilerParams(
            vmem_limit_bytes=66_500_000, collective_id=0, has_side_effects=True
        ),
        name="layer",
    )(
        layer_input.reshape(1024, D), cotangent.reshape(1024, D), segments.reshape(2, 1024),
        w_qkv, w_attn_out, w_up, vec, w_down,
    )
    fin = fin.astype(F32)
    part = lax.dynamic_slice(sums, (0, f * 48), (8, 48))
    g_bup = lax.dynamic_slice(sums, (8 + f // 4, (f % 4) * 192), (1, 192))[0]
    return (
        act.reshape(2, 1, 512, D), gx.reshape(2, 1, 512, D), part[0], part[1],
        jnp.concatenate([fin[0], fin[1], fin[2]], 1), part[2], part[3], fin[3], part[4], part[5], part[6],
        jnp.concatenate([fin[4], fin[5], fin[6], fin[7]], 1), g_bup, find.astype(F32), part[7],
    )


def solution(mesh):
    in_specs = (
        P(None, "fsdp", "ctx", None),
        P(None, "fsdp", None),
        P("fsdp"),
        P("fsdp"),
        P("fsdp", None),
        P("fsdp"),
        P("fsdp"),
        P("fsdp", None),
        P("fsdp"),
        P("fsdp"),
        P("fsdp"),
        P("fsdp", None),
        P("fsdp"),
        P("fsdp", None),
        P("fsdp"),
        P(None, "fsdp", "ctx", None),
    )
    out_specs = (
        P(None, "fsdp", "ctx", None),
        P(None, "fsdp", "ctx", None),
        P("fsdp"),
        P("fsdp"),
        P("fsdp", None),
        P("fsdp"),
        P("fsdp"),
        P("fsdp", None),
        P("fsdp"),
        P("fsdp"),
        P("fsdp"),
        P("fsdp", None),
        P("fsdp"),
        P("fsdp", None),
        P("fsdp"),
    )
    fast = mesh.shape["ctx"] == 2 and mesh.shape["fsdp"] == 16
    return jax.shard_map(
        fast_device if fast else on_device, mesh=mesh, in_specs=in_specs, out_specs=out_specs, check_vma=False
    )
```

```python
import jax
import jax.numpy as jnp
from jax import lax
from jax.experimental import pallas as pl
from jax.experimental.pallas import tpu as pltpu
from jax.sharding import PartitionSpec as P

H = 12


def stored_positions(length, groups):
    block_size = length // (2 * groups)
    stored = jnp.arange(length, dtype=jnp.int32)
    holder = stored // (2 * block_size)
    within = stored % (2 * block_size)
    second = within // block_size
    offset = within % block_size
    block_index = jnp.where(second == 0, holder, 2 * groups - 1 - holder)
    return block_index * block_size + offset


def normalize_parts(values):
    center = jnp.mean(values, -1, keepdims=True)
    centered = values - center
    inverse = lax.rsqrt(jnp.mean(centered * centered, -1, keepdims=True) + 1e-05)
    return (centered * inverse, inverse)


def normalize_back(grad_normed, normed, inverse):
    first = jnp.mean(grad_normed, -1, keepdims=True)
    second = jnp.mean(grad_normed * normed, -1, keepdims=True)
    return inverse * (grad_normed - first - normed * second)


def tile_allowed(query_pos, query_seg, key_pos, key_seg):
    return (key_pos[None, :] <= query_pos[:, None]) & (key_seg[None, :] == query_seg[:, None])


def tile_scores(query, keys_tile, allowed):
    scores = (
        jnp.einsum("qhd,khd->hqk", query, keys_tile, preferred_element_type=jnp.float32) * 0.125
    )
    return jnp.where(allowed[None], scores, -1e30)


def online_softmax(query, query_pos, query_seg, tiles):
    heads = query.shape[1]
    count_rows = query.shape[0]

    def advance(carry, tile):
        keys_tile, values_tile, key_pos, key_seg = tile
        allowed = tile_allowed(query_pos, query_seg, key_pos, key_seg)

        def compute(state):
            peak, total, accum = state
            scores = tile_scores(query, keys_tile, allowed)
            new_peak = jnp.maximum(peak, jnp.max(scores, -1))
            terms = jnp.where(allowed[None], jnp.exp(scores - new_peak[..., None]), 0.0)
            factor = jnp.exp(peak - new_peak)
            upper = terms.astype(jnp.bfloat16)
            lower = (terms - upper.astype(jnp.float32)).astype(jnp.bfloat16)
            added = jnp.einsum(
                "hqk,khd->qhd", upper, values_tile, preferred_element_type=jnp.float32
            )
            added = added + jnp.einsum(
                "hqk,khd->qhd", lower, values_tile, preferred_element_type=jnp.float32
            )
            accum = accum * jnp.transpose(factor)[..., None] + added
            return (new_peak, total * factor + jnp.sum(terms, -1), accum)

        return (compute(carry), None)

    start_state = (
        jnp.full((heads, count_rows), -1e30, jnp.float32),
        jnp.zeros((heads, count_rows), jnp.float32),
        jnp.zeros(query.shape, jnp.float32),
    )
    (peak, total, accum), unused = lax.scan(advance, start_state, tiles)
    exact = accum / jnp.transpose(total)[..., None]
    return (peak + jnp.log(total), exact)


def attention_out(query, log_total, query_pos, query_seg, tiles):

    def advance(carry, tile):
        keys_tile, values_tile, key_pos, key_seg = tile
        allowed = tile_allowed(query_pos, query_seg, key_pos, key_seg)

        def compute(summed):
            scores = tile_scores(query, keys_tile, allowed)
            probs = jnp.where(allowed[None], jnp.exp(scores - log_total[..., None]), 0.0)
            lowered = probs.astype(jnp.bfloat16)
            return summed + jnp.einsum(
                "hqk,khd->qhd", lowered, values_tile, preferred_element_type=jnp.float32
            )

        return (compute(carry), None)

    summed, unused = lax.scan(advance, jnp.zeros(query.shape, jnp.float32), tiles)
    return summed


def attention_back(query, log_total, grad_attended, delta, query_pos, query_seg, tiles):

    def advance(grad_query, tile):
        keys_tile, values_tile, key_pos, key_seg = tile
        allowed = tile_allowed(query_pos, query_seg, key_pos, key_seg)

        def compute(carry_query):
            scores = tile_scores(query, keys_tile, allowed)
            probs = jnp.where(allowed[None], jnp.exp(scores - log_total[..., None]), 0.0)
            lowered = probs.astype(jnp.bfloat16)
            grad_values = jnp.einsum(
                "hqk,qhd->khd", lowered, grad_attended, preferred_element_type=jnp.float32
            )
            grad_probs = jnp.einsum(
                "qhd,khd->hqk", grad_attended, values_tile, preferred_element_type=jnp.float32
            )
            grad_scores = (probs * (grad_probs - delta[..., None])).astype(jnp.bfloat16)
            new_query = carry_query + 0.125 * jnp.einsum(
                "hqk,khd->qhd", grad_scores, keys_tile, preferred_element_type=jnp.float32
            )
            grad_keys = 0.125 * jnp.einsum(
                "hqk,qhd->khd", grad_scores, query, preferred_element_type=jnp.float32
            )
            return (new_query, grad_keys, grad_values)

        new_query, grad_keys, grad_values = compute(grad_query)
        return (new_query, (grad_keys, grad_values))

    grad_query, (grad_keys, grad_values) = lax.scan(
        advance, jnp.zeros(query.shape, jnp.float32), tiles
    )
    return (grad_query, grad_keys, grad_values)


def column_sums(values):
    return jnp.sum(values.astype(jnp.float32), 0)


def layer_pass(inputs, cots, seg_row, weights, positions, start):
    (
        gain_one,
        shift_one,
        proj_mixed,
        bias_query,
        bias_value,
        proj_out,
        bias_out,
        gain_two,
        shift_two,
        proj_up,
        bias_up,
        proj_down,
        bias_down,
    ) = weights
    count_rows = inputs.shape[0]
    width = inputs.shape[1]
    heads = H
    head_size = width // heads
    length = seg_row.shape[0]
    query_pos = lax.dynamic_slice_in_dim(positions, start, count_rows)
    query_seg = lax.dynamic_slice_in_dim(seg_row, start, count_rows)
    values_in = inputs.astype(jnp.float32)
    normed_one, inverse_one = normalize_parts(values_in)
    lowered_one = (
        normed_one * gain_one.astype(jnp.float32) + shift_one.astype(jnp.float32)
    ).astype(jnp.bfloat16)
    mixed_bias = jnp.concatenate(
        [
            bias_query.astype(jnp.float32),
            jnp.zeros((width,), jnp.float32),
            bias_value.astype(jnp.float32),
        ]
    )
    mixed = (
        jnp.dot(lowered_one, proj_mixed, preferred_element_type=jnp.float32) + mixed_bias
    ).astype(jnp.bfloat16)
    query = mixed[:, :width].reshape(count_rows, heads, head_size)
    keys_values = lax.all_gather(mixed[:, width:], "ctx", axis=0, tiled=True)
    block = min(512, length)
    count = length // block
    tiles = (
        keys_values[:, :width].reshape(count, block, heads, head_size),
        keys_values[:, width:].reshape(count, block, heads, head_size),
        positions.reshape(count, block),
        seg_row.reshape(count, block),
    )
    log_total, exact = online_softmax(query, query_pos, query_seg, tiles)
    summed = attention_out(query, log_total, query_pos, query_seg, tiles)
    attended = summed.reshape(count_rows, width).astype(jnp.bfloat16)
    branch = jnp.dot(attended, proj_out, preferred_element_type=jnp.float32) + bias_out.astype(
        jnp.float32
    )
    resid = values_in + branch
    normed_two, inverse_two = normalize_parts(resid)
    lowered_two = (
        normed_two * gain_two.astype(jnp.float32) + shift_two.astype(jnp.float32)
    ).astype(jnp.bfloat16)
    hidden = jnp.dot(lowered_two, proj_up, preferred_element_type=jnp.float32) + bias_up.astype(
        jnp.float32
    )

    def smooth(pre_active):
        return jax.nn.gelu(pre_active, approximate=True)

    active_full, gelu_back = jax.vjp(smooth, hidden)
    active = active_full.astype(jnp.bfloat16)
    down = jnp.dot(active, proj_down, preferred_element_type=jnp.float32) + bias_down.astype(
        jnp.float32
    )
    output = (resid + down).astype(jnp.bfloat16)
    grad_out = cots.astype(jnp.float32)
    grad_bias_down = column_sums(cots)
    grad_proj_down = jnp.einsum("tf,td->fd", active, cots, preferred_element_type=jnp.float32)
    grad_active = jnp.einsum("td,fd->tf", cots, proj_down, preferred_element_type=jnp.float32)
    grad_hidden = gelu_back(grad_active)[0].astype(jnp.bfloat16)
    grad_bias_up = column_sums(grad_hidden)
    grad_proj_up = jnp.einsum(
        "td,tf->df", lowered_two, grad_hidden, preferred_element_type=jnp.float32
    )
    grad_lowered_two = jnp.einsum(
        "tf,df->td", grad_hidden, proj_up, preferred_element_type=jnp.float32
    )
    grad_gain_two = jnp.sum(grad_lowered_two * normed_two, 0)
    grad_shift_two = jnp.sum(grad_lowered_two, 0)
    grad_resid = grad_out + normalize_back(
        grad_lowered_two * gain_two.astype(jnp.float32), normed_two, inverse_two
    )
    grad_branch = grad_resid.astype(jnp.bfloat16)
    grad_bias_out = column_sums(grad_branch)
    grad_proj_out = jnp.einsum(
        "td,te->de", attended, grad_branch, preferred_element_type=jnp.float32
    )
    grad_attended = jnp.einsum(
        "te,de->td", grad_branch, proj_out, preferred_element_type=jnp.float32
    ).astype(jnp.bfloat16)
    grad_attended = grad_attended.reshape(count_rows, heads, head_size)
    delta = jnp.einsum("qhd,qhd->hq", grad_attended.astype(jnp.float32), exact)
    grad_query, grad_keys, grad_values = attention_back(
        query, log_total, grad_attended, delta, query_pos, query_seg, tiles
    )
    grad_pairs = jnp.concatenate(
        [grad_keys.reshape(length, width), grad_values.reshape(length, width)], 1
    )
    grad_pairs_local = lax.psum_scatter(grad_pairs, "ctx", scatter_dimension=0, tiled=True)
    grad_mixed = jnp.concatenate(
        [grad_query.reshape(count_rows, width), grad_pairs_local], 1
    ).astype(jnp.bfloat16)
    grad_bias_query = column_sums(grad_mixed[:, :width])
    grad_bias_value = column_sums(grad_mixed[:, 2 * width :])
    grad_proj_mixed = jnp.einsum(
        "td,te->de", lowered_one, grad_mixed, preferred_element_type=jnp.float32
    )
    grad_lowered_one = jnp.einsum(
        "te,de->td", grad_mixed, proj_mixed, preferred_element_type=jnp.float32
    )
    grad_gain_one = jnp.sum(grad_lowered_one * normed_one, 0)
    grad_shift_one = jnp.sum(grad_lowered_one, 0)
    grad_input = grad_resid + normalize_back(
        grad_lowered_one * gain_one.astype(jnp.float32), normed_one, inverse_one
    )
    grads = (
        grad_gain_one,
        grad_shift_one,
        grad_proj_mixed,
        grad_bias_query,
        grad_bias_value,
        grad_proj_out,
        grad_bias_out,
        grad_gain_two,
        grad_shift_two,
        grad_proj_up,
        grad_bias_up,
        grad_proj_down,
        grad_bias_down,
    )
    return (output, grad_input.astype(jnp.bfloat16), grads)


def fetch(shards):
    return (
        lax.all_gather(shards[0], "fsdp", axis=0, tiled=True),
        lax.all_gather(shards[1], "fsdp", axis=0, tiled=True),
        lax.all_gather(shards[2], "fsdp", axis=0, tiled=True),
        lax.all_gather(shards[3], "fsdp", axis=0, tiled=True),
        lax.all_gather(shards[4], "fsdp", axis=0, tiled=True),
        lax.all_gather(shards[5], "fsdp", axis=0, tiled=True),
        lax.all_gather(shards[6], "fsdp", axis=0, tiled=True),
        lax.all_gather(shards[7], "fsdp", axis=0, tiled=True),
        lax.all_gather(shards[8], "fsdp", axis=0, tiled=True),
        lax.all_gather(shards[9], "fsdp", axis=0, tiled=True),
        lax.all_gather(shards[10], "fsdp", axis=0, tiled=True),
        lax.all_gather(shards[11], "fsdp", axis=0, tiled=True),
        lax.all_gather(shards[12], "fsdp", axis=0, tiled=True),
    )


def share(grads):
    return (
        lax.psum_scatter(grads[0], "fsdp", scatter_dimension=0, tiled=True),
        lax.psum_scatter(grads[1], "fsdp", scatter_dimension=0, tiled=True),
        lax.psum_scatter(grads[2], "fsdp", scatter_dimension=0, tiled=True),
        lax.psum_scatter(grads[3], "fsdp", scatter_dimension=0, tiled=True),
        lax.psum_scatter(grads[4], "fsdp", scatter_dimension=0, tiled=True),
        lax.psum_scatter(grads[5], "fsdp", scatter_dimension=0, tiled=True),
        lax.psum_scatter(grads[6], "fsdp", scatter_dimension=0, tiled=True),
        lax.psum_scatter(grads[7], "fsdp", scatter_dimension=0, tiled=True),
        lax.psum_scatter(grads[8], "fsdp", scatter_dimension=0, tiled=True),
        lax.psum_scatter(grads[9], "fsdp", scatter_dimension=0, tiled=True),
        lax.psum_scatter(grads[10], "fsdp", scatter_dimension=0, tiled=True),
        lax.psum_scatter(grads[11], "fsdp", scatter_dimension=0, tiled=True),
        lax.psum_scatter(grads[12], "fsdp", scatter_dimension=0, tiled=True),
    )


def on_device(
    layer_input,
    segments,
    ln1_gain,
    ln1_bias,
    w_qkv,
    q_bias,
    v_bias,
    w_attn_out,
    b_attn_out,
    ln2_gain,
    ln2_bias,
    w_up,
    b_up,
    w_down,
    b_down,
    cotangent,
):
    shards = (
        ln1_gain,
        ln1_bias,
        w_qkv,
        q_bias,
        v_bias,
        w_attn_out,
        b_attn_out,
        ln2_gain,
        ln2_bias,
        w_up,
        b_up,
        w_down,
        b_down,
    )
    micro = layer_input.shape[0]
    count_rows = layer_input.shape[2]
    length = segments.shape[2]
    positions = stored_positions(length, lax.axis_size("ctx"))
    start = lax.axis_index("ctx") * count_rows
    outputs = []
    input_grads = []
    shared = None
    for number in range(micro):
        weights = fetch(shards)
        output, grad_input, grads = layer_pass(
            layer_input[number, 0],
            cotangent[number, 0],
            segments[number, 0],
            weights,
            positions,
            start,
        )
        summed = share(grads)
        shared = summed if shared is None else jax.tree.map(jnp.add, shared, summed)
        outputs.append(output)
        input_grads.append(grad_input)
    final = lax.psum(
        (
            shared[0],
            shared[1],
            shared[2],
            shared[3],
            shared[4],
            shared[5],
            shared[6],
            shared[7],
            shared[8],
            shared[9],
            shared[10],
            shared[11],
            shared[12],
        ),
        "ctx",
    )
    activations = jnp.stack(outputs)[:, None]
    input_grad = jnp.stack(input_grads)[:, None]
    return (
        activations,
        input_grad,
        final[0],
        final[1],
        final[2],
        final[3],
        final[4],
        final[5],
        final[6],
        final[7],
        final[8],
        final[9],
        final[10],
        final[11],
        final[12],
    )


D = 768
HD = 64
BLK = 256
NEG = -1e30
F32 = jnp.float32
BF16 = jnp.bfloat16


def dot(lhs, rhs, lhs_dim, rhs_dim):
    return lax.dot_general(
        lhs, rhs, (((lhs_dim,), (rhs_dim,)), ((), ())), preferred_element_type=F32
    )


def norm(v):
    center = v - jnp.mean(v, -1, keepdims=True)
    inverse = lax.rsqrt(jnp.mean(center * center, -1, keepdims=True) + 1e-05)
    return center * inverse, inverse


def colsum(v):
    return jnp.sum(v, 0, keepdims=True)


def loop(count, body):
    def step(index, carry):
        body(index)
        return carry

    lax.fori_loop(0, count, step, 0)


def lanes(index, size):
    return pl.ds(pl.multiple_of(index * size, size), size)


def attention_masks(seg_ref, bias_ref, mine):
    key = lax.broadcasted_iota(jnp.int32, (BLK, BLK), 0)
    query = lax.broadcasted_iota(jnp.int32, (BLK, BLK), 1)
    causal = key <= query
    for micro in range(2):

        def row(start):
            piece = seg_ref[micro, :, pl.ds(pl.multiple_of(start, BLK), BLK)]
            return jnp.broadcast_to(piece.astype(F32), (BLK, BLK))

        solo = row(mine * 2 * BLK + mine * BLK)
        wide = row(mine * 2 * BLK + (1 - mine) * BLK)
        extra = row((1 - mine) * 3 * BLK)
        rows = slice(micro * BLK, micro * BLK + BLK)
        tiles = ((solo.T == solo) & causal, extra.T == wide, (wide.T == wide) & causal)
        for t, allowed in enumerate(tiles):
            bias_ref[rows, t * BLK : t * BLK + BLK] = jnp.where(allowed, 0.0, NEG).astype(BF16)


def attention_rows(micro, mine):
    solo = pl.ds(pl.multiple_of(micro * 2 * BLK + mine * BLK, BLK), BLK)
    wide = pl.ds(pl.multiple_of(micro * 2 * BLK + (1 - mine) * BLK, BLK), BLK)
    extra = pl.ds(pl.multiple_of(1024 + micro * BLK, BLK), BLK)
    return solo, wide, extra


def halves(value):
    left = lax.broadcasted_iota(jnp.int32, value.shape, 1) < HD
    zero = jnp.zeros_like(value)
    return jnp.where(left, value, zero), jnp.where(left, zero, value)


def heads_of(group, which):
    return lanes(2 * group + which, 128)


def column_softmax(rows):
    peaks = []
    for tiles in rows:
        peak = tiles[0].max(0, keepdims=True)
        for tile in tiles[1:]:
            peak = jnp.maximum(peak, tile.max(0, keepdims=True))
        peaks.append(peak)
    terms = [[jnp.exp(tile - peak) for tile in tiles] for tiles, peak in zip(rows, peaks)]
    scales = []
    for tiles in terms:
        total = colsum(tiles[0])
        for tile in tiles[1:]:
            total = total + colsum(tile)
        scales.append(1.0 / total)
    return [[(tile * scale).astype(BF16) for tile in tiles] for tiles, scale in zip(terms, scales)]


def forward_heads(micro, group, refs, mine, tiles):
    q_ref, k_ref, v_ref, o_ref, p_ref, bias_ref = refs
    solo, wide, extra = attention_rows(micro, mine)
    queries = solo if tiles == (0,) else wide
    keys = [(solo, extra, wide)[t] for t in tiles]
    pairs = [heads_of(group, which) for which in range(2)]
    k = [[k_ref[rows, pair] for rows in keys] for pair in pairs]
    vt = [[v_ref[rows, pair].T for rows in keys] for pair in pairs]
    q = [halves(q_ref[queries, pair]) for pair in pairs]
    rows = pl.ds(pl.multiple_of(micro * BLK, BLK), BLK)
    bias = [bias_ref[rows, t * BLK : t * BLK + BLK].astype(F32) for t in tiles]
    heads = [(which, head) for which in range(2) for head in range(2)]
    scores = [
        [dot(k[which][t], q[which][head], 1, 1) + bias[t] for t in range(len(tiles))] for which, head in heads
    ]
    probs = column_softmax(scores)
    outs = []
    for (which, head), parts in zip(heads, probs):
        out = None
        for t, part in enumerate(parts):
            value = dot(vt[which][t][head * HD : head * HD + HD], part, 1, 0)
            out = value if out is None else out + value
        outs.append(out)
    for (which, head), parts in zip(heads, probs):
        for t, part in zip(tiles, parts):
            p_ref[6 * micro + 2 * group + which, head, t * BLK : t * BLK + BLK] = part
    for which, pair in enumerate(pairs):
        o_ref[queries, pair] = jnp.concatenate(outs[2 * which : 2 * which + 2], 0).T.astype(BF16)


def backward_heads(micro, group, refs, mine, tiles):
    q_ref, k_ref, v_ref, go_ref, p_ref = refs
    solo, wide, extra = attention_rows(micro, mine)
    queries = solo if tiles == (0,) else wide
    keys = [(solo, extra, wide)[t] for t in tiles]
    pairs = [heads_of(group, which) for which in range(2)]
    k = [[k_ref[rows, pair] for rows in keys] for pair in pairs]
    v = [[v_ref[rows, pair] for rows in keys] for pair in pairs]
    kt = [[tile.T for tile in tiles_of] for tiles_of in k]
    q = [halves(q_ref[queries, pair]) for pair in pairs]
    go = [halves(go_ref[queries, pair]) for pair in pairs]
    heads = [(which, head) for which in range(2) for head in range(2)]
    count = range(len(tiles))
    probs = [
        [p_ref[6 * micro + 2 * group + which, head, t * BLK : t * BLK + BLK] for t in tiles] for which, head in heads
    ]
    full = [[tile.astype(F32) for tile in parts] for parts in probs]
    terms = [
        [full[i][t] * dot(v[which][t], go[which][head], 1, 1) for t in count] for i, (which, head) in enumerate(heads)
    ]
    deltas = []
    for parts in terms:
        delta = colsum(parts[0])
        for part in parts[1:]:
            delta = delta + colsum(part)
        deltas.append(delta)
    grads = [
        [(terms[i][t] - full[i][t] * deltas[i]).astype(BF16) for t in count] for i in range(4)
    ]
    outs = []
    for i, (which, head) in enumerate(heads):
        out = None
        for t in count:
            value = dot(kt[which][t][head * HD : head * HD + HD], grads[i][t], 1, 0)
            out = value if out is None else out + value
        outs.append(out)
    results = []
    for which, pair in enumerate(pairs):
        first = 2 * which
        for t in count:
            results.append((v_ref, keys[t], pair, both(probs[first][t], probs[first + 1][t], go[which])))
            results.append((k_ref, keys[t], pair, both(grads[first][t], grads[first + 1][t], q[which])))
        grad = jnp.concatenate(outs[first : first + 2], 0).T * 0.125
        results.append((q_ref, queries, pair, grad.astype(BF16)))
    for ref, rows, pair, value in results:
        ref[rows, pair] = value


def both(left, right, values):
    return dot(jnp.concatenate([left, right], 1), jnp.concatenate(values, 0), 1, 0).astype(BF16)


PLAN = {
    0: (2100, 2101, 2000, 2012, 2001, 2002,),
    1: (2003, 2004, 2008, 200, 212, 201, 300, 312, 202, 301, 400, 2102, 412, 203, 2103, 500, 512,),
    10: (302, 2005, 2009, 2006, 2010, 2007, 401, 2011,),
    11: (204,),
    20: (501,),
    21: (402,),
    30: (303, 502,),
    40: (208,),
    41: (403,),
    42: (304,),
    43: (205, 503,),
    44: (308,),
    45: (404,),
    50: (305,),
    51: (504, 209,),
    60: (408, 405, 206, 508,),
    61: (505, 309,),
    62: (210,),
    63: (409, 306,),
    64: (207, 211, 1004,),
    70: (509, 310, 406, 1008,),
    71: (1104,),
    72: (506, 307,),
    73: (311, 1108,),
    74: (410, 1005,),
    80: (1009, 510,),
    81: (1204, 1105,),
    82: (407, 1109,),
    83: (507, 411,),
    84: (1208, 1006,),
    90: (511, 1304, 1010,),
    91: (1205, 1106,),
    92: (1110,),
    93: (1404, 1209,),
    94: (1308, 1305, 1007,),
    100: (1011,),
    101: (1206, 1107, 1111,),
    102: (1210,),
    120: (1309, 1003,),
    121: (1306, 1103, 1408,),
    122: (1207,),
    130: (1405, 1211, 1000,),
    131: (1310, 1100,),
    132: (1203, 1409,),
    140: (1307, 1001,),
    141: (1406, 1311, 1101,),
    142: (1410,),
    110: (1200, 1002,),
    150: (2202, 1407, 1303, 2201,),
    151: (1102,),
    152: (1201,),
    153: (1300,),
    155: (2300, 1411, 2301, 1202, 1403, 1301, 2200, 2203, 1400, 2302, 2303, 1302, 1401, 2304, 1402,),
}
GATHER_ACROSS = (3, 2)
SCATTER_ACROSS = (0, 2)
MESH = pl.DeviceIdType.MESH
HALF = D // 2


class Place:
    def __init__(self):
        self.c = lax.axis_index("ctx")
        f = lax.axis_index("fsdp")
        self.z, self.y, self.k = f // 4, (f // 2) % 2, f % 2
        self.sibling = self.at(self.c, self.z, self.y, 1 - self.k)
        self.beside = self.at(1 - self.c, self.z, self.y, self.k)
        self.across = self.at(self.c, self.z, 1 - self.y, self.k)

    def at(self, c, z, y, k):
        return (c, z * 4 + y * 2 + k)

    def level(self, step):
        return lax.rem(self.z + step, 4)

    def along(self, step):
        return self.at(self.c, self.level(step), self.y, self.k)

    def pick(self, side, first, second):
        return first + side * (second - first)

    def onward(self, side):
        c = self.c + (1 - side) * (1 - 2 * self.c)
        y = self.y + side * (1 - 2 * self.y)
        return self.at(c, self.z, y, self.k)


def half(index):
    return pl.ds(pl.multiple_of(index * HALF, 128), HALF)


def send(source, target, sends, recvs, device):
    return pltpu.make_async_remote_copy(
        src_ref=source, dst_ref=target, send_sem=sends, recv_sem=recvs, device_id=device, device_id_type=MESH
    )


def fixed(piece):
    return not isinstance(piece[1] if isinstance(piece, tuple) else piece, jax.Array)


def begin(copies):
    for copy in copies:
        copy.start()


def landed(copies):
    for copy in copies:
        copy.wait_recv()


def gone(copies):
    for copy in copies:
        copy.wait_send()


class Gather:
    def __init__(self, place, sources, w_ref, d_ref, vec_ref, sends, recvs, local):
        self.p, self.sources = place, sources
        self.w, self.d, self.v = w_ref, d_ref, vec_ref
        self.sends, self.recvs, self.local = sends, recvs, local

    def whole(self, piece):
        return self.v if piece is None else self.w.at[piece]

    def row(self, piece):
        return 12 if piece is None else piece

    def lead(self, piece):
        return 1 if fixed(piece) and piece in GATHER_ACROSS else self.p.k

    def own(self, piece):
        if piece is None:
            return self.sources[3]
        if piece < 3:
            return self.sources[0].at[:, piece * D : piece * D + D]
        if piece == 3:
            return self.sources[1]
        return self.sources[2].at[:, (piece - 4) * D : (piece - 3) * D]

    def own_half(self, piece):
        cols = half(self.p.c)
        if piece is None:
            return self.sources[3].at[:, cols]
        if piece == 3:
            return self.sources[1].at[:, cols]
        base, first = (self.sources[0], 0) if piece < 3 else (self.sources[2], 4)
        return base.at[:, pl.ds(pl.multiple_of((piece - first) * D + self.p.c * HALF, 128), HALF)]

    def keep(self, piece):
        p = self.p
        return pltpu.make_async_copy(
            self.own(piece), self.whole(piece).at[p.z, p.y, p.k], self.local.at[self.row(piece)]
        )

    def keep_down(self):
        p = self.p
        return pltpu.make_async_copy(self.sources[4], self.d.at[p.z, p.y, p.k], self.local.at[8])

    def z_copy(self, piece, step, level):
        p, row = self.p, self.row(piece)
        return send(
            self.own_half(piece),
            self.whole(piece).at[level, p.y, p.k, :, half(p.c)],
            self.sends.at[row, step - 1],
            self.recvs.at[row, step - 1],
            p.along(step),
        )

    def z_down(self, step, level, sem):
        p = self.p
        return send(
            self.sources[4].at[:, half(p.c)],
            self.d.at[level, p.y, p.k, :, half(p.c)],
            self.sends.at[13, sem],
            self.recvs.at[13, sem],
            p.along(step),
        )

    def own_across(self, piece):
        p, row = self.p, self.row(piece)
        return send(
            self.own_half(piece),
            self.whole(piece).at[p.z, p.y, p.k, :, half(p.c)],
            self.sends.at[row, 6],
            self.recvs.at[row, 6],
            p.across,
        )

    def start(self, *pieces):
        for piece in pieces:
            for step in (1, 2, 3):
                self.z_copy(piece, step, self.p.z).start()
            self.own_across(piece).start()
            self.keep(piece).start()

    def start_down(self, j):
        @pl.when(self.p.z == j)
        def _():
            for step in (1, 2, 3):
                self.z_down(step, self.p.z, step - 1).start()
            self.keep_down().start()

    def copies(self, piece):
        p, row = self.p, self.row(piece)
        whole = self.whole(piece)

        def to(part, column, device):
            return send(part, part, self.sends.at[row, column], self.recvs.at[row, column], device)

        def beside():
            return [
                to(whole.at[p.level(step), p.y, p.k, :, half(p.c)], 2 + step, p.beside) for step in (1, 2, 3)
            ]

        def across():
            return [
                to(whole.at[p.level(step), p.y, p.k, :, half(p.c)], 8 + step, p.across) for step in (1, 2, 3)
            ]

        def forward():
            lead = self.lead(piece)
            part = whole.at[:, p.pick(lead, 1 - p.y, p.y), p.k, :, half(p.pick(lead, p.c, 1 - p.c))]
            return [to(part, 7, p.onward(lead))]

        def sibling():
            return [to(whole.at[:, :, p.k], 8, p.sibling)]

        return beside, across, forward, sibling

    def copies_down(self, j):
        p, row = self.p, 8 + j

        def to(part, column, device):
            return send(part, part, self.sends.at[row, column], self.recvs.at[row, column], device)

        def beside():
            return [to(self.d.at[j, p.y, p.k, :, half(p.c)], 3, p.beside)]

        def across():
            return [to(self.d.at[j, p.y, p.k, :, half(p.c)], 6, p.across)]

        def forward():
            lead = self.lead(("d", j))
            part = self.d.at[j, p.pick(lead, 1 - p.y, p.y), p.k, :, half(p.pick(lead, p.c, 1 - p.c))]
            return [to(part, 7, p.onward(lead))]

        def sibling():
            return [to(self.d.at[j, :, p.k], 8, p.sibling)]

        return beside, across, forward, sibling

    def stage(self, number, piece):
        if isinstance(piece, tuple):
            return self.stage_down(number, piece[1])
        p, row, whole = self.p, self.row(piece), self.whole(piece)
        beside, across, forward, sibling = self.copies(piece)
        if number == 2:
            self.keep_wait(piece)
            for step in (1, 2, 3):
                self.z_wait(piece, step)
            begin(across() + beside())
        elif number == 3:
            part = whole.at[p.z, p.y, p.k, :, half(p.c)]
            own = send(part, part, self.sends.at[row, 6], self.recvs.at[row, 6], p.across)
            landed([own] + across() + beside())
            begin(forward())
        elif number == 4:
            landed(forward())
            begin(sibling())
        elif number == 5:
            landed(sibling())
        else:
            gone(beside() + across() + forward() + sibling())

    def keep_wait(self, piece):
        p = self.p
        part = self.whole(piece).at[p.z, p.y, p.k]
        pltpu.make_async_copy(part, part, self.local.at[self.row(piece)]).wait()

    def z_wait(self, piece, step):
        p, row = self.p, self.row(piece)
        part = self.whole(piece).at[p.level(4 - step), p.y, p.k, :, half(p.c)]
        send(part, part, self.sends.at[row, step - 1], self.recvs.at[row, step - 1], p.along(step)).wait_recv()

    def stage_down(self, number, j):
        p = self.p
        beside, across, forward, sibling = self.copies_down(j)
        away = p.z != j
        if number == 2:

            @pl.when(away)
            def _():
                step = lax.rem(p.z - j + 4, 4)
                part = self.d.at[j, p.y, p.k, :, half(p.c)]
                landed([send(part, part, self.sends.at[13, step - 1], self.recvs.at[13, step - 1], p.along(1))])
                begin(beside())

            @pl.when(p.z == j)
            def _():
                self.keep_down().wait()

            begin(across())
        elif number == 3:

            @pl.when(away)
            def _():
                landed(beside())

            landed(across())
            begin(forward())
        elif number == 4:
            landed(forward())
            begin(sibling())
        elif number == 5:
            landed(sibling())
        else:

            @pl.when(away)
            def _():
                gone(beside())

            gone(across() + forward() + sibling())

    def finish(self):
        for piece in (None, *range(8)):
            for step in (1, 2, 3):
                self.z_copy(piece, step, self.p.z).wait_send()
            self.own_across(piece).wait_send()
        for step in (1, 2, 3):
            self.z_down(step, self.p.z, step - 1).wait_send()


class Scatter:
    def __init__(self, place, w_ref, d_ref, rings, sends, recvs):
        self.p, self.w, self.d = place, w_ref, d_ref
        self.rings = rings
        self.sends, self.recvs = sends, recvs

    def held(self, block):
        return block + 4 if not isinstance(block, tuple) and block < 3 else block

    def lead(self, block):
        return 1 if fixed(block) and block in SCATTER_ACROSS else self.p.k

    def pick(self, block, first, second):
        return first + self.lead(block) * (second - first)

    def turn(self, block, number):
        return self.p.onward(self.lead(block) if number == 0 else 1 - self.lead(block))

    def part(self, block, y, col):
        if isinstance(block, tuple):
            return self.d.at[block[1], y, self.p.k, :, half(col)]
        return self.w.at[self.held(block), :, y, self.p.k, :, half(col)]

    def row(self, block):
        return 8 + block[1] if isinstance(block, tuple) else block

    def ring(self, block, which, slot):
        ring = self.rings[2 * which + (1 if isinstance(block, tuple) else 0)]
        return ring.at[slot % ring.shape[0]]

    def sem(self, block, column):
        row = self.row(block)
        return self.sends.at[row, column], self.recvs.at[row, column]

    def to_sibling(self, block, slot):
        p = self.p
        part = self.d.at[block[1], :, 1 - p.k] if isinstance(block, tuple) else self.w.at[self.held(block), :, :, 1 - p.k]
        return send(part, self.ring(block, 0, slot), *self.sem(block, 0), p.sibling)

    def first(self, block, slot, i):
        p = self.p
        part = self.part(block, self.pick(block, i, 1 - p.y), self.pick(block, 1 - p.c, i))
        ring = self.ring(block, 1, slot)
        ring = ring.at[i] if isinstance(block, tuple) else ring.at[:, i]
        return send(part, ring, *self.sem(block, 1 + i), self.turn(block, 0))

    def second(self, block, slot):
        p = self.p
        part = self.part(block, self.pick(block, 1 - p.y, p.y), self.pick(block, p.c, 1 - p.c))
        return send(part, self.ring(block, 2, slot), *self.sem(block, 3), self.turn(block, 1))

    def third(self, block, slot, step):
        p = self.p
        part = self.w.at[self.held(block), p.level(step), p.y, p.k, :, half(p.c)]
        return send(part, self.rings[6].at[slot % 4, step - 1], *self.sem(block, 3 + step), p.along(step))

    def third_down(self, j, step):
        p = self.p
        part = self.part(("d", j), p.y, p.c)
        return send(part, self.rings[7].at[step - 1], *self.sem(("d", j), 3 + step), p.at(p.c, j, p.y, p.k))

    def last(self, block):
        p = self.p
        land = self.rings[9] if isinstance(block, tuple) else self.rings[8].at[block]
        return send(self.total(block), land, *self.sem(block, 7), p.beside)

    def total(self, block):
        return self.rings[11] if isinstance(block, tuple) else self.rings[10].at[block]

    def store(self, block, target, sems):
        c = self.p.c
        land = self.rings[9] if isinstance(block, tuple) else self.rings[8].at[block]
        return [
            pltpu.make_async_copy(self.total(block), target.at[:, half(c)], sems.at[0]),
            pltpu.make_async_copy(land, target.at[:, half(1 - c)], sems.at[1]),
        ]

    def stage(self, number, block, slot):
        p = self.p
        down = isinstance(block, tuple)
        if number == 0:
            self.to_sibling(block, slot).start()
        elif number == 1:
            self.to_sibling(block, slot).wait_recv()
            mine = self.d.at[block[1], :, p.k] if down else self.w.at[self.held(block), :, :, p.k]
            mine[...] = mine[...] + self.ring(block, 0, slot)[...]
            for i in (0, 1):
                self.first(block, slot, i).start()
        elif number == 2:
            for i in (0, 1):
                self.first(block, slot, i).wait_recv()
                mine = self.part(block, self.pick(block, i, p.y), self.pick(block, p.c, i))
                ring = self.ring(block, 1, slot)
                mine[...] = mine[...] + (ring[i] if down else ring[:, i])
            self.second(block, slot).start()
        elif number == 3:
            self.second(block, slot).wait_recv()
            mine = self.part(block, p.y, p.c)
            mine[...] = mine[...] + self.ring(block, 2, slot)[...]
            if down:
                j = block[1]

                @pl.when(p.z != j)
                def _():
                    step = lax.rem(j - p.z + 4, 4)
                    self.third_down(j, step).start()
            else:
                for step in (1, 2, 3):
                    self.third(block, slot, step).start()
        elif number == 4:
            if down:
                j = block[1]

                @pl.when(p.z == j)
                def _():
                    total = self.part(block, p.y, p.c)[...].astype(F32)
                    for step in (1, 2, 3):
                        self.third_down(j, step).wait_recv()
                        total = total + self.rings[7][step - 1].astype(F32)
                    self.total(block)[...] = total.astype(BF16)
                    self.last(block).start()
            else:
                total = self.w[self.held(block), p.z, p.y, p.k, :, half(p.c)].astype(F32)
                for step in (1, 2, 3):
                    self.third(block, slot, step).wait_recv()
                    total = total + self.rings[6][slot % 4, step - 1].astype(F32)
                self.total(block)[...] = total.astype(BF16)
                self.last(block).start()
        elif number == 5:
            if down:

                @pl.when(p.z == block[1])
                def _():
                    self.last(block).wait_recv()
            else:
                self.last(block).wait_recv()

    def finish(self, block, slot):
        self.finish_block(block, slot)
        if isinstance(block, tuple):

            @pl.when(self.p.z == block[1])
            def _():
                self.last(block).wait_send()
        else:
            self.last(block).wait_send()

    def finish_block(self, block, slot):
        p = self.p
        self.to_sibling(block, slot).wait_send()
        for i in (0, 1):
            self.first(block, slot, i).wait_send()
        self.second(block, slot).wait_send()
        if isinstance(block, tuple):
            j = block[1]

            @pl.when(p.z != j)
            def _():
                self.third_down(j, lax.rem(j - p.z + 4, 4)).wait_send()
        else:
            for step in (1, 2, 3):
                self.third(block, slot, step).wait_send()


def layer_kernel(
    x_hbm, cot_hbm, seg_ref, qkv_hbm, out_hbm, up_hbm, rows_ref, bup_own_ref, down_hbm,
    act_hbm, gx_hbm, fin_hbm, find_hbm, vg_hbm,
    w_ref, d_ref, vecs_ref, vec_ref, x_ref, cot_ref, q_ref, k_ref, v_ref, o_ref, p_ref, bias_ref,
    acc_ref, n2_ref, a2_ref, rs2_ref, g2_ref, a1_ref, gu_ref, vg_ref, bup_ref,
    ring0, ring1, ring2, ring3, ring4, ring5, ring6, ring7, land_ref, landd_ref, own_ref, ownd_ref, vr_ref,
    qs_ref, vloc_ref, small_ref, ag_send, ag_recv, ag_local, rs_send, rs_recv, v_send, v_recv, x_send, x_recv, sem, out_sem,
):
    place = Place()
    mine = place.c
    a3_ref = x_ref.at[0:1024]
    gather = Gather(
        place, (qs_ref, out_hbm, up_hbm, vloc_ref, down_hbm), w_ref, d_ref, vecs_ref, ag_send, ag_recv, ag_local
    )
    scatter = Scatter(
        place, w_ref, d_ref, (ring0, ring1, ring2, ring3, ring4, ring5, ring6, ring7, land_ref, landd_ref, own_ref, ownd_ref), rs_send, rs_recv
    )
    barrier = pltpu.get_barrier_semaphore()
    for device in (place.sibling, place.beside, place.across, place.along(1), place.along(2), place.along(3)):
        pl.semaphore_signal(barrier, 1, device_id=device, device_id_type=MESH)
    load_x = pltpu.make_async_copy(x_hbm, x_ref.at[0:1024], sem.at[0])
    load_cot = pltpu.make_async_copy(cot_hbm, cot_ref, sem.at[1])
    loads = [
        pltpu.make_async_copy(
            qkv_hbm.at[:, D * part + 256 * group : D * part + 256 * group + 256],
            qs_ref.at[:, D * group + 256 * part : D * group + 256 * part + 256],
            sem.at[5 + 3 * group + part],
        )
        for group in range(3)
        for part in range(3)
    ]
    begin(loads)
    load_x.start()
    load_cot.start()
    def lane_match(rows, cols, shift, limit):
        row = lax.broadcasted_iota(jnp.int32, (rows, cols), 0)
        col = lax.broadcasted_iota(jnp.int32, (rows, cols), 1)
        return (row - col == shift) & (col < limit)

    owner = place.z * 4 + place.y * 2 + place.k
    inner = place.y * 2 + place.k
    spread = jnp.where(lane_match(48, D, -48 * owner, D), 1.0, 0.0).astype(BF16)
    vloc_ref[0:8, :] = dot(rows_ref[...], spread, 1, 0).astype(BF16)
    spread = jnp.where(lane_match(192, D, -192 * inner, D), 1.0, 0.0).astype(BF16)
    wide = dot(jnp.broadcast_to(bup_own_ref[...], (8, 192)), spread, 1, 0)
    chosen = lax.broadcasted_iota(jnp.int32, (8, D), 0) == place.z
    vloc_ref[8:16, :] = jnp.where(chosen, wide, 0.0).astype(BF16)
    pl.semaphore_wait(barrier, 6)
    for copy in loads:
        copy.wait()

    def give(part):
        start = pl.multiple_of((part // 2) * 512 + mine * BLK + (part % 2) * 128, 128)
        return send(
            x_hbm.at[pl.ds(start, 128)],
            x_ref.at[1024 + part * 128 : 1152 + part * 128],
            x_send.at[part],
            x_recv.at[part],
            place.beside,
        )

    def give_back(part):
        rows = slice(part * 128, part * 128 + 128)
        return send(
            a2_ref.at[rows], bias_ref.at[rows], x_send.at[4 + part], x_recv.at[4 + part], place.beside
        )

    rounds = (
        [(0, place.sibling)],
        [(1, place.beside)],
        [(2, place.across)],
        [(3, place.along(1)), (4, place.along(2)), (5, place.along(3))],
    )

    def exchange(index, device):
        return send(vg_ref, vr_ref.at[index], v_send.at[index], v_recv.at[index], device)

    def vectors(number):
        if number > 0:
            for index, device in rounds[number - 1]:
                exchange(index, device).wait()
            value = vg_ref[...]
            for index, _ in rounds[number - 1]:
                value = value + vr_ref[index]
            vg_ref[...] = value
        if number < 4:
            for index, device in rounds[number]:
                exchange(index, device).start()

    def piece(number):
        return None if number == 12 else number if number < 8 else ("d", number - 8)

    places = (5, 6, 7, 4, 0, 1, 2, 3, 0, 1, 2, 3)

    def step(code):
        kind, rest = code // 100, code % 100
        if kind < 10:
            gather.stage(kind, piece(rest))
        elif kind < 20:
            scatter.stage(kind - 10, piece(rest), places[rest])
        elif kind == 20:
            if 8 <= rest < 12:
                gather.start_down(rest - 8)
            else:
                gather.start(piece(rest))
        elif kind == 21:
            give(rest).start()
        elif kind == 22:
            give_back(rest).start()
        else:
            vectors(rest)

    def at(slot):
        for code in PLAN.get(slot, ()):
            step(code)

    def at_loop(slot, index, count):
        for i in range(count):
            if PLAN.get(slot + i):

                @pl.when(index == i)
                def _():
                    at(slot + i)

    def weight(index):
        return w_ref[index].reshape(D, D)

    def weight_down(index):
        return d_ref[index].reshape(D, D)

    def vec(row):
        return vec_ref[row : row + 1, :]

    def add_vec(row, value):
        vg_ref[row : row + 1, :] += value

    at(0)
    vg_ref[...] = jnp.zeros_like(vg_ref)
    attention_masks(seg_ref, bias_ref, mine)
    at(1)
    total = vecs_ref[0, 0, 0].astype(F32)
    for shard in range(1, 16):
        total = total + vecs_ref[shard // 4, (shard // 2) % 2, shard % 2].astype(F32)
    vec_ref[...] = total
    load_x.wait()

    def first_norm(r):
        rows = pl.ds(r * BLK, BLK)
        normed, _ = norm(x_ref[rows, :].astype(F32))
        a1_ref[rows, :] = (normed * vec(0) + vec(1)).astype(BF16)

    loop(4, first_norm)
    refs = (q_ref, k_ref, v_ref, o_ref, p_ref, bias_ref)
    for g in range(3):
        at(10 + 10 * g)
        cols = slice(256 * g, 256 * g + 256)
        mixed = dot(a1_ref[0:1024, :], weight(g), 1, 0)
        q_ref[:, cols] = ((mixed[:, :256] + vec(2)[:, cols]).astype(BF16) * 0.125).astype(BF16)
        k_ref[0:1024, cols] = mixed[:, 256:512].astype(BF16)
        v_ref[0:1024, cols] = (mixed[:, 512:] + vec(3)[:, cols]).astype(BF16)

        def solo(m):
            at_loop(11 + 10 * g, m, 2)
            forward_heads(m, g, refs, mine, (0,))

        loop(2, solo)
    at(40)
    for part in range(4):
        give(part).wait_recv()
    loop(2, lambda r: first_norm(4 + r))
    for g in range(3):
        cols = slice(256 * g, 256 * g + 256)
        mixed = dot(a1_ref[1024:1536, :], weight(g)[:, 256:], 1, 0)
        k_ref[1024:1536, cols] = mixed[:, :256].astype(BF16)
        v_ref[1024:1536, cols] = (mixed[:, 256:] + vec(3)[:, cols]).astype(BF16)

    def wide(i):
        at_loop(41, i, 6)
        forward_heads(i // 3, i % 3, refs, mine, (1, 2))

    loop(6, wide)

    at(50)
    acc_ref[...] = dot(o_ref[...], weight(3), 1, 0)
    load_cot.wait()
    at(51)

    def second_norm(r):
        rows = pl.ds(r * BLK, BLK)
        resid = acc_ref[rows, :] + x_ref[rows, :].astype(F32) + vec(4)
        normed, inverse = norm(resid)
        acc_ref[rows, :] = resid + vec(7)
        n2_ref[rows, :] = normed.astype(BF16)
        a2_ref[rows, :] = (normed * vec(5) + vec(6)).astype(BF16)
        rs2_ref[:, lanes(r, BLK)] = jnp.broadcast_to(inverse, (BLK, 128)).T[0:8]
        add_vec(7, colsum(cot_ref[rows, :].astype(F32)))
        g2_ref[rows, :] = jnp.zeros((BLK, D), F32)

    loop(4, second_norm)
    for j in range(4):
        bup_ref[j, 0:1] = vec(8 + j)
        bup_ref[j, 1:2] = jnp.zeros((1, D), F32)

    def feed(j):
        up = 4 + j
        bias = bup_ref[j, 0:1]

        def at_chunk(slot):
            for i in range(4):
                if PLAN.get(slot + 10 * i):

                    @pl.when(j == i)
                    def _():
                        at(slot + 10 * i)

        def part(r):
            rows = slice(r * 512, r * 512 + 512)
            u = dot(a2_ref[rows, :], weight(up), 1, 0) + bias
            back = dot(cot_ref[rows, :], weight_down(j), 1, 1)
            square = u * u
            th = jnp.tanh(u * (0.7978845608028654 + 0.035677408136300125 * square))
            half_up = 0.5 + 0.5 * th
            a3_ref[rows, :] = (u * half_up).astype(BF16)
            slope = half_up + (half_up * (1.0 - th)) * (u * (0.7978845608028654 + 0.10703222440890037 * square))
            gu = (back * slope).astype(BF16)
            gu_ref[rows, :] = gu
            bup_ref[j, 1:2] += colsum(gu.astype(F32))

        at_chunk(60)
        part(0)
        at_chunk(61)
        part(1)
        at_chunk(62)
        acc_ref[...] += dot(a3_ref[...], weight_down(j), 1, 0)
        g2_ref[...] += dot(gu_ref[...], weight(up), 1, 1)
        at_chunk(63)
        gather.stage(6, up)
        w_ref[up] = dot(a2_ref[...], gu_ref[...], 0, 0).astype(BF16).reshape(4, 2, 2, 48, D)
        at_chunk(64)
        gather.stage(6, ("d", j))
        d_ref[j] = dot(a3_ref[...], cot_ref[...], 0, 0).astype(BF16).reshape(2, 2, 192, D)

    loop(4, feed)
    at(100)
    for j in range(4):
        vg_ref[8 + j : 9 + j, :] = bup_ref[j, 1:2]

    def second_back(r):
        rows = pl.ds(r * BLK, BLK)
        a3_ref[rows, :] = acc_ref[rows, :].astype(BF16)
        g2 = g2_ref[rows, :]
        normed = n2_ref[rows, :].astype(F32)
        add_vec(5, colsum(g2 * normed))
        add_vec(6, colsum(g2))
        inverse = jnp.broadcast_to(rs2_ref[0:1, lanes(r, BLK)], (128, BLK)).T[:, 0:1]
        t = g2 * vec(5)
        first = jnp.mean(t, -1, keepdims=True)
        second = jnp.mean(t * normed, -1, keepdims=True)
        grad = cot_ref[rows, :].astype(F32) + inverse * (t - first - normed * second)
        g2_ref[rows, :] = grad
        lowered = grad.astype(BF16)
        a2_ref[rows, :] = lowered
        add_vec(4, colsum(lowered.astype(F32)))

    loop(4, second_back)
    out_copies = [
        pltpu.make_async_copy(x_ref.at[micro * 512 : micro * 512 + 512], act_hbm.at[micro, 0], sem.at[3 + micro])
        for micro in range(2)
    ]
    begin(out_copies)
    at(101)
    gu_ref[...] = dot(a2_ref[...], weight(3), 1, 1).astype(BF16)
    at(102)
    gather.stage(6, 3)
    w_ref[3] = dot(o_ref[...], a2_ref[...], 0, 0).astype(BF16).reshape(4, 2, 2, 48, D)
    refs = (q_ref, k_ref, v_ref, gu_ref, p_ref)

    for g in range(3):
        cols = slice(256 * g, 256 * g + 256)

        def back(m):
            at_loop(120 + 10 * g, m, 2)
            backward_heads(m, g, refs, mine, (1, 2))
            backward_heads(m, g, refs, mine, (0,))

        loop(2, back)
        at(122 + 10 * g)
        scatter.finish_block(4 + g, g)
        mixed = jnp.concatenate([k_ref[:, cols], v_ref[:, cols]], 1)
        w_ref[4 + g, :, :, :, :, 0:256] = (
            dot(a1_ref[0:1024, :], q_ref[:, cols], 0, 0).astype(BF16).reshape(4, 2, 2, 48, 256)
        )
        w_ref[4 + g, :, :, :, :, 256:] = dot(a1_ref[...], mixed, 0, 0).astype(BF16).reshape(4, 2, 2, 48, 512)
    at(110)
    for g in range(3):
        cols = slice(256 * g, 256 * g + 256)
        mixed = jnp.concatenate([k_ref[1024:1536, cols], v_ref[1024:1536, cols]], 1)
        value = dot(mixed, weight(g)[:, 256:], 1, 1)
        acc_ref[0:512, :] = value if g == 0 else acc_ref[0:512, :] + value
    a2_ref[0:512, :] = acc_ref[0:512, :].astype(BF16)
    for copy in out_copies:
        copy.wait()
    load_x.start()

    for g in range(3):
        at(150 + g)
        cols = slice(256 * g, 256 * g + 256)
        mixed = jnp.concatenate([q_ref[:, cols], k_ref[0:1024, cols], v_ref[0:1024, cols]], 1)
        value = dot(mixed, weight(g), 1, 1)
        acc_ref[...] = value if g == 0 else acc_ref[...] + value
    at(153)
    add_vec(2, colsum(q_ref[...].astype(F32)))
    add_vec(3, colsum(v_ref[...].astype(F32)))
    at(154)

    def extra_back(r):
        rows = pl.ds(1024 + r * BLK, BLK)
        normed, _ = norm(x_ref[rows, :].astype(F32))
        g1 = a2_ref[pl.ds(r * BLK, BLK), :].astype(F32)
        add_vec(0, colsum(g1 * normed))
        add_vec(1, colsum(g1))

    loop(2, extra_back)

    def first_sums(r):
        rows = pl.ds(r * BLK, BLK)
        normed, inverse = norm(x_ref[rows, :].astype(F32))
        g1 = acc_ref[rows, :]
        add_vec(0, colsum(g1 * normed))
        add_vec(1, colsum(g1))

    load_x.wait()
    loop(4, first_sums)
    at(155)
    for part in range(4):
        give_back(part).wait_recv()

    def first_back(r):
        rows = pl.ds(r * BLK, BLK)
        normed, inverse = norm(x_ref[rows, :].astype(F32))
        t = acc_ref[rows, :] * vec(0)
        first = jnp.mean(t, -1, keepdims=True)
        second = jnp.mean(t * normed, -1, keepdims=True)
        gu_ref[rows, :] = (g2_ref[rows, :] + inverse * (t - first - normed * second)).astype(BF16)

    for micro in range(2):
        rows = pl.ds(pl.multiple_of(micro * 512 + mine * BLK, BLK), BLK)
        acc_ref[rows, :] += bias_ref[micro * BLK : micro * BLK + BLK, :].astype(F32)
    loop(4, first_back)
    gx_copies = [
        pltpu.make_async_copy(gu_ref.at[micro * 512 : micro * 512 + 512], gx_hbm.at[micro, 0], sem.at[3 + micro])
        for micro in range(2)
    ]
    begin(gx_copies)
    at(156)
    for block in range(12):
        scatter.stage(5, piece(block), places[block])
    pick = jnp.where(lane_match(D, 128, 48 * owner, 48), 1.0, 0.0)
    highest = lax.Precision.HIGHEST
    small_ref[0:8, 0:128] = jnp.dot(vg_ref[0:8, :], pick, precision=highest, preferred_element_type=F32)
    pick = jnp.where(lane_match(D, 256, 192 * inner, 192), 1.0, 0.0)
    chosen = lax.broadcasted_iota(jnp.int32, (8, D), 0) == place.z
    value = colsum(jnp.where(chosen, vg_ref[8:16, :], 0.0))
    small_ref[8:16, :] = jnp.dot(
        jnp.broadcast_to(value, (8, D)), pick, precision=highest, preferred_element_type=F32
    )
    ends = [pltpu.make_async_copy(small_ref, vg_hbm, sem.at[2])]
    for block in range(8):
        ends += scatter.store(block, fin_hbm.at[block], out_sem.at[block])
    ends += scatter.store(("d", 0), find_hbm, out_sem.at[8])
    for copy in ends:
        copy.start()
    for block in range(12):
        if 4 <= block < 7:
            scatter.last(block).wait_send()
        else:
            scatter.finish(piece(block), places[block])
    for part in (None, 0, 1, 2):
        gather.stage(6, part)
    gather.finish()
    for part in range(4):
        give(part).wait_send()
        give_back(part).wait_send()
    for copy in gx_copies:
        copy.wait()
    for copy in ends:
        copy.wait()


def hand_out(
    act_ref, gx_ref, fin_ref, find_ref, small_ref, act_out, gx_out, qkv_ref, out_ref, up_ref, down_ref, *rest
):
    vectors = rest
    act_out[...] = act_ref[...]
    gx_out[...] = gx_ref[...]
    for part in range(3):
        for g in range(3):
            start = D * part + 256 * g
            qkv_ref[:, start : start + 256] = fin_ref[g, :, 256 * part : 256 * part + 256].astype(F32)
    out_ref[...] = fin_ref[3].astype(F32)
    for j in range(4):
        up_ref[:, D * j : D * j + D] = fin_ref[4 + j].astype(F32)
    down_ref[...] = find_ref[...].astype(F32)
    for i in range(8):
        vectors[i][...] = small_ref[i : i + 1, 0:48]
    vectors[8][...] = small_ref[8:9, 0:192]


def fast_device(
    layer_input, segments, ln1_gain, ln1_bias, w_qkv, q_bias, v_bias, w_attn_out, b_attn_out,
    ln2_gain, ln2_bias, w_up, b_up, w_down, b_down, cotangent,
):
    rows = jnp.stack([ln1_gain, ln1_bias, q_bias, v_bias, b_attn_out, ln2_gain, ln2_bias, b_down])
    big = lambda *shape, dtype=BF16: jax.ShapeDtypeStruct(shape, dtype)
    hbm = pl.BlockSpec(memory_space=pltpu.HBM)
    vmem = pl.BlockSpec(memory_space=pltpu.VMEM)
    act, gx, fin, find, small = pl.pallas_call(
        layer_kernel,
        out_shape=(
            big(2, 1, 512, D), big(2, 1, 512, D), big(8, 48, D), big(192, D), big(16, 256, dtype=F32),
        ),
        in_specs=[hbm, hbm, vmem, hbm, hbm, hbm, vmem, vmem, hbm],
        out_specs=(hbm,) * 5,
        scratch_shapes=[
            pltpu.VMEM((8, 4, 2, 2, 48, D), BF16),
            pltpu.VMEM((4, 2, 2, 192, D), BF16),
            pltpu.VMEM((4, 2, 2, 16, D), BF16),
            pltpu.VMEM((16, D), F32),
            pltpu.VMEM((1536, D), BF16),
            pltpu.VMEM((1024, D), BF16),
            pltpu.VMEM((1024, D), BF16),
            pltpu.VMEM((1536, D), BF16),
            pltpu.VMEM((1536, D), BF16),
            pltpu.VMEM((1024, D), BF16),
            pltpu.VMEM((12, 2, 3 * BLK, BLK), BF16),
            pltpu.VMEM((2 * BLK, 3 * BLK), BF16),
            pltpu.VMEM((1024, D), F32),
            pltpu.VMEM((1024, D), BF16),
            pltpu.VMEM((1024, D), BF16),
            pltpu.VMEM((8, 1024), F32),
            pltpu.VMEM((1024, D), F32),
            pltpu.VMEM((1536, D), BF16),
            pltpu.VMEM((1024, D), BF16),
            pltpu.VMEM((16, D), F32),
            pltpu.VMEM((4, 8, D), F32),
            pltpu.VMEM((3, 4, 2, 48, D), BF16),
            pltpu.VMEM((2, 2, 192, D), BF16),
            pltpu.VMEM((4, 4, 2, 48, HALF), BF16),
            pltpu.VMEM((4, 2, 192, HALF), BF16),
            pltpu.VMEM((4, 4, 48, HALF), BF16),
            pltpu.VMEM((4, 192, HALF), BF16),
            pltpu.VMEM((4, 3, 48, HALF), BF16),
            pltpu.VMEM((3, 192, HALF), BF16),
            pltpu.VMEM((8, 48, HALF), BF16),
            pltpu.VMEM((192, HALF), BF16),
            pltpu.VMEM((8, 48, HALF), BF16),
            pltpu.VMEM((192, HALF), BF16),
            pltpu.VMEM((6, 16, D), F32),
            pltpu.VMEM((48, 3 * D), BF16),
            pltpu.VMEM((16, D), BF16),
            pltpu.VMEM((16, 256), F32),
            pltpu.SemaphoreType.DMA((14, 12)),
            pltpu.SemaphoreType.DMA((14, 12)),
            pltpu.SemaphoreType.DMA((13,)),
            pltpu.SemaphoreType.DMA((12, 8)),
            pltpu.SemaphoreType.DMA((12, 8)),
            pltpu.SemaphoreType.DMA((6,)),
            pltpu.SemaphoreType.DMA((6,)),
            pltpu.SemaphoreType.DMA((8,)),
            pltpu.SemaphoreType.DMA((8,)),
            pltpu.SemaphoreType.DMA((14,)),
            pltpu.SemaphoreType.DMA((9, 2)),
        ],
        compiler_params=pltpu.CompilerParams(
            vmem_limit_bytes=66_500_000, collective_id=0, has_side_effects=True
        ),
        name="layer",
    )(
        layer_input.reshape(1024, D), cotangent.reshape(1024, D), segments,
        w_qkv, w_attn_out, w_up, rows, b_up[None], w_down,
    )
    blocks = pl.BlockSpec()
    f32 = lambda *shape: jax.ShapeDtypeStruct(shape, F32)
    act, gx, g_qkv, g_out, g_up, g_down, *vectors = pl.pallas_call(
        hand_out,
        out_shape=(
            big(2, 1, 512, D), big(2, 1, 512, D), f32(48, 3 * D), f32(48, D), f32(48, 4 * D), f32(192, D),
        ) + (f32(1, 48),) * 8 + (f32(1, 192),),
        in_specs=[blocks] * 5,
        out_specs=(blocks,) * 15,
        name="hand_out",
    )(act, gx, fin, find, small)
    part = [v[0] for v in vectors]
    return (
        act, gx, part[0], part[1], g_qkv, part[2], part[3], g_out, part[4], part[5], part[6], g_up, part[8], g_down, part[7],
    )


def solution(mesh):
    in_specs = (
        P(None, "fsdp", "ctx", None),
        P(None, "fsdp", None),
        P("fsdp"),
        P("fsdp"),
        P("fsdp", None),
        P("fsdp"),
        P("fsdp"),
        P("fsdp", None),
        P("fsdp"),
        P("fsdp"),
        P("fsdp"),
        P("fsdp", None),
        P("fsdp"),
        P("fsdp", None),
        P("fsdp"),
        P(None, "fsdp", "ctx", None),
    )
    out_specs = (
        P(None, "fsdp", "ctx", None),
        P(None, "fsdp", "ctx", None),
        P("fsdp"),
        P("fsdp"),
        P("fsdp", None),
        P("fsdp"),
        P("fsdp"),
        P("fsdp", None),
        P("fsdp"),
        P("fsdp"),
        P("fsdp"),
        P("fsdp", None),
        P("fsdp"),
        P("fsdp", None),
        P("fsdp"),
    )
    fast = mesh.shape["ctx"] == 2 and mesh.shape["fsdp"] == 16
    return jax.shard_map(
        fast_device if fast else on_device, mesh=mesh, in_specs=in_specs, out_specs=out_specs, check_vma=False
    )
```

```python
import jax
import jax.numpy as jnp
from jax import lax
from jax.experimental import pallas as pl
from jax.experimental.pallas import tpu as pltpu
from jax.sharding import PartitionSpec as P

H = 12


def stored_positions(length, groups):
    block_size = length // (2 * groups)
    stored = jnp.arange(length, dtype=jnp.int32)
    holder = stored // (2 * block_size)
    within = stored % (2 * block_size)
    second = within // block_size
    offset = within % block_size
    block_index = jnp.where(second == 0, holder, 2 * groups - 1 - holder)
    return block_index * block_size + offset


def normalize_parts(values):
    center = jnp.mean(values, -1, keepdims=True)
    centered = values - center
    inverse = lax.rsqrt(jnp.mean(centered * centered, -1, keepdims=True) + 1e-05)
    return (centered * inverse, inverse)


def normalize_back(grad_normed, normed, inverse):
    first = jnp.mean(grad_normed, -1, keepdims=True)
    second = jnp.mean(grad_normed * normed, -1, keepdims=True)
    return inverse * (grad_normed - first - normed * second)


def tile_allowed(query_pos, query_seg, key_pos, key_seg):
    return (key_pos[None, :] <= query_pos[:, None]) & (key_seg[None, :] == query_seg[:, None])


def tile_scores(query, keys_tile, allowed):
    scores = (
        jnp.einsum("qhd,khd->hqk", query, keys_tile, preferred_element_type=jnp.float32) * 0.125
    )
    return jnp.where(allowed[None], scores, -1e30)


def online_softmax(query, query_pos, query_seg, tiles):
    heads = query.shape[1]
    count_rows = query.shape[0]

    def advance(carry, tile):
        keys_tile, values_tile, key_pos, key_seg = tile
        allowed = tile_allowed(query_pos, query_seg, key_pos, key_seg)

        def compute(state):
            peak, total, accum = state
            scores = tile_scores(query, keys_tile, allowed)
            new_peak = jnp.maximum(peak, jnp.max(scores, -1))
            terms = jnp.where(allowed[None], jnp.exp(scores - new_peak[..., None]), 0.0)
            factor = jnp.exp(peak - new_peak)
            upper = terms.astype(jnp.bfloat16)
            lower = (terms - upper.astype(jnp.float32)).astype(jnp.bfloat16)
            added = jnp.einsum(
                "hqk,khd->qhd", upper, values_tile, preferred_element_type=jnp.float32
            )
            added = added + jnp.einsum(
                "hqk,khd->qhd", lower, values_tile, preferred_element_type=jnp.float32
            )
            accum = accum * jnp.transpose(factor)[..., None] + added
            return (new_peak, total * factor + jnp.sum(terms, -1), accum)

        return (compute(carry), None)

    start_state = (
        jnp.full((heads, count_rows), -1e30, jnp.float32),
        jnp.zeros((heads, count_rows), jnp.float32),
        jnp.zeros(query.shape, jnp.float32),
    )
    (peak, total, accum), unused = lax.scan(advance, start_state, tiles)
    exact = accum / jnp.transpose(total)[..., None]
    return (peak + jnp.log(total), exact)


def attention_out(query, log_total, query_pos, query_seg, tiles):

    def advance(carry, tile):
        keys_tile, values_tile, key_pos, key_seg = tile
        allowed = tile_allowed(query_pos, query_seg, key_pos, key_seg)

        def compute(summed):
            scores = tile_scores(query, keys_tile, allowed)
            probs = jnp.where(allowed[None], jnp.exp(scores - log_total[..., None]), 0.0)
            lowered = probs.astype(jnp.bfloat16)
            return summed + jnp.einsum(
                "hqk,khd->qhd", lowered, values_tile, preferred_element_type=jnp.float32
            )

        return (compute(carry), None)

    summed, unused = lax.scan(advance, jnp.zeros(query.shape, jnp.float32), tiles)
    return summed


def attention_back(query, log_total, grad_attended, delta, query_pos, query_seg, tiles):

    def advance(grad_query, tile):
        keys_tile, values_tile, key_pos, key_seg = tile
        allowed = tile_allowed(query_pos, query_seg, key_pos, key_seg)

        def compute(carry_query):
            scores = tile_scores(query, keys_tile, allowed)
            probs = jnp.where(allowed[None], jnp.exp(scores - log_total[..., None]), 0.0)
            lowered = probs.astype(jnp.bfloat16)
            grad_values = jnp.einsum(
                "hqk,qhd->khd", lowered, grad_attended, preferred_element_type=jnp.float32
            )
            grad_probs = jnp.einsum(
                "qhd,khd->hqk", grad_attended, values_tile, preferred_element_type=jnp.float32
            )
            grad_scores = (probs * (grad_probs - delta[..., None])).astype(jnp.bfloat16)
            new_query = carry_query + 0.125 * jnp.einsum(
                "hqk,khd->qhd", grad_scores, keys_tile, preferred_element_type=jnp.float32
            )
            grad_keys = 0.125 * jnp.einsum(
                "hqk,qhd->khd", grad_scores, query, preferred_element_type=jnp.float32
            )
            return (new_query, grad_keys, grad_values)

        new_query, grad_keys, grad_values = compute(grad_query)
        return (new_query, (grad_keys, grad_values))

    grad_query, (grad_keys, grad_values) = lax.scan(
        advance, jnp.zeros(query.shape, jnp.float32), tiles
    )
    return (grad_query, grad_keys, grad_values)


def column_sums(values):
    return jnp.sum(values.astype(jnp.float32), 0)


def layer_pass(inputs, cots, seg_row, weights, positions, start):
    (
        gain_one,
        shift_one,
        proj_mixed,
        bias_query,
        bias_value,
        proj_out,
        bias_out,
        gain_two,
        shift_two,
        proj_up,
        bias_up,
        proj_down,
        bias_down,
    ) = weights
    count_rows = inputs.shape[0]
    width = inputs.shape[1]
    heads = H
    head_size = width // heads
    length = seg_row.shape[0]
    query_pos = lax.dynamic_slice_in_dim(positions, start, count_rows)
    query_seg = lax.dynamic_slice_in_dim(seg_row, start, count_rows)
    values_in = inputs.astype(jnp.float32)
    normed_one, inverse_one = normalize_parts(values_in)
    lowered_one = (
        normed_one * gain_one.astype(jnp.float32) + shift_one.astype(jnp.float32)
    ).astype(jnp.bfloat16)
    mixed_bias = jnp.concatenate(
        [
            bias_query.astype(jnp.float32),
            jnp.zeros((width,), jnp.float32),
            bias_value.astype(jnp.float32),
        ]
    )
    mixed = (
        jnp.dot(lowered_one, proj_mixed, preferred_element_type=jnp.float32) + mixed_bias
    ).astype(jnp.bfloat16)
    query = mixed[:, :width].reshape(count_rows, heads, head_size)
    keys_values = lax.all_gather(mixed[:, width:], "ctx", axis=0, tiled=True)
    block = min(512, length)
    count = length // block
    tiles = (
        keys_values[:, :width].reshape(count, block, heads, head_size),
        keys_values[:, width:].reshape(count, block, heads, head_size),
        positions.reshape(count, block),
        seg_row.reshape(count, block),
    )
    log_total, exact = online_softmax(query, query_pos, query_seg, tiles)
    summed = attention_out(query, log_total, query_pos, query_seg, tiles)
    attended = summed.reshape(count_rows, width).astype(jnp.bfloat16)
    branch = jnp.dot(attended, proj_out, preferred_element_type=jnp.float32) + bias_out.astype(
        jnp.float32
    )
    resid = values_in + branch
    normed_two, inverse_two = normalize_parts(resid)
    lowered_two = (
        normed_two * gain_two.astype(jnp.float32) + shift_two.astype(jnp.float32)
    ).astype(jnp.bfloat16)
    hidden = jnp.dot(lowered_two, proj_up, preferred_element_type=jnp.float32) + bias_up.astype(
        jnp.float32
    )

    def smooth(pre_active):
        return jax.nn.gelu(pre_active, approximate=True)

    active_full, gelu_back = jax.vjp(smooth, hidden)
    active = active_full.astype(jnp.bfloat16)
    down = jnp.dot(active, proj_down, preferred_element_type=jnp.float32) + bias_down.astype(
        jnp.float32
    )
    output = (resid + down).astype(jnp.bfloat16)
    grad_out = cots.astype(jnp.float32)
    grad_bias_down = column_sums(cots)
    grad_proj_down = jnp.einsum("tf,td->fd", active, cots, preferred_element_type=jnp.float32)
    grad_active = jnp.einsum("td,fd->tf", cots, proj_down, preferred_element_type=jnp.float32)
    grad_hidden = gelu_back(grad_active)[0].astype(jnp.bfloat16)
    grad_bias_up = column_sums(grad_hidden)
    grad_proj_up = jnp.einsum(
        "td,tf->df", lowered_two, grad_hidden, preferred_element_type=jnp.float32
    )
    grad_lowered_two = jnp.einsum(
        "tf,df->td", grad_hidden, proj_up, preferred_element_type=jnp.float32
    )
    grad_gain_two = jnp.sum(grad_lowered_two * normed_two, 0)
    grad_shift_two = jnp.sum(grad_lowered_two, 0)
    grad_resid = grad_out + normalize_back(
        grad_lowered_two * gain_two.astype(jnp.float32), normed_two, inverse_two
    )
    grad_branch = grad_resid.astype(jnp.bfloat16)
    grad_bias_out = column_sums(grad_branch)
    grad_proj_out = jnp.einsum(
        "td,te->de", attended, grad_branch, preferred_element_type=jnp.float32
    )
    grad_attended = jnp.einsum(
        "te,de->td", grad_branch, proj_out, preferred_element_type=jnp.float32
    ).astype(jnp.bfloat16)
    grad_attended = grad_attended.reshape(count_rows, heads, head_size)
    delta = jnp.einsum("qhd,qhd->hq", grad_attended.astype(jnp.float32), exact)
    grad_query, grad_keys, grad_values = attention_back(
        query, log_total, grad_attended, delta, query_pos, query_seg, tiles
    )
    grad_pairs = jnp.concatenate(
        [grad_keys.reshape(length, width), grad_values.reshape(length, width)], 1
    )
    grad_pairs_local = lax.psum_scatter(grad_pairs, "ctx", scatter_dimension=0, tiled=True)
    grad_mixed = jnp.concatenate(
        [grad_query.reshape(count_rows, width), grad_pairs_local], 1
    ).astype(jnp.bfloat16)
    grad_bias_query = column_sums(grad_mixed[:, :width])
    grad_bias_value = column_sums(grad_mixed[:, 2 * width :])
    grad_proj_mixed = jnp.einsum(
        "td,te->de", lowered_one, grad_mixed, preferred_element_type=jnp.float32
    )
    grad_lowered_one = jnp.einsum(
        "te,de->td", grad_mixed, proj_mixed, preferred_element_type=jnp.float32
    )
    grad_gain_one = jnp.sum(grad_lowered_one * normed_one, 0)
    grad_shift_one = jnp.sum(grad_lowered_one, 0)
    grad_input = grad_resid + normalize_back(
        grad_lowered_one * gain_one.astype(jnp.float32), normed_one, inverse_one
    )
    grads = (
        grad_gain_one,
        grad_shift_one,
        grad_proj_mixed,
        grad_bias_query,
        grad_bias_value,
        grad_proj_out,
        grad_bias_out,
        grad_gain_two,
        grad_shift_two,
        grad_proj_up,
        grad_bias_up,
        grad_proj_down,
        grad_bias_down,
    )
    return (output, grad_input.astype(jnp.bfloat16), grads)


def fetch(shards):
    return (
        lax.all_gather(shards[0], "fsdp", axis=0, tiled=True),
        lax.all_gather(shards[1], "fsdp", axis=0, tiled=True),
        lax.all_gather(shards[2], "fsdp", axis=0, tiled=True),
        lax.all_gather(shards[3], "fsdp", axis=0, tiled=True),
        lax.all_gather(shards[4], "fsdp", axis=0, tiled=True),
        lax.all_gather(shards[5], "fsdp", axis=0, tiled=True),
        lax.all_gather(shards[6], "fsdp", axis=0, tiled=True),
        lax.all_gather(shards[7], "fsdp", axis=0, tiled=True),
        lax.all_gather(shards[8], "fsdp", axis=0, tiled=True),
        lax.all_gather(shards[9], "fsdp", axis=0, tiled=True),
        lax.all_gather(shards[10], "fsdp", axis=0, tiled=True),
        lax.all_gather(shards[11], "fsdp", axis=0, tiled=True),
        lax.all_gather(shards[12], "fsdp", axis=0, tiled=True),
    )


def share(grads):
    return (
        lax.psum_scatter(grads[0], "fsdp", scatter_dimension=0, tiled=True),
        lax.psum_scatter(grads[1], "fsdp", scatter_dimension=0, tiled=True),
        lax.psum_scatter(grads[2], "fsdp", scatter_dimension=0, tiled=True),
        lax.psum_scatter(grads[3], "fsdp", scatter_dimension=0, tiled=True),
        lax.psum_scatter(grads[4], "fsdp", scatter_dimension=0, tiled=True),
        lax.psum_scatter(grads[5], "fsdp", scatter_dimension=0, tiled=True),
        lax.psum_scatter(grads[6], "fsdp", scatter_dimension=0, tiled=True),
        lax.psum_scatter(grads[7], "fsdp", scatter_dimension=0, tiled=True),
        lax.psum_scatter(grads[8], "fsdp", scatter_dimension=0, tiled=True),
        lax.psum_scatter(grads[9], "fsdp", scatter_dimension=0, tiled=True),
        lax.psum_scatter(grads[10], "fsdp", scatter_dimension=0, tiled=True),
        lax.psum_scatter(grads[11], "fsdp", scatter_dimension=0, tiled=True),
        lax.psum_scatter(grads[12], "fsdp", scatter_dimension=0, tiled=True),
    )


def on_device(
    layer_input,
    segments,
    ln1_gain,
    ln1_bias,
    w_qkv,
    q_bias,
    v_bias,
    w_attn_out,
    b_attn_out,
    ln2_gain,
    ln2_bias,
    w_up,
    b_up,
    w_down,
    b_down,
    cotangent,
):
    shards = (
        ln1_gain,
        ln1_bias,
        w_qkv,
        q_bias,
        v_bias,
        w_attn_out,
        b_attn_out,
        ln2_gain,
        ln2_bias,
        w_up,
        b_up,
        w_down,
        b_down,
    )
    micro = layer_input.shape[0]
    count_rows = layer_input.shape[2]
    length = segments.shape[2]
    positions = stored_positions(length, lax.axis_size("ctx"))
    start = lax.axis_index("ctx") * count_rows
    outputs = []
    input_grads = []
    shared = None
    for number in range(micro):
        weights = fetch(shards)
        output, grad_input, grads = layer_pass(
            layer_input[number, 0],
            cotangent[number, 0],
            segments[number, 0],
            weights,
            positions,
            start,
        )
        summed = share(grads)
        shared = summed if shared is None else jax.tree.map(jnp.add, shared, summed)
        outputs.append(output)
        input_grads.append(grad_input)
    final = lax.psum(
        (
            shared[0],
            shared[1],
            shared[2],
            shared[3],
            shared[4],
            shared[5],
            shared[6],
            shared[7],
            shared[8],
            shared[9],
            shared[10],
            shared[11],
            shared[12],
        ),
        "ctx",
    )
    activations = jnp.stack(outputs)[:, None]
    input_grad = jnp.stack(input_grads)[:, None]
    return (
        activations,
        input_grad,
        final[0],
        final[1],
        final[2],
        final[3],
        final[4],
        final[5],
        final[6],
        final[7],
        final[8],
        final[9],
        final[10],
        final[11],
        final[12],
    )


D = 768
HD = 64
BLK = 256
NEG = -1e30
F32 = jnp.float32
BF16 = jnp.bfloat16


def dot(lhs, rhs, lhs_dim, rhs_dim):
    return lax.dot_general(
        lhs, rhs, (((lhs_dim,), (rhs_dim,)), ((), ())), preferred_element_type=F32
    )


def norm(v):
    center = v - jnp.mean(v, -1, keepdims=True)
    inverse = lax.rsqrt(jnp.mean(center * center, -1, keepdims=True) + 1e-05)
    return center * inverse, inverse


def colsum(v):
    return jnp.sum(v, 0, keepdims=True)


def loop(count, body):
    def step(index, carry):
        body(index)
        return carry

    lax.fori_loop(0, count, step, 0)


def lanes(index, size):
    return pl.ds(pl.multiple_of(index * size, size), size)


def attention_masks(seg_ref, bias_ref, mine):
    key = lax.broadcasted_iota(jnp.int32, (BLK, BLK), 0)
    query = lax.broadcasted_iota(jnp.int32, (BLK, BLK), 1)
    causal = key <= query
    for micro in range(2):

        def row(start):
            piece = seg_ref[micro, :, pl.ds(pl.multiple_of(start, BLK), BLK)]
            return jnp.broadcast_to(piece.astype(F32), (BLK, BLK))

        solo = row(mine * 2 * BLK + mine * BLK)
        wide = row(mine * 2 * BLK + (1 - mine) * BLK)
        extra = row((1 - mine) * 3 * BLK)
        rows = slice(micro * BLK, micro * BLK + BLK)
        tiles = ((solo.T == solo) & causal, extra.T == wide, (wide.T == wide) & causal)
        for t, allowed in enumerate(tiles):
            bias_ref[rows, t * BLK : t * BLK + BLK] = jnp.where(allowed, 0.0, NEG).astype(BF16)


def attention_rows(micro, mine):
    solo = pl.ds(pl.multiple_of(micro * 2 * BLK + mine * BLK, BLK), BLK)
    wide = pl.ds(pl.multiple_of(micro * 2 * BLK + (1 - mine) * BLK, BLK), BLK)
    extra = pl.ds(pl.multiple_of(1024 + micro * BLK, BLK), BLK)
    return solo, wide, extra


def halves(value):
    left = lax.broadcasted_iota(jnp.int32, value.shape, 1) < HD
    zero = jnp.zeros_like(value)
    return jnp.where(left, value, zero), jnp.where(left, zero, value)


def heads_of(group, which):
    return lanes(2 * group + which, 128)


def column_softmax(rows):
    peaks = []
    for tiles in rows:
        peak = tiles[0].max(0, keepdims=True)
        for tile in tiles[1:]:
            peak = jnp.maximum(peak, tile.max(0, keepdims=True))
        peaks.append(peak)
    terms = [[jnp.exp(tile - peak) for tile in tiles] for tiles, peak in zip(rows, peaks)]
    scales = []
    for tiles in terms:
        total = colsum(tiles[0])
        for tile in tiles[1:]:
            total = total + colsum(tile)
        scales.append(1.0 / total)
    return [[(tile * scale).astype(BF16) for tile in tiles] for tiles, scale in zip(terms, scales)]


def forward_heads(micro, group, refs, mine, tiles):
    q_ref, k_ref, v_ref, o_ref, p_ref, bias_ref = refs
    solo, wide, extra = attention_rows(micro, mine)
    queries = solo if tiles == (0,) else wide
    keys = [(solo, extra, wide)[t] for t in tiles]
    pairs = [heads_of(group, which) for which in range(2)]
    k = [[k_ref[rows, pair] for rows in keys] for pair in pairs]
    vt = [[v_ref[rows, pair].T for rows in keys] for pair in pairs]
    q = [halves(q_ref[queries, pair]) for pair in pairs]
    rows = pl.ds(pl.multiple_of(micro * BLK, BLK), BLK)
    bias = [bias_ref[rows, t * BLK : t * BLK + BLK].astype(F32) for t in tiles]
    heads = [(which, head) for which in range(2) for head in range(2)]
    scores = [
        [dot(k[which][t], q[which][head], 1, 1) + bias[t] for t in range(len(tiles))] for which, head in heads
    ]
    probs = column_softmax(scores)
    outs = []
    for (which, head), parts in zip(heads, probs):
        out = None
        for t, part in enumerate(parts):
            value = dot(vt[which][t][head * HD : head * HD + HD], part, 1, 0)
            out = value if out is None else out + value
        outs.append(out)
    for (which, head), parts in zip(heads, probs):
        for t, part in zip(tiles, parts):
            p_ref[6 * micro + 2 * group + which, head, t * BLK : t * BLK + BLK] = part
    for which, pair in enumerate(pairs):
        o_ref[queries, pair] = jnp.concatenate(outs[2 * which : 2 * which + 2], 0).T.astype(BF16)


def backward_heads(micro, group, refs, mine, tiles):
    q_ref, k_ref, v_ref, go_ref, p_ref = refs
    solo, wide, extra = attention_rows(micro, mine)
    queries = solo if tiles == (0,) else wide
    keys = [(solo, extra, wide)[t] for t in tiles]
    pairs = [heads_of(group, which) for which in range(2)]
    k = [[k_ref[rows, pair] for rows in keys] for pair in pairs]
    v = [[v_ref[rows, pair] for rows in keys] for pair in pairs]
    kt = [[tile.T for tile in tiles_of] for tiles_of in k]
    q = [halves(q_ref[queries, pair]) for pair in pairs]
    go = [halves(go_ref[queries, pair]) for pair in pairs]
    heads = [(which, head) for which in range(2) for head in range(2)]
    count = range(len(tiles))
    probs = [
        [p_ref[6 * micro + 2 * group + which, head, t * BLK : t * BLK + BLK] for t in tiles] for which, head in heads
    ]
    full = [[tile.astype(F32) for tile in parts] for parts in probs]
    terms = [
        [full[i][t] * dot(v[which][t], go[which][head], 1, 1) for t in count] for i, (which, head) in enumerate(heads)
    ]
    deltas = []
    for parts in terms:
        delta = colsum(parts[0])
        for part in parts[1:]:
            delta = delta + colsum(part)
        deltas.append(delta)
    grads = [
        [(terms[i][t] - full[i][t] * deltas[i]).astype(BF16) for t in count] for i in range(4)
    ]
    outs = []
    for i, (which, head) in enumerate(heads):
        out = None
        for t in count:
            value = dot(kt[which][t][head * HD : head * HD + HD], grads[i][t], 1, 0)
            out = value if out is None else out + value
        outs.append(out)
    results = []
    for which, pair in enumerate(pairs):
        first = 2 * which
        for t in count:
            results.append((v_ref, keys[t], pair, both(probs[first][t], probs[first + 1][t], go[which])))
            results.append((k_ref, keys[t], pair, both(grads[first][t], grads[first + 1][t], q[which])))
        grad = jnp.concatenate(outs[first : first + 2], 0).T * 0.125
        results.append((q_ref, queries, pair, grad.astype(BF16)))
    for ref, rows, pair, value in results:
        ref[rows, pair] = value


def both(left, right, values):
    return dot(jnp.concatenate([left, right], 1), jnp.concatenate(values, 0), 1, 0).astype(BF16)


PLAN = {
    0: (2100, 2103, 2000, 2012, 2001, 2002,),
    1: (2003, 2004, 2008, 200, 212, 201, 300, 312, 202, 301, 400, 412, 203, 2101, 500, 512,),
    10: (302, 2005, 2009, 2006, 2010, 2007, 2011,),
    11: (401, 204,),
    20: (303, 2102, 501,),
    30: (402, 502,),
    31: (304, 208,),
    32: (403,),
    40: (503, 205,),
    41: (404,),
    44: (504, 308,),
    45: (209,),
    46: (305,),
    51: (408, 206,),
    60: (309, 508,),
    61: (405, 210,),
    63: (505, 409, 306, 207, 211,),
    64: (1004,),
    70: (509, 310, 1008,),
    71: (406, 1104,),
    72: (307, 1108,),
    73: (506,),
    74: (311, 1005,),
    80: (410, 1009, 1105, 1204, 510,),
    81: (407,),
    82: (1109,),
    83: (507, 411, 1208,),
    84: (1006,),
    90: (511, 1205, 1010,),
    91: (1304, 1106,),
    92: (1110,),
    93: (1308, 1209,),
    94: (1404, 1305, 1007,),
    100: (1011,),
    101: (1206, 1107,),
    102: (1210, 1111,),
    120: (1309, 1003,),
    121: (1408, 1306,),
    122: (1310, 1207, 1103, 1405,),
    130: (1000,),
    131: (1211,),
    132: (1409, 1307, 1100,),
    140: (1001,),
    141: (1406, 1203,),
    142: (1410, 1311, 1101,),
    110: (1200, 1002,),
    150: (2202, 2203, 1407, 1303,),
    151: (1102,),
    154: (1201,),
    155: (2300, 1300,),
    156: (1411, 2301, 1403, 1202, 2201, 1301, 2200, 1400, 2302, 2303, 1302, 1401, 2304, 1402,),
}
GATHER_ACROSS = (1, 4)
SCATTER_ACROSS = (3, 1, 2)
MESH = pl.DeviceIdType.MESH
HALF = D // 2


class Place:
    def __init__(self):
        self.c = lax.axis_index("ctx")
        f = lax.axis_index("fsdp")
        self.z, self.y, self.k = f // 4, (f // 2) % 2, f % 2
        self.sibling = self.at(self.c, self.z, self.y, 1 - self.k)
        self.beside = self.at(1 - self.c, self.z, self.y, self.k)
        self.across = self.at(self.c, self.z, 1 - self.y, self.k)

    def at(self, c, z, y, k):
        return (c, z * 4 + y * 2 + k)

    def level(self, step):
        return lax.rem(self.z + step, 4)

    def along(self, step):
        return self.at(self.c, self.level(step), self.y, self.k)

    def pick(self, side, first, second):
        return first + side * (second - first)

    def onward(self, side):
        c = self.c + (1 - side) * (1 - 2 * self.c)
        y = self.y + side * (1 - 2 * self.y)
        return self.at(c, self.z, y, self.k)


def half(index):
    return pl.ds(pl.multiple_of(index * HALF, 128), HALF)


def send(source, target, sends, recvs, device):
    return pltpu.make_async_remote_copy(
        src_ref=source, dst_ref=target, send_sem=sends, recv_sem=recvs, device_id=device, device_id_type=MESH
    )


def fixed(piece):
    return not isinstance(piece[1] if isinstance(piece, tuple) else piece, jax.Array)


def begin(copies):
    for copy in copies:
        copy.start()


def landed(copies):
    for copy in copies:
        copy.wait_recv()


def gone(copies):
    for copy in copies:
        copy.wait_send()


class Gather:
    def __init__(self, place, sources, w_ref, d_ref, vec_ref, sends, recvs, local):
        self.p, self.sources = place, sources
        self.w, self.d, self.v = w_ref, d_ref, vec_ref
        self.sends, self.recvs, self.local = sends, recvs, local

    def whole(self, piece):
        return self.v if piece is None else self.w.at[piece]

    def row(self, piece):
        return 12 if piece is None else piece

    def lead(self, piece):
        return 1 if fixed(piece) and piece in GATHER_ACROSS else self.p.k

    def own(self, piece):
        if piece is None:
            return self.sources[3]
        if piece < 3:
            return self.sources[0].at[:, piece * D : piece * D + D]
        if piece == 3:
            return self.sources[1]
        return self.sources[2].at[:, (piece - 4) * D : (piece - 3) * D]

    def own_half(self, piece):
        cols = half(self.p.c)
        if piece is None:
            return self.sources[3].at[:, cols]
        if piece == 3:
            return self.sources[1].at[:, cols]
        base, first = (self.sources[0], 0) if piece < 3 else (self.sources[2], 4)
        return base.at[:, pl.ds(pl.multiple_of((piece - first) * D + self.p.c * HALF, 128), HALF)]

    def keep(self, piece):
        p = self.p
        return pltpu.make_async_copy(
            self.own(piece), self.whole(piece).at[p.z, p.y, p.k], self.local.at[self.row(piece)]
        )

    def keep_down(self):
        p = self.p
        return pltpu.make_async_copy(self.sources[4], self.d.at[p.z, p.y, p.k], self.local.at[8])

    def z_copy(self, piece, step, level):
        p, row = self.p, self.row(piece)
        return send(
            self.own_half(piece),
            self.whole(piece).at[level, p.y, p.k, :, half(p.c)],
            self.sends.at[row, step - 1],
            self.recvs.at[row, step - 1],
            p.along(step),
        )

    def z_down(self, step, level, sem):
        p = self.p
        return send(
            self.sources[4].at[:, half(p.c)],
            self.d.at[level, p.y, p.k, :, half(p.c)],
            self.sends.at[13, sem],
            self.recvs.at[13, sem],
            p.along(step),
        )

    def own_across(self, piece):
        p, row = self.p, self.row(piece)
        return send(
            self.own_half(piece),
            self.whole(piece).at[p.z, p.y, p.k, :, half(p.c)],
            self.sends.at[row, 6],
            self.recvs.at[row, 6],
            p.across,
        )

    def start(self, *pieces):
        for piece in pieces:
            for step in (1, 2, 3):
                self.z_copy(piece, step, self.p.z).start()
            self.own_across(piece).start()
            self.keep(piece).start()

    def start_down(self, j):
        @pl.when(self.p.z == j)
        def _():
            for step in (1, 2, 3):
                self.z_down(step, self.p.z, step - 1).start()
            self.keep_down().start()

    def copies(self, piece):
        p, row = self.p, self.row(piece)
        whole = self.whole(piece)

        def to(part, column, device):
            return send(part, part, self.sends.at[row, column], self.recvs.at[row, column], device)

        def beside():
            return [
                to(whole.at[p.level(step), p.y, p.k, :, half(p.c)], 2 + step, p.beside) for step in (1, 2, 3)
            ]

        def across():
            return [
                to(whole.at[p.level(step), p.y, p.k, :, half(p.c)], 8 + step, p.across) for step in (1, 2, 3)
            ]

        def forward():
            lead = self.lead(piece)
            part = whole.at[:, p.pick(lead, 1 - p.y, p.y), p.k, :, half(p.pick(lead, p.c, 1 - p.c))]
            return [to(part, 7, p.onward(lead))]

        def sibling():
            return [to(whole.at[:, :, p.k], 8, p.sibling)]

        return beside, across, forward, sibling

    def copies_down(self, j):
        p, row = self.p, 8 + j

        def to(part, column, device):
            return send(part, part, self.sends.at[row, column], self.recvs.at[row, column], device)

        def beside():
            return [to(self.d.at[j, p.y, p.k, :, half(p.c)], 3, p.beside)]

        def across():
            return [to(self.d.at[j, p.y, p.k, :, half(p.c)], 6, p.across)]

        def forward():
            lead = self.lead(("d", j))
            part = self.d.at[j, p.pick(lead, 1 - p.y, p.y), p.k, :, half(p.pick(lead, p.c, 1 - p.c))]
            return [to(part, 7, p.onward(lead))]

        def sibling():
            return [to(self.d.at[j, :, p.k], 8, p.sibling)]

        return beside, across, forward, sibling

    def stage(self, number, piece):
        if isinstance(piece, tuple):
            return self.stage_down(number, piece[1])
        p, row, whole = self.p, self.row(piece), self.whole(piece)
        beside, across, forward, sibling = self.copies(piece)
        if number == 2:
            self.keep_wait(piece)
            for step in (1, 2, 3):
                self.z_wait(piece, step)
            begin(across() + beside())
        elif number == 3:
            part = whole.at[p.z, p.y, p.k, :, half(p.c)]
            own = send(part, part, self.sends.at[row, 6], self.recvs.at[row, 6], p.across)
            landed([own] + across() + beside())
            begin(forward())
        elif number == 4:
            landed(forward())
            begin(sibling())
        elif number == 5:
            landed(sibling())
        else:
            gone(beside() + across() + forward() + sibling())

    def keep_wait(self, piece):
        p = self.p
        part = self.whole(piece).at[p.z, p.y, p.k]
        pltpu.make_async_copy(part, part, self.local.at[self.row(piece)]).wait()

    def z_wait(self, piece, step):
        p, row = self.p, self.row(piece)
        part = self.whole(piece).at[p.level(4 - step), p.y, p.k, :, half(p.c)]
        send(part, part, self.sends.at[row, step - 1], self.recvs.at[row, step - 1], p.along(step)).wait_recv()

    def stage_down(self, number, j):
        p = self.p
        beside, across, forward, sibling = self.copies_down(j)
        away = p.z != j
        if number == 2:

            @pl.when(away)
            def _():
                step = lax.rem(p.z - j + 4, 4)
                part = self.d.at[j, p.y, p.k, :, half(p.c)]
                landed([send(part, part, self.sends.at[13, step - 1], self.recvs.at[13, step - 1], p.along(1))])
                begin(beside())

            @pl.when(p.z == j)
            def _():
                self.keep_down().wait()

            begin(across())
        elif number == 3:

            @pl.when(away)
            def _():
                landed(beside())

            landed(across())
            begin(forward())
        elif number == 4:
            landed(forward())
            begin(sibling())
        elif number == 5:
            landed(sibling())
        else:

            @pl.when(away)
            def _():
                gone(beside())

            gone(across() + forward() + sibling())

    def finish(self):
        for piece in (None, *range(8)):
            for step in (1, 2, 3):
                self.z_copy(piece, step, self.p.z).wait_send()
            self.own_across(piece).wait_send()
        for step in (1, 2, 3):
            self.z_down(step, self.p.z, step - 1).wait_send()


class Scatter:
    def __init__(self, place, w_ref, d_ref, rings, sends, recvs):
        self.p, self.w, self.d = place, w_ref, d_ref
        self.rings = rings
        self.sends, self.recvs = sends, recvs

    def held(self, block):
        return block + 4 if not isinstance(block, tuple) and block < 3 else block

    def lead(self, block):
        return 1 if fixed(block) and block in SCATTER_ACROSS else self.p.k

    def pick(self, block, first, second):
        return first + self.lead(block) * (second - first)

    def turn(self, block, number):
        return self.p.onward(self.lead(block) if number == 0 else 1 - self.lead(block))

    def part(self, block, y, col):
        if isinstance(block, tuple):
            return self.d.at[block[1], y, self.p.k, :, half(col)]
        return self.w.at[self.held(block), :, y, self.p.k, :, half(col)]

    def row(self, block):
        return 8 + block[1] if isinstance(block, tuple) else block

    def ring(self, block, which, slot):
        ring = self.rings[2 * which + (1 if isinstance(block, tuple) else 0)]
        return ring.at[slot % ring.shape[0]]

    def sem(self, block, column):
        row = self.row(block)
        return self.sends.at[row, column], self.recvs.at[row, column]

    def to_sibling(self, block, slot):
        p = self.p
        part = self.d.at[block[1], :, 1 - p.k] if isinstance(block, tuple) else self.w.at[self.held(block), :, :, 1 - p.k]
        return send(part, self.ring(block, 0, slot), *self.sem(block, 0), p.sibling)

    def first(self, block, slot, i):
        p = self.p
        part = self.part(block, self.pick(block, i, 1 - p.y), self.pick(block, 1 - p.c, i))
        ring = self.ring(block, 1, slot)
        ring = ring.at[i] if isinstance(block, tuple) else ring.at[:, i]
        return send(part, ring, *self.sem(block, 1 + i), self.turn(block, 0))

    def second(self, block, slot):
        p = self.p
        part = self.part(block, self.pick(block, 1 - p.y, p.y), self.pick(block, p.c, 1 - p.c))
        return send(part, self.ring(block, 2, slot), *self.sem(block, 3), self.turn(block, 1))

    def third(self, block, slot, step):
        p = self.p
        part = self.w.at[self.held(block), p.level(step), p.y, p.k, :, half(p.c)]
        return send(part, self.rings[6].at[slot % 4, step - 1], *self.sem(block, 3 + step), p.along(step))

    def third_down(self, j, step):
        p = self.p
        part = self.part(("d", j), p.y, p.c)
        return send(part, self.rings[7].at[step - 1], *self.sem(("d", j), 3 + step), p.at(p.c, j, p.y, p.k))

    def last(self, block):
        p = self.p
        land = self.rings[9] if isinstance(block, tuple) else self.rings[8].at[block]
        return send(self.total(block), land, *self.sem(block, 7), p.beside)

    def total(self, block):
        return self.rings[11] if isinstance(block, tuple) else self.rings[10].at[block]

    def store(self, block, target, sems):
        c = self.p.c
        land = self.rings[9] if isinstance(block, tuple) else self.rings[8].at[block]
        return [
            pltpu.make_async_copy(self.total(block), target.at[:, half(c)], sems.at[0]),
            pltpu.make_async_copy(land, target.at[:, half(1 - c)], sems.at[1]),
        ]

    def stage(self, number, block, slot):
        p = self.p
        down = isinstance(block, tuple)
        if number == 0:
            self.to_sibling(block, slot).start()
        elif number == 1:
            self.to_sibling(block, slot).wait_recv()
            mine = self.d.at[block[1], :, p.k] if down else self.w.at[self.held(block), :, :, p.k]
            mine[...] = mine[...] + self.ring(block, 0, slot)[...]
            for i in (0, 1):
                self.first(block, slot, i).start()
        elif number == 2:
            for i in (0, 1):
                self.first(block, slot, i).wait_recv()
                mine = self.part(block, self.pick(block, i, p.y), self.pick(block, p.c, i))
                ring = self.ring(block, 1, slot)
                mine[...] = mine[...] + (ring[i] if down else ring[:, i])
            self.second(block, slot).start()
        elif number == 3:
            self.second(block, slot).wait_recv()
            mine = self.part(block, p.y, p.c)
            mine[...] = mine[...] + self.ring(block, 2, slot)[...]
            if down:
                j = block[1]

                @pl.when(p.z != j)
                def _():
                    step = lax.rem(j - p.z + 4, 4)
                    self.third_down(j, step).start()
            else:
                for step in (1, 2, 3):
                    self.third(block, slot, step).start()
        elif number == 4:
            if down:
                j = block[1]

                @pl.when(p.z == j)
                def _():
                    total = self.part(block, p.y, p.c)[...].astype(F32)
                    for step in (1, 2, 3):
                        self.third_down(j, step).wait_recv()
                        total = total + self.rings[7][step - 1].astype(F32)
                    self.total(block)[...] = total.astype(BF16)
                    self.last(block).start()
            else:
                total = self.w[self.held(block), p.z, p.y, p.k, :, half(p.c)].astype(F32)
                for step in (1, 2, 3):
                    self.third(block, slot, step).wait_recv()
                    total = total + self.rings[6][slot % 4, step - 1].astype(F32)
                self.total(block)[...] = total.astype(BF16)
                self.last(block).start()
        elif number == 5:
            if down:

                @pl.when(p.z == block[1])
                def _():
                    self.last(block).wait_recv()
            else:
                self.last(block).wait_recv()

    def finish(self, block, slot):
        self.finish_block(block, slot)
        if isinstance(block, tuple):

            @pl.when(self.p.z == block[1])
            def _():
                self.last(block).wait_send()
        else:
            self.last(block).wait_send()

    def finish_block(self, block, slot):
        p = self.p
        self.to_sibling(block, slot).wait_send()
        for i in (0, 1):
            self.first(block, slot, i).wait_send()
        self.second(block, slot).wait_send()
        if isinstance(block, tuple):
            j = block[1]

            @pl.when(p.z != j)
            def _():
                self.third_down(j, lax.rem(j - p.z + 4, 4)).wait_send()
        else:
            for step in (1, 2, 3):
                self.third(block, slot, step).wait_send()


def layer_kernel(
    x_hbm, cot_hbm, seg_ref, qkv_hbm, out_hbm, up_hbm, rows_ref, bup_own_ref, down_hbm,
    act_hbm, gx_hbm, fin_hbm, find_hbm, vg_hbm,
    w_ref, d_ref, vecs_ref, vec_ref, x_ref, cot_ref, q_ref, k_ref, v_ref, o_ref, p_ref, bias_ref,
    acc_ref, n2_ref, a2_ref, rs2_ref, g2_ref, a1_ref, gu_ref, vg_ref, bup_ref,
    ring0, ring1, ring2, ring3, ring4, ring5, ring6, ring7, land_ref, landd_ref, own_ref, ownd_ref, vr_ref,
    qs_ref, vloc_ref, small_ref, slices_ref, parts_ref, ag_send, ag_recv, ag_local, rs_send, rs_recv, v_send, v_recv, x_send, x_recv, sem, out_sem,
):
    place = Place()
    mine = place.c
    a3_ref = x_ref.at[0:1024]
    gather = Gather(
        place, (qs_ref, out_hbm, up_hbm, vloc_ref, down_hbm), w_ref, d_ref, vecs_ref, ag_send, ag_recv, ag_local
    )
    scatter = Scatter(
        place, w_ref, d_ref, (ring0, ring1, ring2, ring3, ring4, ring5, ring6, ring7, land_ref, landd_ref, own_ref, ownd_ref), rs_send, rs_recv
    )
    barrier = pltpu.get_barrier_semaphore()
    for device in (place.sibling, place.beside, place.across, place.along(1), place.along(2), place.along(3)):
        pl.semaphore_signal(barrier, 1, device_id=device, device_id_type=MESH)
    load_x = pltpu.make_async_copy(x_hbm, x_ref.at[0:1024], sem.at[0])
    load_cot = pltpu.make_async_copy(cot_hbm, cot_ref, sem.at[1])
    loads = [
        pltpu.make_async_copy(
            qkv_hbm.at[:, D * part + 256 * group : D * part + 256 * group + 256],
            qs_ref.at[:, D * group + 256 * part : D * group + 256 * part + 256],
            sem.at[5 + 3 * group + part],
        )
        for group in range(3)
        for part in range(3)
    ]
    begin(loads)
    load_x.start()
    load_cot.start()
    def lane_match(rows, cols, shift, limit):
        row = lax.broadcasted_iota(jnp.int32, (rows, cols), 0)
        col = lax.broadcasted_iota(jnp.int32, (rows, cols), 1)
        return (row - col == shift) & (col < limit)

    owner = place.z * 4 + place.y * 2 + place.k
    inner = place.y * 2 + place.k
    spread = jnp.where(lane_match(48, D, -48 * owner, D), 1.0, 0.0).astype(BF16)
    vloc_ref[0:8, :] = dot(rows_ref[...], spread, 1, 0).astype(BF16)
    spread = jnp.where(lane_match(192, D, -192 * inner, D), 1.0, 0.0).astype(BF16)
    wide = dot(jnp.broadcast_to(bup_own_ref[...], (8, 192)), spread, 1, 0)
    chosen = lax.broadcasted_iota(jnp.int32, (8, D), 0) == place.z
    vloc_ref[8:16, :] = jnp.where(chosen, wide, 0.0).astype(BF16)
    pl.semaphore_wait(barrier, 6)
    for copy in loads:
        copy.wait()

    def give(part):
        start = pl.multiple_of((part // 2) * 512 + mine * BLK + (part % 2) * 128, 128)
        return send(
            x_hbm.at[pl.ds(start, 128)],
            x_ref.at[1024 + part * 128 : 1152 + part * 128],
            x_send.at[part],
            x_recv.at[part],
            place.beside,
        )

    def give_back(part):
        rows = slice(part * 128, part * 128 + 128)
        return send(
            a2_ref.at[rows], bias_ref.at[rows], x_send.at[4 + part], x_recv.at[4 + part], place.beside
        )

    rounds = (
        [(0, place.sibling)],
        [(1, place.beside)],
        [(2, place.across)],
        [(3, place.along(1)), (4, place.along(2)), (5, place.along(3))],
    )

    def exchange(index, device):
        if index < 3:
            return send(vg_ref, vr_ref.at[index], v_send.at[index], v_recv.at[index], device)
        source = slices_ref.at[place.level(index - 2)]
        return send(source, parts_ref.at[index - 3], v_send.at[index], v_recv.at[index], device)

    def slice_vectors(value):
        high = value.astype(BF16)
        left = value - high.astype(F32)
        middle = left.astype(BF16)
        low = (left - middle.astype(F32)).astype(BF16)
        exact = jnp.concatenate([high, middle, low], 0)
        row = lax.broadcasted_iota(jnp.int32, (D, 512), 0)
        col = lax.broadcasted_iota(jnp.int32, (D, 512), 1)
        lane = col & 127
        chosen = (row == 192 * (col >> 7) + 48 * inner + lane) & (lane < 48)
        short = dot(exact, jnp.where(chosen, 1.0, 0.0).astype(BF16), 1, 0)
        short = short[0:16] + short[16:32] + short[32:48]
        chosen = lane_match(D, 256, 192 * inner, 192)
        long = dot(exact, jnp.where(chosen, 1.0, 0.0).astype(BF16), 1, 0)
        long = long[0:16] + long[16:32] + long[32:48]
        slices_ref[...] = jnp.zeros_like(slices_ref)
        for z in range(4):
            slices_ref[z, 0:8, :] = short[0:8, 128 * z : 128 * z + 128]
            slices_ref[z, 8:9, :] = long[8 + z : 9 + z, 0:128]
            slices_ref[z, 9:10, :] = long[8 + z : 9 + z, 128:256]

    def vectors(number):
        if number > 0:
            for index, device in rounds[number - 1]:
                exchange(index, device).wait()
        if number in (1, 2, 3):
            value = vg_ref[...] + vr_ref[number - 1]
            if number < 3:
                vg_ref[...] = value
            else:
                slice_vectors(value)
        if number == 4:
            small_ref[...] = slices_ref[place.z] + parts_ref[0] + parts_ref[1] + parts_ref[2]
        else:
            for index, device in rounds[number]:
                exchange(index, device).start()

    def piece(number):
        return None if number == 12 else number if number < 8 else ("d", number - 8)

    places = (5, 6, 7, 4, 0, 1, 2, 3, 0, 1, 2, 3)

    def step(code):
        kind, rest = code // 100, code % 100
        if kind < 10:
            gather.stage(kind, piece(rest))
        elif kind < 20:
            scatter.stage(kind - 10, piece(rest), places[rest])
        elif kind == 20:
            if 8 <= rest < 12:
                gather.start_down(rest - 8)
            else:
                gather.start(piece(rest))
        elif kind == 21:
            give(rest).start()
        elif kind == 22:
            give_back(rest).start()
        else:
            vectors(rest)

    def at(slot):
        for code in PLAN.get(slot, ()):
            step(code)

    def at_loop(slot, index, count):
        for i in range(count):
            if PLAN.get(slot + i):

                @pl.when(index == i)
                def _():
                    at(slot + i)

    def weight(index):
        return w_ref[index].reshape(D, D)

    def weight_down(index):
        return d_ref[index].reshape(D, D)

    def vec(row):
        return vec_ref[row : row + 1, :]

    def add_vec(row, value):
        vg_ref[row : row + 1, :] += value

    at(0)
    vg_ref[...] = jnp.zeros_like(vg_ref)
    attention_masks(seg_ref, bias_ref, mine)
    at(1)
    total = vecs_ref[0, 0, 0].astype(F32)
    for shard in range(1, 16):
        total = total + vecs_ref[shard // 4, (shard // 2) % 2, shard % 2].astype(F32)
    vec_ref[...] = total
    load_x.wait()

    def first_norm(r):
        rows = pl.ds(r * BLK, BLK)
        normed, _ = norm(x_ref[rows, :].astype(F32))
        a1_ref[rows, :] = (normed * vec(0) + vec(1)).astype(BF16)

    loop(4, first_norm)
    refs = (q_ref, k_ref, v_ref, o_ref, p_ref, bias_ref)
    for g in range(3):
        at(10 + 10 * g)
        cols = slice(256 * g, 256 * g + 256)
        mixed = dot(a1_ref[0:1024, :], weight(g), 1, 0)
        q_ref[:, cols] = ((mixed[:, :256] + vec(2)[:, cols]).astype(BF16) * 0.125).astype(BF16)
        k_ref[0:1024, cols] = mixed[:, 256:512].astype(BF16)
        v_ref[0:1024, cols] = (mixed[:, 512:] + vec(3)[:, cols]).astype(BF16)

        def solo(m):
            at_loop(11 + 10 * g, m, 2)
            forward_heads(m, g, refs, mine, (0,))

        loop(2, solo)
    at(40)
    for part in range(4):
        give(part).wait_recv()
    loop(2, lambda r: first_norm(4 + r))
    for g in range(3):
        cols = slice(256 * g, 256 * g + 256)
        mixed = dot(a1_ref[1024:1536, :], weight(g)[:, 256:], 1, 0)
        k_ref[1024:1536, cols] = mixed[:, :256].astype(BF16)
        v_ref[1024:1536, cols] = (mixed[:, 256:] + vec(3)[:, cols]).astype(BF16)

    def wide(i):
        at_loop(41, i, 6)
        forward_heads(i // 3, i % 3, refs, mine, (1, 2))

    loop(6, wide)

    at(50)
    acc_ref[...] = dot(o_ref[...], weight(3), 1, 0)
    load_cot.wait()
    at(51)

    def second_norm(r):
        rows = pl.ds(r * BLK, BLK)
        resid = acc_ref[rows, :] + x_ref[rows, :].astype(F32) + vec(4)
        normed, inverse = norm(resid)
        acc_ref[rows, :] = resid + vec(7)
        n2_ref[rows, :] = normed.astype(BF16)
        a2_ref[rows, :] = (normed * vec(5) + vec(6)).astype(BF16)
        rs2_ref[:, lanes(r, BLK)] = jnp.broadcast_to(inverse, (BLK, 128)).T[0:8]
        add_vec(7, colsum(cot_ref[rows, :].astype(F32)))
        g2_ref[rows, :] = jnp.zeros((BLK, D), F32)

    loop(4, second_norm)
    for j in range(4):
        bup_ref[j, 0:1] = vec(8 + j)
        bup_ref[j, 1:2] = jnp.zeros((1, D), F32)

    def feed(j):
        up = 4 + j
        bias = bup_ref[j, 0:1]

        def at_chunk(slot):
            for i in range(4):
                if PLAN.get(slot + 10 * i):

                    @pl.when(j == i)
                    def _():
                        at(slot + 10 * i)

        def part(r):
            rows = slice(r * 512, r * 512 + 512)
            u = dot(a2_ref[rows, :], weight(up), 1, 0) + bias
            back = dot(cot_ref[rows, :], weight_down(j), 1, 1)
            square = u * u
            th = jnp.tanh(u * (0.7978845608028654 + 0.035677408136300125 * square))
            half_up = 0.5 + 0.5 * th
            a3_ref[rows, :] = (u * half_up).astype(BF16)
            slope = half_up + (half_up * (1.0 - th)) * (u * (0.7978845608028654 + 0.10703222440890037 * square))
            gu = (back * slope).astype(BF16)
            gu_ref[rows, :] = gu
            bup_ref[j, 1:2] += colsum(gu.astype(F32))

        at_chunk(60)
        part(0)
        at_chunk(61)
        part(1)
        at_chunk(62)
        acc_ref[...] += dot(a3_ref[...], weight_down(j), 1, 0)
        g2_ref[...] += dot(gu_ref[...], weight(up), 1, 1)
        at_chunk(63)
        gather.stage(6, up)
        w_ref[up] = dot(a2_ref[...], gu_ref[...], 0, 0).astype(BF16).reshape(4, 2, 2, 48, D)
        at_chunk(64)
        gather.stage(6, ("d", j))
        d_ref[j] = dot(a3_ref[...], cot_ref[...], 0, 0).astype(BF16).reshape(2, 2, 192, D)

    loop(4, feed)
    at(100)
    for j in range(4):
        vg_ref[8 + j : 9 + j, :] = bup_ref[j, 1:2]

    def second_back(r):
        rows = pl.ds(r * BLK, BLK)
        a3_ref[rows, :] = acc_ref[rows, :].astype(BF16)
        g2 = g2_ref[rows, :]
        normed = n2_ref[rows, :].astype(F32)
        add_vec(5, colsum(g2 * normed))
        add_vec(6, colsum(g2))
        inverse = jnp.broadcast_to(rs2_ref[0:1, lanes(r, BLK)], (128, BLK)).T[:, 0:1]
        t = g2 * vec(5)
        first = jnp.mean(t, -1, keepdims=True)
        second = jnp.mean(t * normed, -1, keepdims=True)
        grad = cot_ref[rows, :].astype(F32) + inverse * (t - first - normed * second)
        g2_ref[rows, :] = grad
        lowered = grad.astype(BF16)
        a2_ref[rows, :] = lowered
        add_vec(4, colsum(lowered.astype(F32)))

    loop(4, second_back)
    out_copies = [
        pltpu.make_async_copy(x_ref.at[micro * 512 : micro * 512 + 512], act_hbm.at[micro, 0], sem.at[3 + micro])
        for micro in range(2)
    ]
    begin(out_copies)
    at(101)
    gu_ref[...] = dot(a2_ref[...], weight(3), 1, 1).astype(BF16)
    at(102)
    gather.stage(6, 3)
    w_ref[3] = dot(o_ref[...], a2_ref[...], 0, 0).astype(BF16).reshape(4, 2, 2, 48, D)
    refs = (q_ref, k_ref, v_ref, gu_ref, p_ref)

    for g in range(3):
        cols = slice(256 * g, 256 * g + 256)

        def back(m):
            at_loop(120 + 10 * g, m, 2)
            backward_heads(m, g, refs, mine, (1, 2))
            backward_heads(m, g, refs, mine, (0,))

        loop(2, back)
        at(122 + 10 * g)
        scatter.finish_block(4 + g, g)
        mixed = jnp.concatenate([k_ref[:, cols], v_ref[:, cols]], 1)
        w_ref[4 + g, :, :, :, :, 0:256] = (
            dot(a1_ref[0:1024, :], q_ref[:, cols], 0, 0).astype(BF16).reshape(4, 2, 2, 48, 256)
        )
        w_ref[4 + g, :, :, :, :, 256:] = dot(a1_ref[...], mixed, 0, 0).astype(BF16).reshape(4, 2, 2, 48, 512)
    at(110)
    for g in range(3):
        cols = slice(256 * g, 256 * g + 256)
        mixed = jnp.concatenate([k_ref[1024:1536, cols], v_ref[1024:1536, cols]], 1)
        value = dot(mixed, weight(g)[:, 256:], 1, 1)
        acc_ref[0:512, :] = value if g == 0 else acc_ref[0:512, :] + value
    a2_ref[0:512, :] = acc_ref[0:512, :].astype(BF16)
    for copy in out_copies:
        copy.wait()
    load_x.start()

    for g in range(3):
        at(150 + g)
        cols = slice(256 * g, 256 * g + 256)
        mixed = jnp.concatenate([q_ref[:, cols], k_ref[0:1024, cols], v_ref[0:1024, cols]], 1)
        value = dot(mixed, weight(g), 1, 1)
        acc_ref[...] = value if g == 0 else acc_ref[...] + value
    at(153)
    add_vec(2, colsum(q_ref[...].astype(F32)))
    add_vec(3, colsum(v_ref[...].astype(F32)))
    at(154)

    def extra_back(r):
        rows = pl.ds(1024 + r * BLK, BLK)
        normed, _ = norm(x_ref[rows, :].astype(F32))
        g1 = a2_ref[pl.ds(r * BLK, BLK), :].astype(F32)
        add_vec(0, colsum(g1 * normed))
        add_vec(1, colsum(g1))

    loop(2, extra_back)

    def first_sums(r):
        rows = pl.ds(r * BLK, BLK)
        normed, inverse = norm(x_ref[rows, :].astype(F32))
        g1 = acc_ref[rows, :]
        add_vec(0, colsum(g1 * normed))
        add_vec(1, colsum(g1))

    load_x.wait()
    loop(4, first_sums)

    def first_back(micro, block):
        rows = pl.ds(pl.multiple_of(micro * 512 + block * BLK, BLK), BLK)
        normed, inverse = norm(x_ref[rows, :].astype(F32))
        t = acc_ref[rows, :] * vec(0)
        first = jnp.mean(t, -1, keepdims=True)
        second = jnp.mean(t * normed, -1, keepdims=True)
        gu_ref[rows, :] = (g2_ref[rows, :] + inverse * (t - first - normed * second)).astype(BF16)

    at(155)
    loop(2, lambda micro: first_back(micro, 1 - mine))
    at(156)
    for part in range(4):
        give_back(part).wait_recv()
    for micro in range(2):
        rows = pl.ds(pl.multiple_of(micro * 512 + mine * BLK, BLK), BLK)
        acc_ref[rows, :] += bias_ref[micro * BLK : micro * BLK + BLK, :].astype(F32)
    loop(2, lambda micro: first_back(micro, mine))
    gx_copies = [
        pltpu.make_async_copy(gu_ref.at[micro * 512 : micro * 512 + 512], gx_hbm.at[micro, 0], sem.at[3 + micro])
        for micro in range(2)
    ]
    begin(gx_copies)
    at(157)
    ends = [pltpu.make_async_copy(small_ref, vg_hbm, sem.at[2])]
    begin(ends)
    for block in (4, 5, 6, 8, 9, 10, 7, 3, 11, 0, 1, 2):
        scatter.stage(5, piece(block), places[block])
        if block < 8:
            copies = scatter.store(block, fin_hbm.at[block], out_sem.at[block])
            begin(copies)
            ends += copies
        elif block == 11:
            copies = scatter.store(("d", 0), find_hbm, out_sem.at[8])
            begin(copies)
            ends += copies
    for block in range(12):
        if 4 <= block < 7:
            scatter.last(block).wait_send()
        else:
            scatter.finish(piece(block), places[block])
    for part in (None, 0, 1, 2):
        gather.stage(6, part)
    gather.finish()
    for part in range(4):
        give(part).wait_send()
        give_back(part).wait_send()
    for copy in gx_copies:
        copy.wait()
    for copy in ends:
        copy.wait()


def hand_out(
    act_ref, gx_ref, fin_ref, find_ref, small_ref, act_out, gx_out, qkv_ref, out_ref, up_ref, down_ref, *rest
):
    vectors = rest
    act_out[...] = act_ref[...]
    gx_out[...] = gx_ref[...]
    for part in range(3):
        for g in range(3):
            start = D * part + 256 * g
            qkv_ref[:, start : start + 256] = fin_ref[g, :, 256 * part : 256 * part + 256].astype(F32)
    out_ref[...] = fin_ref[3].astype(F32)
    for j in range(4):
        up_ref[:, D * j : D * j + D] = fin_ref[4 + j].astype(F32)
    down_ref[...] = find_ref[...].astype(F32)
    for i in range(8):
        vectors[i][...] = small_ref[i : i + 1, 0:48]
    vectors[8][:, 0:128] = small_ref[8:9, :]
    vectors[8][:, 128:192] = small_ref[9:10, 0:64]


def fast_device(
    layer_input, segments, ln1_gain, ln1_bias, w_qkv, q_bias, v_bias, w_attn_out, b_attn_out,
    ln2_gain, ln2_bias, w_up, b_up, w_down, b_down, cotangent,
):
    rows = jnp.stack([ln1_gain, ln1_bias, q_bias, v_bias, b_attn_out, ln2_gain, ln2_bias, b_down])
    big = lambda *shape, dtype=BF16: jax.ShapeDtypeStruct(shape, dtype)
    hbm = pl.BlockSpec(memory_space=pltpu.HBM)
    vmem = pl.BlockSpec(memory_space=pltpu.VMEM)
    act, gx, fin, find, small = pl.pallas_call(
        layer_kernel,
        out_shape=(
            big(2, 1, 512, D), big(2, 1, 512, D), big(8, 48, D), big(192, D), big(16, 128, dtype=F32),
        ),
        in_specs=[hbm, hbm, vmem, hbm, hbm, hbm, vmem, vmem, hbm],
        out_specs=(hbm,) * 5,
        scratch_shapes=[
            pltpu.VMEM((8, 4, 2, 2, 48, D), BF16),
            pltpu.VMEM((4, 2, 2, 192, D), BF16),
            pltpu.VMEM((4, 2, 2, 16, D), BF16),
            pltpu.VMEM((16, D), F32),
            pltpu.VMEM((1536, D), BF16),
            pltpu.VMEM((1024, D), BF16),
            pltpu.VMEM((1024, D), BF16),
            pltpu.VMEM((1536, D), BF16),
            pltpu.VMEM((1536, D), BF16),
            pltpu.VMEM((1024, D), BF16),
            pltpu.VMEM((12, 2, 3 * BLK, BLK), BF16),
            pltpu.VMEM((2 * BLK, 3 * BLK), BF16),
            pltpu.VMEM((1024, D), F32),
            pltpu.VMEM((1024, D), BF16),
            pltpu.VMEM((1024, D), BF16),
            pltpu.VMEM((8, 1024), F32),
            pltpu.VMEM((1024, D), F32),
            pltpu.VMEM((1536, D), BF16),
            pltpu.VMEM((1024, D), BF16),
            pltpu.VMEM((16, D), F32),
            pltpu.VMEM((4, 8, D), F32),
            pltpu.VMEM((3, 4, 2, 48, D), BF16),
            pltpu.VMEM((2, 2, 192, D), BF16),
            pltpu.VMEM((4, 4, 2, 48, HALF), BF16),
            pltpu.VMEM((4, 2, 192, HALF), BF16),
            pltpu.VMEM((4, 4, 48, HALF), BF16),
            pltpu.VMEM((4, 192, HALF), BF16),
            pltpu.VMEM((4, 3, 48, HALF), BF16),
            pltpu.VMEM((3, 192, HALF), BF16),
            pltpu.VMEM((8, 48, HALF), BF16),
            pltpu.VMEM((192, HALF), BF16),
            pltpu.VMEM((8, 48, HALF), BF16),
            pltpu.VMEM((192, HALF), BF16),
            pltpu.VMEM((3, 16, D), F32),
            pltpu.VMEM((48, 3 * D), BF16),
            pltpu.VMEM((16, D), BF16),
            pltpu.VMEM((16, 128), F32),
            pltpu.VMEM((4, 16, 128), F32),
            pltpu.VMEM((3, 16, 128), F32),
            pltpu.SemaphoreType.DMA((14, 12)),
            pltpu.SemaphoreType.DMA((14, 12)),
            pltpu.SemaphoreType.DMA((13,)),
            pltpu.SemaphoreType.DMA((12, 8)),
            pltpu.SemaphoreType.DMA((12, 8)),
            pltpu.SemaphoreType.DMA((6,)),
            pltpu.SemaphoreType.DMA((6,)),
            pltpu.SemaphoreType.DMA((8,)),
            pltpu.SemaphoreType.DMA((8,)),
            pltpu.SemaphoreType.DMA((14,)),
            pltpu.SemaphoreType.DMA((9, 2)),
        ],
        compiler_params=pltpu.CompilerParams(
            vmem_limit_bytes=66_500_000, collective_id=0, has_side_effects=True
        ),
        name="layer",
    )(
        layer_input.reshape(1024, D), cotangent.reshape(1024, D), segments,
        w_qkv, w_attn_out, w_up, rows, b_up[None], w_down,
    )
    blocks = pl.BlockSpec()
    f32 = lambda *shape: jax.ShapeDtypeStruct(shape, F32)
    act, gx, g_qkv, g_out, g_up, g_down, *vectors = pl.pallas_call(
        hand_out,
        out_shape=(
            big(2, 1, 512, D), big(2, 1, 512, D), f32(48, 3 * D), f32(48, D), f32(48, 4 * D), f32(192, D),
        ) + (f32(1, 48),) * 8 + (f32(1, 192),),
        in_specs=[blocks] * 5,
        out_specs=(blocks,) * 15,
        name="hand_out",
    )(act, gx, fin, find, small)
    part = [v[0] for v in vectors]
    return (
        act, gx, part[0], part[1], g_qkv, part[2], part[3], g_out, part[4], part[5], part[6], g_up, part[8], g_down, part[7],
    )


def solution(mesh):
    in_specs = (
        P(None, "fsdp", "ctx", None),
        P(None, "fsdp", None),
        P("fsdp"),
        P("fsdp"),
        P("fsdp", None),
        P("fsdp"),
        P("fsdp"),
        P("fsdp", None),
        P("fsdp"),
        P("fsdp"),
        P("fsdp"),
        P("fsdp", None),
        P("fsdp"),
        P("fsdp", None),
        P("fsdp"),
        P(None, "fsdp", "ctx", None),
    )
    out_specs = (
        P(None, "fsdp", "ctx", None),
        P(None, "fsdp", "ctx", None),
        P("fsdp"),
        P("fsdp"),
        P("fsdp", None),
        P("fsdp"),
        P("fsdp"),
        P("fsdp", None),
        P("fsdp"),
        P("fsdp"),
        P("fsdp"),
        P("fsdp", None),
        P("fsdp"),
        P("fsdp", None),
        P("fsdp"),
    )
    fast = mesh.shape["ctx"] == 2 and mesh.shape["fsdp"] == 16
    return jax.shard_map(
        fast_device if fast else on_device, mesh=mesh, in_specs=in_specs, out_specs=out_specs, check_vma=False
    )
```

```python
import jax
import jax.numpy as jnp
from jax import lax
from jax.experimental import pallas as pl
from jax.experimental.pallas import tpu as pltpu
from jax.sharding import PartitionSpec as P

H = 12


def stored_positions(length, groups):
    block_size = length // (2 * groups)
    stored = jnp.arange(length, dtype=jnp.int32)
    holder = stored // (2 * block_size)
    within = stored % (2 * block_size)
    second = within // block_size
    offset = within % block_size
    block_index = jnp.where(second == 0, holder, 2 * groups - 1 - holder)
    return block_index * block_size + offset


def normalize_parts(values):
    center = jnp.mean(values, -1, keepdims=True)
    centered = values - center
    inverse = lax.rsqrt(jnp.mean(centered * centered, -1, keepdims=True) + 1e-05)
    return (centered * inverse, inverse)


def normalize_back(grad_normed, normed, inverse):
    first = jnp.mean(grad_normed, -1, keepdims=True)
    second = jnp.mean(grad_normed * normed, -1, keepdims=True)
    return inverse * (grad_normed - first - normed * second)


def tile_allowed(query_pos, query_seg, key_pos, key_seg):
    return (key_pos[None, :] <= query_pos[:, None]) & (key_seg[None, :] == query_seg[:, None])


def tile_scores(query, keys_tile, allowed):
    scores = (
        jnp.einsum("qhd,khd->hqk", query, keys_tile, preferred_element_type=jnp.float32) * 0.125
    )
    return jnp.where(allowed[None], scores, -1e30)


def online_softmax(query, query_pos, query_seg, tiles):
    heads = query.shape[1]
    count_rows = query.shape[0]

    def advance(carry, tile):
        keys_tile, values_tile, key_pos, key_seg = tile
        allowed = tile_allowed(query_pos, query_seg, key_pos, key_seg)

        def compute(state):
            peak, total, accum = state
            scores = tile_scores(query, keys_tile, allowed)
            new_peak = jnp.maximum(peak, jnp.max(scores, -1))
            terms = jnp.where(allowed[None], jnp.exp(scores - new_peak[..., None]), 0.0)
            factor = jnp.exp(peak - new_peak)
            upper = terms.astype(jnp.bfloat16)
            lower = (terms - upper.astype(jnp.float32)).astype(jnp.bfloat16)
            added = jnp.einsum(
                "hqk,khd->qhd", upper, values_tile, preferred_element_type=jnp.float32
            )
            added = added + jnp.einsum(
                "hqk,khd->qhd", lower, values_tile, preferred_element_type=jnp.float32
            )
            accum = accum * jnp.transpose(factor)[..., None] + added
            return (new_peak, total * factor + jnp.sum(terms, -1), accum)

        return (compute(carry), None)

    start_state = (
        jnp.full((heads, count_rows), -1e30, jnp.float32),
        jnp.zeros((heads, count_rows), jnp.float32),
        jnp.zeros(query.shape, jnp.float32),
    )
    (peak, total, accum), unused = lax.scan(advance, start_state, tiles)
    exact = accum / jnp.transpose(total)[..., None]
    return (peak + jnp.log(total), exact)


def attention_out(query, log_total, query_pos, query_seg, tiles):

    def advance(carry, tile):
        keys_tile, values_tile, key_pos, key_seg = tile
        allowed = tile_allowed(query_pos, query_seg, key_pos, key_seg)

        def compute(summed):
            scores = tile_scores(query, keys_tile, allowed)
            probs = jnp.where(allowed[None], jnp.exp(scores - log_total[..., None]), 0.0)
            lowered = probs.astype(jnp.bfloat16)
            return summed + jnp.einsum(
                "hqk,khd->qhd", lowered, values_tile, preferred_element_type=jnp.float32
            )

        return (compute(carry), None)

    summed, unused = lax.scan(advance, jnp.zeros(query.shape, jnp.float32), tiles)
    return summed


def attention_back(query, log_total, grad_attended, delta, query_pos, query_seg, tiles):

    def advance(grad_query, tile):
        keys_tile, values_tile, key_pos, key_seg = tile
        allowed = tile_allowed(query_pos, query_seg, key_pos, key_seg)

        def compute(carry_query):
            scores = tile_scores(query, keys_tile, allowed)
            probs = jnp.where(allowed[None], jnp.exp(scores - log_total[..., None]), 0.0)
            lowered = probs.astype(jnp.bfloat16)
            grad_values = jnp.einsum(
                "hqk,qhd->khd", lowered, grad_attended, preferred_element_type=jnp.float32
            )
            grad_probs = jnp.einsum(
                "qhd,khd->hqk", grad_attended, values_tile, preferred_element_type=jnp.float32
            )
            grad_scores = (probs * (grad_probs - delta[..., None])).astype(jnp.bfloat16)
            new_query = carry_query + 0.125 * jnp.einsum(
                "hqk,khd->qhd", grad_scores, keys_tile, preferred_element_type=jnp.float32
            )
            grad_keys = 0.125 * jnp.einsum(
                "hqk,qhd->khd", grad_scores, query, preferred_element_type=jnp.float32
            )
            return (new_query, grad_keys, grad_values)

        new_query, grad_keys, grad_values = compute(grad_query)
        return (new_query, (grad_keys, grad_values))

    grad_query, (grad_keys, grad_values) = lax.scan(
        advance, jnp.zeros(query.shape, jnp.float32), tiles
    )
    return (grad_query, grad_keys, grad_values)


def column_sums(values):
    return jnp.sum(values.astype(jnp.float32), 0)


def layer_pass(inputs, cots, seg_row, weights, positions, start):
    (
        gain_one,
        shift_one,
        proj_mixed,
        bias_query,
        bias_value,
        proj_out,
        bias_out,
        gain_two,
        shift_two,
        proj_up,
        bias_up,
        proj_down,
        bias_down,
    ) = weights
    count_rows = inputs.shape[0]
    width = inputs.shape[1]
    heads = H
    head_size = width // heads
    length = seg_row.shape[0]
    query_pos = lax.dynamic_slice_in_dim(positions, start, count_rows)
    query_seg = lax.dynamic_slice_in_dim(seg_row, start, count_rows)
    values_in = inputs.astype(jnp.float32)
    normed_one, inverse_one = normalize_parts(values_in)
    lowered_one = (
        normed_one * gain_one.astype(jnp.float32) + shift_one.astype(jnp.float32)
    ).astype(jnp.bfloat16)
    mixed_bias = jnp.concatenate(
        [
            bias_query.astype(jnp.float32),
            jnp.zeros((width,), jnp.float32),
            bias_value.astype(jnp.float32),
        ]
    )
    mixed = (
        jnp.dot(lowered_one, proj_mixed, preferred_element_type=jnp.float32) + mixed_bias
    ).astype(jnp.bfloat16)
    query = mixed[:, :width].reshape(count_rows, heads, head_size)
    keys_values = lax.all_gather(mixed[:, width:], "ctx", axis=0, tiled=True)
    block = min(512, length)
    count = length // block
    tiles = (
        keys_values[:, :width].reshape(count, block, heads, head_size),
        keys_values[:, width:].reshape(count, block, heads, head_size),
        positions.reshape(count, block),
        seg_row.reshape(count, block),
    )
    log_total, exact = online_softmax(query, query_pos, query_seg, tiles)
    summed = attention_out(query, log_total, query_pos, query_seg, tiles)
    attended = summed.reshape(count_rows, width).astype(jnp.bfloat16)
    branch = jnp.dot(attended, proj_out, preferred_element_type=jnp.float32) + bias_out.astype(
        jnp.float32
    )
    resid = values_in + branch
    normed_two, inverse_two = normalize_parts(resid)
    lowered_two = (
        normed_two * gain_two.astype(jnp.float32) + shift_two.astype(jnp.float32)
    ).astype(jnp.bfloat16)
    hidden = jnp.dot(lowered_two, proj_up, preferred_element_type=jnp.float32) + bias_up.astype(
        jnp.float32
    )

    def smooth(pre_active):
        return jax.nn.gelu(pre_active, approximate=True)

    active_full, gelu_back = jax.vjp(smooth, hidden)
    active = active_full.astype(jnp.bfloat16)
    down = jnp.dot(active, proj_down, preferred_element_type=jnp.float32) + bias_down.astype(
        jnp.float32
    )
    output = (resid + down).astype(jnp.bfloat16)
    grad_out = cots.astype(jnp.float32)
    grad_bias_down = column_sums(cots)
    grad_proj_down = jnp.einsum("tf,td->fd", active, cots, preferred_element_type=jnp.float32)
    grad_active = jnp.einsum("td,fd->tf", cots, proj_down, preferred_element_type=jnp.float32)
    grad_hidden = gelu_back(grad_active)[0].astype(jnp.bfloat16)
    grad_bias_up = column_sums(grad_hidden)
    grad_proj_up = jnp.einsum(
        "td,tf->df", lowered_two, grad_hidden, preferred_element_type=jnp.float32
    )
    grad_lowered_two = jnp.einsum(
        "tf,df->td", grad_hidden, proj_up, preferred_element_type=jnp.float32
    )
    grad_gain_two = jnp.sum(grad_lowered_two * normed_two, 0)
    grad_shift_two = jnp.sum(grad_lowered_two, 0)
    grad_resid = grad_out + normalize_back(
        grad_lowered_two * gain_two.astype(jnp.float32), normed_two, inverse_two
    )
    grad_branch = grad_resid.astype(jnp.bfloat16)
    grad_bias_out = column_sums(grad_branch)
    grad_proj_out = jnp.einsum(
        "td,te->de", attended, grad_branch, preferred_element_type=jnp.float32
    )
    grad_attended = jnp.einsum(
        "te,de->td", grad_branch, proj_out, preferred_element_type=jnp.float32
    ).astype(jnp.bfloat16)
    grad_attended = grad_attended.reshape(count_rows, heads, head_size)
    delta = jnp.einsum("qhd,qhd->hq", grad_attended.astype(jnp.float32), exact)
    grad_query, grad_keys, grad_values = attention_back(
        query, log_total, grad_attended, delta, query_pos, query_seg, tiles
    )
    grad_pairs = jnp.concatenate(
        [grad_keys.reshape(length, width), grad_values.reshape(length, width)], 1
    )
    grad_pairs_local = lax.psum_scatter(grad_pairs, "ctx", scatter_dimension=0, tiled=True)
    grad_mixed = jnp.concatenate(
        [grad_query.reshape(count_rows, width), grad_pairs_local], 1
    ).astype(jnp.bfloat16)
    grad_bias_query = column_sums(grad_mixed[:, :width])
    grad_bias_value = column_sums(grad_mixed[:, 2 * width :])
    grad_proj_mixed = jnp.einsum(
        "td,te->de", lowered_one, grad_mixed, preferred_element_type=jnp.float32
    )
    grad_lowered_one = jnp.einsum(
        "te,de->td", grad_mixed, proj_mixed, preferred_element_type=jnp.float32
    )
    grad_gain_one = jnp.sum(grad_lowered_one * normed_one, 0)
    grad_shift_one = jnp.sum(grad_lowered_one, 0)
    grad_input = grad_resid + normalize_back(
        grad_lowered_one * gain_one.astype(jnp.float32), normed_one, inverse_one
    )
    grads = (
        grad_gain_one,
        grad_shift_one,
        grad_proj_mixed,
        grad_bias_query,
        grad_bias_value,
        grad_proj_out,
        grad_bias_out,
        grad_gain_two,
        grad_shift_two,
        grad_proj_up,
        grad_bias_up,
        grad_proj_down,
        grad_bias_down,
    )
    return (output, grad_input.astype(jnp.bfloat16), grads)


def fetch(shards):
    return (
        lax.all_gather(shards[0], "fsdp", axis=0, tiled=True),
        lax.all_gather(shards[1], "fsdp", axis=0, tiled=True),
        lax.all_gather(shards[2], "fsdp", axis=0, tiled=True),
        lax.all_gather(shards[3], "fsdp", axis=0, tiled=True),
        lax.all_gather(shards[4], "fsdp", axis=0, tiled=True),
        lax.all_gather(shards[5], "fsdp", axis=0, tiled=True),
        lax.all_gather(shards[6], "fsdp", axis=0, tiled=True),
        lax.all_gather(shards[7], "fsdp", axis=0, tiled=True),
        lax.all_gather(shards[8], "fsdp", axis=0, tiled=True),
        lax.all_gather(shards[9], "fsdp", axis=0, tiled=True),
        lax.all_gather(shards[10], "fsdp", axis=0, tiled=True),
        lax.all_gather(shards[11], "fsdp", axis=0, tiled=True),
        lax.all_gather(shards[12], "fsdp", axis=0, tiled=True),
    )


def share(grads):
    return (
        lax.psum_scatter(grads[0], "fsdp", scatter_dimension=0, tiled=True),
        lax.psum_scatter(grads[1], "fsdp", scatter_dimension=0, tiled=True),
        lax.psum_scatter(grads[2], "fsdp", scatter_dimension=0, tiled=True),
        lax.psum_scatter(grads[3], "fsdp", scatter_dimension=0, tiled=True),
        lax.psum_scatter(grads[4], "fsdp", scatter_dimension=0, tiled=True),
        lax.psum_scatter(grads[5], "fsdp", scatter_dimension=0, tiled=True),
        lax.psum_scatter(grads[6], "fsdp", scatter_dimension=0, tiled=True),
        lax.psum_scatter(grads[7], "fsdp", scatter_dimension=0, tiled=True),
        lax.psum_scatter(grads[8], "fsdp", scatter_dimension=0, tiled=True),
        lax.psum_scatter(grads[9], "fsdp", scatter_dimension=0, tiled=True),
        lax.psum_scatter(grads[10], "fsdp", scatter_dimension=0, tiled=True),
        lax.psum_scatter(grads[11], "fsdp", scatter_dimension=0, tiled=True),
        lax.psum_scatter(grads[12], "fsdp", scatter_dimension=0, tiled=True),
    )


def on_device(
    layer_input,
    segments,
    ln1_gain,
    ln1_bias,
    w_qkv,
    q_bias,
    v_bias,
    w_attn_out,
    b_attn_out,
    ln2_gain,
    ln2_bias,
    w_up,
    b_up,
    w_down,
    b_down,
    cotangent,
):
    shards = (
        ln1_gain,
        ln1_bias,
        w_qkv,
        q_bias,
        v_bias,
        w_attn_out,
        b_attn_out,
        ln2_gain,
        ln2_bias,
        w_up,
        b_up,
        w_down,
        b_down,
    )
    micro = layer_input.shape[0]
    count_rows = layer_input.shape[2]
    length = segments.shape[2]
    positions = stored_positions(length, lax.axis_size("ctx"))
    start = lax.axis_index("ctx") * count_rows
    outputs = []
    input_grads = []
    shared = None
    for number in range(micro):
        weights = fetch(shards)
        output, grad_input, grads = layer_pass(
            layer_input[number, 0],
            cotangent[number, 0],
            segments[number, 0],
            weights,
            positions,
            start,
        )
        summed = share(grads)
        shared = summed if shared is None else jax.tree.map(jnp.add, shared, summed)
        outputs.append(output)
        input_grads.append(grad_input)
    final = lax.psum(
        (
            shared[0],
            shared[1],
            shared[2],
            shared[3],
            shared[4],
            shared[5],
            shared[6],
            shared[7],
            shared[8],
            shared[9],
            shared[10],
            shared[11],
            shared[12],
        ),
        "ctx",
    )
    activations = jnp.stack(outputs)[:, None]
    input_grad = jnp.stack(input_grads)[:, None]
    return (
        activations,
        input_grad,
        final[0],
        final[1],
        final[2],
        final[3],
        final[4],
        final[5],
        final[6],
        final[7],
        final[8],
        final[9],
        final[10],
        final[11],
        final[12],
    )


D = 768
HD = 64
BLK = 256
NEG = -1e30
F32 = jnp.float32
BF16 = jnp.bfloat16


def dot(lhs, rhs, lhs_dim, rhs_dim):
    return lax.dot_general(
        lhs, rhs, (((lhs_dim,), (rhs_dim,)), ((), ())), preferred_element_type=F32
    )


def norm(v):
    center = v - jnp.mean(v, -1, keepdims=True)
    inverse = lax.rsqrt(jnp.mean(center * center, -1, keepdims=True) + 1e-05)
    return center * inverse, inverse


def colsum(v):
    return jnp.sum(v, 0, keepdims=True)


def loop(count, body):
    def step(index, carry):
        body(index)
        return carry

    lax.fori_loop(0, count, step, 0)


def lanes(index, size):
    return pl.ds(pl.multiple_of(index * size, size), size)


def attention_masks(seg_ref, bias_ref, mine):
    key = lax.broadcasted_iota(jnp.int32, (BLK, BLK), 0)
    query = lax.broadcasted_iota(jnp.int32, (BLK, BLK), 1)
    causal = key <= query
    for micro in range(2):

        def row(start):
            piece = seg_ref[micro, :, pl.ds(pl.multiple_of(start, BLK), BLK)]
            return jnp.broadcast_to(piece.astype(F32), (BLK, BLK))

        solo = row(mine * 2 * BLK + mine * BLK)
        wide = row(mine * 2 * BLK + (1 - mine) * BLK)
        extra = row((1 - mine) * 3 * BLK)
        rows = slice(micro * BLK, micro * BLK + BLK)
        tiles = ((solo.T == solo) & causal, extra.T == wide, (wide.T == wide) & causal)
        for t, allowed in enumerate(tiles):
            bias_ref[rows, t * BLK : t * BLK + BLK] = jnp.where(allowed, 0.0, NEG).astype(BF16)


def attention_rows(micro, mine):
    solo = pl.ds(pl.multiple_of(micro * 2 * BLK + mine * BLK, BLK), BLK)
    wide = pl.ds(pl.multiple_of(micro * 2 * BLK + (1 - mine) * BLK, BLK), BLK)
    extra = pl.ds(pl.multiple_of(1024 + micro * BLK, BLK), BLK)
    return solo, wide, extra


def halves(value):
    left = lax.broadcasted_iota(jnp.int32, value.shape, 1) < HD
    zero = jnp.zeros_like(value)
    return jnp.where(left, value, zero), jnp.where(left, zero, value)


def heads_of(group, which):
    return lanes(2 * group + which, 128)


def column_softmax(rows):
    peaks = []
    for tiles in rows:
        peak = tiles[0].max(0, keepdims=True)
        for tile in tiles[1:]:
            peak = jnp.maximum(peak, tile.max(0, keepdims=True))
        peaks.append(peak)
    terms = [[jnp.exp(tile - peak) for tile in tiles] for tiles, peak in zip(rows, peaks)]
    scales = []
    for tiles in terms:
        total = colsum(tiles[0])
        for tile in tiles[1:]:
            total = total + colsum(tile)
        scales.append(1.0 / total)
    return [[(tile * scale).astype(BF16) for tile in tiles] for tiles, scale in zip(terms, scales)]


def forward_heads(micro, group, refs, mine, tiles):
    q_ref, k_ref, v_ref, o_ref, p_ref, bias_ref = refs
    solo, wide, extra = attention_rows(micro, mine)
    queries = solo if tiles == (0,) else wide
    keys = [(solo, extra, wide)[t] for t in tiles]
    pairs = [heads_of(group, which) for which in range(2)]
    k = [[k_ref[rows, pair] for rows in keys] for pair in pairs]
    vt = [[v_ref[rows, pair].T for rows in keys] for pair in pairs]
    q = [halves(q_ref[queries, pair]) for pair in pairs]
    rows = pl.ds(pl.multiple_of(micro * BLK, BLK), BLK)
    bias = [bias_ref[rows, t * BLK : t * BLK + BLK].astype(F32) for t in tiles]
    heads = [(which, head) for which in range(2) for head in range(2)]
    scores = [
        [dot(k[which][t], q[which][head], 1, 1) + bias[t] for t in range(len(tiles))] for which, head in heads
    ]
    probs = column_softmax(scores)
    outs = []
    for (which, head), parts in zip(heads, probs):
        out = None
        for t, part in enumerate(parts):
            value = dot(vt[which][t][head * HD : head * HD + HD], part, 1, 0)
            out = value if out is None else out + value
        outs.append(out)
    for (which, head), parts in zip(heads, probs):
        for t, part in zip(tiles, parts):
            p_ref[6 * micro + 2 * group + which, head, t * BLK : t * BLK + BLK] = part
    for which, pair in enumerate(pairs):
        o_ref[queries, pair] = jnp.concatenate(outs[2 * which : 2 * which + 2], 0).T.astype(BF16)


def backward_heads(micro, group, refs, mine, tiles):
    q_ref, k_ref, v_ref, go_ref, p_ref = refs
    solo, wide, extra = attention_rows(micro, mine)
    queries = solo if tiles == (0,) else wide
    keys = [(solo, extra, wide)[t] for t in tiles]
    pairs = [heads_of(group, which) for which in range(2)]
    k = [[k_ref[rows, pair] for rows in keys] for pair in pairs]
    v = [[v_ref[rows, pair] for rows in keys] for pair in pairs]
    kt = [[tile.T for tile in tiles_of] for tiles_of in k]
    q = [halves(q_ref[queries, pair]) for pair in pairs]
    go = [halves(go_ref[queries, pair]) for pair in pairs]
    heads = [(which, head) for which in range(2) for head in range(2)]
    count = range(len(tiles))
    probs = [
        [p_ref[6 * micro + 2 * group + which, head, t * BLK : t * BLK + BLK] for t in tiles] for which, head in heads
    ]
    full = [[tile.astype(F32) for tile in parts] for parts in probs]
    terms = [
        [full[i][t] * dot(v[which][t], go[which][head], 1, 1) for t in count] for i, (which, head) in enumerate(heads)
    ]
    deltas = []
    for parts in terms:
        delta = colsum(parts[0])
        for part in parts[1:]:
            delta = delta + colsum(part)
        deltas.append(delta)
    grads = [
        [(terms[i][t] - full[i][t] * deltas[i]).astype(BF16) for t in count] for i in range(4)
    ]
    outs = []
    for i, (which, head) in enumerate(heads):
        out = None
        for t in count:
            value = dot(kt[which][t][head * HD : head * HD + HD], grads[i][t], 1, 0)
            out = value if out is None else out + value
        outs.append(out)
    results = []
    for which, pair in enumerate(pairs):
        first = 2 * which
        for t in count:
            results.append((v_ref, keys[t], pair, both(probs[first][t], probs[first + 1][t], go[which])))
            results.append((k_ref, keys[t], pair, both(grads[first][t], grads[first + 1][t], q[which])))
        grad = jnp.concatenate(outs[first : first + 2], 0).T * 0.125
        results.append((q_ref, queries, pair, grad.astype(BF16)))
    for ref, rows, pair, value in results:
        ref[rows, pair] = value


def both(left, right, values):
    return dot(jnp.concatenate([left, right], 1), jnp.concatenate(values, 0), 1, 0).astype(BF16)


PLAN = {
    0: (2100, 2103, 2000, 2012, 2001, 2002,),
    1: (2003, 2004, 2008, 200, 212, 201, 300, 312, 202, 301, 400, 412, 203, 2101, 500, 512,),
    10: (302, 2005, 2009, 2006, 2010, 2007, 2011,),
    11: (401, 204,),
    20: (303, 2102, 501,),
    30: (402, 502,),
    31: (304, 208,),
    32: (403,),
    40: (503, 205,),
    41: (404,),
    44: (504, 308,),
    45: (209,),
    46: (305,),
    51: (408, 206,),
    60: (309, 508,),
    61: (405, 210,),
    63: (505, 409, 306, 207, 211,),
    64: (1004,),
    70: (509, 310, 1008,),
    71: (406, 1104,),
    72: (307, 1108,),
    73: (506,),
    74: (311, 1005,),
    80: (410, 1009, 1105, 1204, 510,),
    81: (407,),
    82: (1109,),
    83: (507, 411, 1208,),
    84: (1006,),
    90: (511, 1205, 1010,),
    91: (1304, 1106,),
    92: (1110,),
    93: (1308, 1209,),
    94: (1404, 1305, 1007,),
    100: (1011,),
    101: (1206, 1107,),
    102: (1210, 1111,),
    120: (1309, 1003,),
    121: (1408, 1306,),
    122: (1310, 1207, 1103, 1405,),
    130: (1000,),
    131: (1211,),
    132: (1409, 1307, 1100,),
    140: (1001,),
    141: (1406, 1203,),
    142: (1410, 1311, 1101,),
    110: (1200, 1002,),
    150: (2202, 2203, 1407, 1303,),
    151: (1102,),
    154: (1201,),
    155: (2300, 1300,),
    156: (1411, 2301, 1403, 1202, 2201, 1301, 2200, 1400, 2302, 2303, 1302, 1401, 2304, 1402,),
}
GATHER_ACROSS = (1, 4)
SCATTER_ACROSS = (3, 1, 2)
MESH = pl.DeviceIdType.MESH
HALF = D // 2


class Place:
    def __init__(self):
        self.c = lax.axis_index("ctx")
        f = lax.axis_index("fsdp")
        self.z, self.y, self.k = f // 4, (f // 2) % 2, f % 2
        self.sibling = self.at(self.c, self.z, self.y, 1 - self.k)
        self.beside = self.at(1 - self.c, self.z, self.y, self.k)
        self.across = self.at(self.c, self.z, 1 - self.y, self.k)

    def at(self, c, z, y, k):
        return (c, z * 4 + y * 2 + k)

    def level(self, step):
        return lax.rem(self.z + step, 4)

    def along(self, step):
        return self.at(self.c, self.level(step), self.y, self.k)

    def pick(self, side, first, second):
        return first + side * (second - first)

    def onward(self, side):
        c = self.c + (1 - side) * (1 - 2 * self.c)
        y = self.y + side * (1 - 2 * self.y)
        return self.at(c, self.z, y, self.k)


def half(index):
    return pl.ds(pl.multiple_of(index * HALF, 128), HALF)


def send(source, target, sends, recvs, device):
    return pltpu.make_async_remote_copy(
        src_ref=source, dst_ref=target, send_sem=sends, recv_sem=recvs, device_id=device, device_id_type=MESH
    )


def fixed(piece):
    return not isinstance(piece[1] if isinstance(piece, tuple) else piece, jax.Array)


def begin(copies):
    for copy in copies:
        copy.start()


def landed(copies):
    for copy in copies:
        copy.wait_recv()


def gone(copies):
    for copy in copies:
        copy.wait_send()


class Gather:
    def __init__(self, place, sources, w_ref, d_ref, vec_ref, sends, recvs, local):
        self.p, self.sources = place, sources
        self.w, self.d, self.v = w_ref, d_ref, vec_ref
        self.sends, self.recvs, self.local = sends, recvs, local

    def whole(self, piece):
        return self.v if piece is None else self.w.at[piece]

    def row(self, piece):
        return 12 if piece is None else piece

    def lead(self, piece):
        return 1 if fixed(piece) and piece in GATHER_ACROSS else self.p.k

    def own(self, piece):
        if piece is None:
            return self.sources[3]
        if piece < 3:
            return self.sources[0].at[:, piece * D : piece * D + D]
        if piece == 3:
            return self.sources[1]
        return self.sources[2].at[:, (piece - 4) * D : (piece - 3) * D]

    def own_half(self, piece):
        cols = half(self.p.c)
        if piece is None:
            return self.sources[3].at[:, cols]
        if piece == 3:
            return self.sources[1].at[:, cols]
        base, first = (self.sources[0], 0) if piece < 3 else (self.sources[2], 4)
        return base.at[:, pl.ds(pl.multiple_of((piece - first) * D + self.p.c * HALF, 128), HALF)]

    def keep(self, piece):
        p = self.p
        return pltpu.make_async_copy(
            self.own(piece), self.whole(piece).at[p.z, p.y, p.k], self.local.at[self.row(piece)]
        )

    def keep_down(self):
        p = self.p
        return pltpu.make_async_copy(self.sources[4], self.d.at[p.z, p.y, p.k], self.local.at[8])

    def z_copy(self, piece, step, level):
        p, row = self.p, self.row(piece)
        return send(
            self.own_half(piece),
            self.whole(piece).at[level, p.y, p.k, :, half(p.c)],
            self.sends.at[row, step - 1],
            self.recvs.at[row, step - 1],
            p.along(step),
        )

    def z_down(self, step, level, sem):
        p = self.p
        return send(
            self.sources[4].at[:, half(p.c)],
            self.d.at[level, p.y, p.k, :, half(p.c)],
            self.sends.at[13, sem],
            self.recvs.at[13, sem],
            p.along(step),
        )

    def own_across(self, piece):
        p, row = self.p, self.row(piece)
        return send(
            self.own_half(piece),
            self.whole(piece).at[p.z, p.y, p.k, :, half(p.c)],
            self.sends.at[row, 6],
            self.recvs.at[row, 6],
            p.across,
        )

    def start(self, *pieces):
        for piece in pieces:
            for step in (1, 2, 3):
                self.z_copy(piece, step, self.p.z).start()
            self.own_across(piece).start()
            self.keep(piece).start()

    def start_down(self, j):
        @pl.when(self.p.z == j)
        def _():
            for step in (1, 2, 3):
                self.z_down(step, self.p.z, step - 1).start()
            self.keep_down().start()

    def copies(self, piece):
        p, row = self.p, self.row(piece)
        whole = self.whole(piece)

        def to(part, column, device):
            return send(part, part, self.sends.at[row, column], self.recvs.at[row, column], device)

        def beside():
            return [
                to(whole.at[p.level(step), p.y, p.k, :, half(p.c)], 2 + step, p.beside) for step in (1, 2, 3)
            ]

        def across():
            return [
                to(whole.at[p.level(step), p.y, p.k, :, half(p.c)], 8 + step, p.across) for step in (1, 2, 3)
            ]

        def forward():
            lead = self.lead(piece)
            part = whole.at[:, p.pick(lead, 1 - p.y, p.y), p.k, :, half(p.pick(lead, p.c, 1 - p.c))]
            return [to(part, 7, p.onward(lead))]

        def sibling():
            return [to(whole.at[:, :, p.k], 8, p.sibling)]

        return beside, across, forward, sibling

    def copies_down(self, j):
        p, row = self.p, 8 + j

        def to(part, column, device):
            return send(part, part, self.sends.at[row, column], self.recvs.at[row, column], device)

        def beside():
            return [to(self.d.at[j, p.y, p.k, :, half(p.c)], 3, p.beside)]

        def across():
            return [to(self.d.at[j, p.y, p.k, :, half(p.c)], 6, p.across)]

        def forward():
            lead = self.lead(("d", j))
            part = self.d.at[j, p.pick(lead, 1 - p.y, p.y), p.k, :, half(p.pick(lead, p.c, 1 - p.c))]
            return [to(part, 7, p.onward(lead))]

        def sibling():
            return [to(self.d.at[j, :, p.k], 8, p.sibling)]

        return beside, across, forward, sibling

    def stage(self, number, piece):
        if isinstance(piece, tuple):
            return self.stage_down(number, piece[1])
        p, row, whole = self.p, self.row(piece), self.whole(piece)
        beside, across, forward, sibling = self.copies(piece)
        if number == 2:
            self.keep_wait(piece)
            for step in (1, 2, 3):
                self.z_wait(piece, step)
            begin(across() + beside())
        elif number == 3:
            part = whole.at[p.z, p.y, p.k, :, half(p.c)]
            own = send(part, part, self.sends.at[row, 6], self.recvs.at[row, 6], p.across)
            landed([own] + across() + beside())
            begin(forward())
        elif number == 4:
            landed(forward())
            begin(sibling())
        elif number == 5:
            landed(sibling())
        else:
            gone(beside() + across() + forward() + sibling())

    def keep_wait(self, piece):
        p = self.p
        part = self.whole(piece).at[p.z, p.y, p.k]
        pltpu.make_async_copy(part, part, self.local.at[self.row(piece)]).wait()

    def z_wait(self, piece, step):
        p, row = self.p, self.row(piece)
        part = self.whole(piece).at[p.level(4 - step), p.y, p.k, :, half(p.c)]
        send(part, part, self.sends.at[row, step - 1], self.recvs.at[row, step - 1], p.along(step)).wait_recv()

    def stage_down(self, number, j):
        p = self.p
        beside, across, forward, sibling = self.copies_down(j)
        away = p.z != j
        if number == 2:

            @pl.when(away)
            def _():
                step = lax.rem(p.z - j + 4, 4)
                part = self.d.at[j, p.y, p.k, :, half(p.c)]
                landed([send(part, part, self.sends.at[13, step - 1], self.recvs.at[13, step - 1], p.along(1))])
                begin(beside())

            @pl.when(p.z == j)
            def _():
                self.keep_down().wait()

            begin(across())
        elif number == 3:

            @pl.when(away)
            def _():
                landed(beside())

            landed(across())
            begin(forward())
        elif number == 4:
            landed(forward())
            begin(sibling())
        elif number == 5:
            landed(sibling())
        else:

            @pl.when(away)
            def _():
                gone(beside())

            gone(across() + forward() + sibling())

    def finish(self):
        for piece in (None, *range(8)):
            for step in (1, 2, 3):
                self.z_copy(piece, step, self.p.z).wait_send()
            self.own_across(piece).wait_send()
        for step in (1, 2, 3):
            self.z_down(step, self.p.z, step - 1).wait_send()


class Scatter:
    def __init__(self, place, w_ref, d_ref, rings, sends, recvs):
        self.p, self.w, self.d = place, w_ref, d_ref
        self.rings = rings
        self.sends, self.recvs = sends, recvs

    def held(self, block):
        return block + 4 if not isinstance(block, tuple) and block < 3 else block

    def lead(self, block):
        return 1 if fixed(block) and block in SCATTER_ACROSS else self.p.k

    def pick(self, block, first, second):
        return first + self.lead(block) * (second - first)

    def turn(self, block, number):
        return self.p.onward(self.lead(block) if number == 0 else 1 - self.lead(block))

    def part(self, block, y, col):
        if isinstance(block, tuple):
            return self.d.at[block[1], y, self.p.k, :, half(col)]
        return self.w.at[self.held(block), :, y, self.p.k, :, half(col)]

    def row(self, block):
        return 8 + block[1] if isinstance(block, tuple) else block

    def ring(self, block, which, slot):
        ring = self.rings[2 * which + (1 if isinstance(block, tuple) else 0)]
        return ring.at[slot % ring.shape[0]]

    def sem(self, block, column):
        row = self.row(block)
        return self.sends.at[row, column], self.recvs.at[row, column]

    def to_sibling(self, block, slot):
        p = self.p
        part = self.d.at[block[1], :, 1 - p.k] if isinstance(block, tuple) else self.w.at[self.held(block), :, :, 1 - p.k]
        return send(part, self.ring(block, 0, slot), *self.sem(block, 0), p.sibling)

    def first(self, block, slot, i):
        p = self.p
        part = self.part(block, self.pick(block, i, 1 - p.y), self.pick(block, 1 - p.c, i))
        ring = self.ring(block, 1, slot)
        ring = ring.at[i] if isinstance(block, tuple) else ring.at[:, i]
        return send(part, ring, *self.sem(block, 1 + i), self.turn(block, 0))

    def second(self, block, slot):
        p = self.p
        part = self.part(block, self.pick(block, 1 - p.y, p.y), self.pick(block, p.c, 1 - p.c))
        return send(part, self.ring(block, 2, slot), *self.sem(block, 3), self.turn(block, 1))

    def third(self, block, slot, step):
        p = self.p
        part = self.w.at[self.held(block), p.level(step), p.y, p.k, :, half(p.c)]
        return send(part, self.rings[6].at[slot % 4, step - 1], *self.sem(block, 3 + step), p.along(step))

    def third_down(self, j, step):
        p = self.p
        part = self.part(("d", j), p.y, p.c)
        return send(part, self.rings[7].at[step - 1], *self.sem(("d", j), 3 + step), p.at(p.c, j, p.y, p.k))

    def last(self, block):
        p = self.p
        land = self.rings[9] if isinstance(block, tuple) else self.rings[8].at[block]
        return send(self.total(block), land, *self.sem(block, 7), p.beside)

    def total(self, block):
        return self.rings[11] if isinstance(block, tuple) else self.rings[10].at[block]

    def store(self, block, target, sems):
        c = self.p.c
        land = self.rings[9] if isinstance(block, tuple) else self.rings[8].at[block]
        return [
            pltpu.make_async_copy(self.total(block), target.at[:, half(c)], sems.at[0]),
            pltpu.make_async_copy(land, target.at[:, half(1 - c)], sems.at[1]),
        ]

    def stage(self, number, block, slot):
        p = self.p
        down = isinstance(block, tuple)
        if number == 0:
            self.to_sibling(block, slot).start()
        elif number == 1:
            self.to_sibling(block, slot).wait_recv()
            mine = self.d.at[block[1], :, p.k] if down else self.w.at[self.held(block), :, :, p.k]
            mine[...] = mine[...] + self.ring(block, 0, slot)[...]
            for i in (0, 1):
                self.first(block, slot, i).start()
        elif number == 2:
            for i in (0, 1):
                self.first(block, slot, i).wait_recv()
                mine = self.part(block, self.pick(block, i, p.y), self.pick(block, p.c, i))
                ring = self.ring(block, 1, slot)
                mine[...] = mine[...] + (ring[i] if down else ring[:, i])
            self.second(block, slot).start()
        elif number == 3:
            self.second(block, slot).wait_recv()
            mine = self.part(block, p.y, p.c)
            mine[...] = mine[...] + self.ring(block, 2, slot)[...]
            if down:
                j = block[1]

                @pl.when(p.z != j)
                def _():
                    step = lax.rem(j - p.z + 4, 4)
                    self.third_down(j, step).start()
            else:
                for step in (1, 2, 3):
                    self.third(block, slot, step).start()
        elif number == 4:
            if down:
                j = block[1]

                @pl.when(p.z == j)
                def _():
                    total = self.part(block, p.y, p.c)[...].astype(F32)
                    for step in (1, 2, 3):
                        self.third_down(j, step).wait_recv()
                        total = total + self.rings[7][step - 1].astype(F32)
                    self.total(block)[...] = total.astype(BF16)
                    self.last(block).start()
            else:
                total = self.w[self.held(block), p.z, p.y, p.k, :, half(p.c)].astype(F32)
                for step in (1, 2, 3):
                    self.third(block, slot, step).wait_recv()
                    total = total + self.rings[6][slot % 4, step - 1].astype(F32)
                self.total(block)[...] = total.astype(BF16)
                self.last(block).start()
        elif number == 5:
            if down:

                @pl.when(p.z == block[1])
                def _():
                    self.last(block).wait_recv()
            else:
                self.last(block).wait_recv()

    def finish(self, block, slot):
        self.finish_block(block, slot)
        if isinstance(block, tuple):

            @pl.when(self.p.z == block[1])
            def _():
                self.last(block).wait_send()
        else:
            self.last(block).wait_send()

    def finish_block(self, block, slot):
        p = self.p
        self.to_sibling(block, slot).wait_send()
        for i in (0, 1):
            self.first(block, slot, i).wait_send()
        self.second(block, slot).wait_send()
        if isinstance(block, tuple):
            j = block[1]

            @pl.when(p.z != j)
            def _():
                self.third_down(j, lax.rem(j - p.z + 4, 4)).wait_send()
        else:
            for step in (1, 2, 3):
                self.third(block, slot, step).wait_send()


def layer_kernel(
    x_hbm, cot_hbm, seg_ref, qkv_hbm, out_hbm, up_hbm, rows_ref, bup_own_ref, down_hbm,
    act_hbm, gx_hbm, fin_hbm, find_hbm, vg_hbm,
    w_ref, d_ref, vecs_ref, vec_ref, x_ref, cot_ref, q_ref, k_ref, v_ref, o_ref, p_ref, bias_ref,
    acc_ref, n2_ref, a2_ref, rs2_ref, g2_ref, a1_ref, gu_ref, vg_ref, bup_ref,
    ring0, ring1, ring2, ring3, ring4, ring5, ring6, ring7, land_ref, landd_ref, own_ref, ownd_ref, vr_ref,
    qs_ref, vloc_ref, small_ref, slices_ref, parts_ref, ag_send, ag_recv, ag_local, rs_send, rs_recv, v_send, v_recv, x_send, x_recv, sem, out_sem,
):
    place = Place()
    mine = place.c
    a3_ref = x_ref.at[0:1024]
    gather = Gather(
        place, (qs_ref, out_hbm, up_hbm, vloc_ref, down_hbm), w_ref, d_ref, vecs_ref, ag_send, ag_recv, ag_local
    )
    scatter = Scatter(
        place, w_ref, d_ref, (ring0, ring1, ring2, ring3, ring4, ring5, ring6, ring7, land_ref, landd_ref, own_ref, ownd_ref), rs_send, rs_recv
    )
    barrier = pltpu.get_barrier_semaphore()
    for device in (place.sibling, place.beside, place.across, place.along(1), place.along(2), place.along(3)):
        pl.semaphore_signal(barrier, 1, device_id=device, device_id_type=MESH)
    load_x = pltpu.make_async_copy(x_hbm, x_ref.at[0:1024], sem.at[0])
    load_cot = pltpu.make_async_copy(cot_hbm, cot_ref, sem.at[1])
    loads = [
        pltpu.make_async_copy(
            qkv_hbm.at[:, D * part + 256 * group : D * part + 256 * group + 256],
            qs_ref.at[:, D * group + 256 * part : D * group + 256 * part + 256],
            sem.at[5 + 3 * group + part],
        )
        for group in range(3)
        for part in range(3)
    ]
    begin(loads)
    load_x.start()
    load_cot.start()
    def lane_match(rows, cols, shift, limit):
        row = lax.broadcasted_iota(jnp.int32, (rows, cols), 0)
        col = lax.broadcasted_iota(jnp.int32, (rows, cols), 1)
        return (row - col == shift) & (col < limit)

    owner = place.z * 4 + place.y * 2 + place.k
    inner = place.y * 2 + place.k
    spread = jnp.where(lane_match(48, D, -48 * owner, D), 1.0, 0.0).astype(BF16)
    vloc_ref[0:8, :] = dot(rows_ref[...], spread, 1, 0).astype(BF16)
    spread = jnp.where(lane_match(192, D, -192 * inner, D), 1.0, 0.0).astype(BF16)
    wide = dot(jnp.broadcast_to(bup_own_ref[...], (8, 192)), spread, 1, 0)
    chosen = lax.broadcasted_iota(jnp.int32, (8, D), 0) == place.z
    vloc_ref[8:16, :] = jnp.where(chosen, wide, 0.0).astype(BF16)
    pl.semaphore_wait(barrier, 6)
    for copy in loads:
        copy.wait()

    def give(part):
        start = pl.multiple_of((part // 2) * 512 + mine * BLK + (part % 2) * 128, 128)
        return send(
            x_hbm.at[pl.ds(start, 128)],
            x_ref.at[1024 + part * 128 : 1152 + part * 128],
            x_send.at[part],
            x_recv.at[part],
            place.beside,
        )

    def give_back(part):
        rows = slice(part * 128, part * 128 + 128)
        return send(
            a2_ref.at[rows], bias_ref.at[rows], x_send.at[4 + part], x_recv.at[4 + part], place.beside
        )

    rounds = (
        [(0, place.sibling)],
        [(1, place.beside)],
        [(2, place.across)],
        [(3, place.along(1)), (4, place.along(2)), (5, place.along(3))],
    )

    def exchange(index, device):
        if index < 3:
            return send(vg_ref, vr_ref.at[index], v_send.at[index], v_recv.at[index], device)
        source = slices_ref.at[place.level(index - 2)]
        return send(source, parts_ref.at[index - 3], v_send.at[index], v_recv.at[index], device)

    def slice_vectors(value):
        high = value.astype(BF16)
        left = value - high.astype(F32)
        middle = left.astype(BF16)
        low = (left - middle.astype(F32)).astype(BF16)
        exact = jnp.concatenate([high, middle, low], 0)
        row = lax.broadcasted_iota(jnp.int32, (D, 512), 0)
        col = lax.broadcasted_iota(jnp.int32, (D, 512), 1)
        lane = col & 127
        chosen = (row == 192 * (col >> 7) + 48 * inner + lane) & (lane < 48)
        short = dot(exact, jnp.where(chosen, 1.0, 0.0).astype(BF16), 1, 0)
        short = short[0:16] + short[16:32] + short[32:48]
        chosen = lane_match(D, 256, 192 * inner, 192)
        long = dot(exact, jnp.where(chosen, 1.0, 0.0).astype(BF16), 1, 0)
        long = long[0:16] + long[16:32] + long[32:48]
        slices_ref[...] = jnp.zeros_like(slices_ref)
        for z in range(4):
            slices_ref[z, 0:8, :] = short[0:8, 128 * z : 128 * z + 128]
            slices_ref[z, 8:9, :] = long[8 + z : 9 + z, 0:128]
            slices_ref[z, 9:10, :] = long[8 + z : 9 + z, 128:256]

    def vectors(number):
        if number > 0:
            for index, device in rounds[number - 1]:
                exchange(index, device).wait()
        if number in (1, 2, 3):
            value = vg_ref[...] + vr_ref[number - 1]
            if number < 3:
                vg_ref[...] = value
            else:
                slice_vectors(value)
        if number == 4:
            small_ref[...] = slices_ref[place.z] + parts_ref[0] + parts_ref[1] + parts_ref[2]
        else:
            for index, device in rounds[number]:
                exchange(index, device).start()

    def piece(number):
        return None if number == 12 else number if number < 8 else ("d", number - 8)

    places = (5, 6, 7, 4, 0, 1, 2, 3, 0, 1, 2, 3)

    def step(code):
        kind, rest = code // 100, code % 100
        if kind < 10:
            gather.stage(kind, piece(rest))
        elif kind < 20:
            scatter.stage(kind - 10, piece(rest), places[rest])
        elif kind == 20:
            if 8 <= rest < 12:
                gather.start_down(rest - 8)
            else:
                gather.start(piece(rest))
        elif kind == 21:
            give(rest).start()
        elif kind == 22:
            give_back(rest).start()
        else:
            vectors(rest)

    def at(slot):
        for code in PLAN.get(slot, ()):
            step(code)

    def at_loop(slot, index, count):
        for i in range(count):
            if PLAN.get(slot + i):

                @pl.when(index == i)
                def _():
                    at(slot + i)

    def weight(index):
        return w_ref[index].reshape(D, D)

    def weight_down(index):
        return d_ref[index].reshape(D, D)

    def vec(row):
        return vec_ref[row : row + 1, :]

    def add_vec(row, value):
        vg_ref[row : row + 1, :] += value

    at(0)
    vg_ref[...] = jnp.zeros_like(vg_ref)
    attention_masks(seg_ref, bias_ref, mine)
    at(1)
    total = vecs_ref[0, 0, 0].astype(F32)
    for shard in range(1, 16):
        total = total + vecs_ref[shard // 4, (shard // 2) % 2, shard % 2].astype(F32)
    vec_ref[...] = total
    load_x.wait()

    def first_norm(r):
        rows = pl.ds(r * BLK, BLK)
        normed, _ = norm(x_ref[rows, :].astype(F32))
        a1_ref[rows, :] = (normed * vec(0) + vec(1)).astype(BF16)

    loop(4, first_norm)
    refs = (q_ref, k_ref, v_ref, o_ref, p_ref, bias_ref)
    for g in range(3):
        at(10 + 10 * g)
        cols = slice(256 * g, 256 * g + 256)
        mixed = dot(a1_ref[0:1024, :], weight(g), 1, 0)
        q_ref[:, cols] = ((mixed[:, :256] + vec(2)[:, cols]).astype(BF16) * 0.125).astype(BF16)
        k_ref[0:1024, cols] = mixed[:, 256:512].astype(BF16)
        v_ref[0:1024, cols] = (mixed[:, 512:] + vec(3)[:, cols]).astype(BF16)

        def solo(m):
            at_loop(11 + 10 * g, m, 2)
            forward_heads(m, g, refs, mine, (0,))

        loop(2, solo)
    at(40)
    for part in range(4):
        give(part).wait_recv()
    loop(2, lambda r: first_norm(4 + r))
    for g in range(3):
        cols = slice(256 * g, 256 * g + 256)
        mixed = dot(a1_ref[1024:1536, :], weight(g)[:, 256:], 1, 0)
        k_ref[1024:1536, cols] = mixed[:, :256].astype(BF16)
        v_ref[1024:1536, cols] = (mixed[:, 256:] + vec(3)[:, cols]).astype(BF16)

    def wide(i):
        at_loop(41, i, 6)
        forward_heads(i // 3, i % 3, refs, mine, (1, 2))

    loop(6, wide)

    at(50)
    acc_ref[...] = dot(o_ref[...], weight(3), 1, 0)
    load_cot.wait()
    at(51)

    def second_norm(r):
        rows = pl.ds(r * BLK, BLK)
        resid = acc_ref[rows, :] + x_ref[rows, :].astype(F32) + vec(4)
        normed, inverse = norm(resid)
        acc_ref[rows, :] = resid + vec(7)
        n2_ref[rows, :] = normed.astype(BF16)
        a2_ref[rows, :] = (normed * vec(5) + vec(6)).astype(BF16)
        rs2_ref[:, lanes(r, BLK)] = jnp.broadcast_to(inverse, (BLK, 128)).T[0:8]
        add_vec(7, colsum(cot_ref[rows, :].astype(F32)))
        g2_ref[rows, :] = jnp.zeros((BLK, D), F32)

    loop(4, second_norm)
    for j in range(4):
        bup_ref[j, 0:1] = vec(8 + j)
        bup_ref[j, 1:2] = jnp.zeros((1, D), F32)

    def feed(j):
        up = 4 + j
        bias = bup_ref[j, 0:1]

        def at_chunk(slot):
            for i in range(4):
                if PLAN.get(slot + 10 * i):

                    @pl.when(j == i)
                    def _():
                        at(slot + 10 * i)

        def part(r):
            rows = slice(r * 512, r * 512 + 512)
            u = dot(a2_ref[rows, :], weight(up), 1, 0) + bias
            back = dot(cot_ref[rows, :], weight_down(j), 1, 1)
            square = u * u
            th = jnp.tanh(u * (0.7978845608028654 + 0.035677408136300125 * square))
            half_up = 0.5 + 0.5 * th
            a3_ref[rows, :] = (u * half_up).astype(BF16)
            slope = half_up + (half_up * (1.0 - th)) * (u * (0.7978845608028654 + 0.10703222440890037 * square))
            gu = (back * slope).astype(BF16)
            gu_ref[rows, :] = gu
            bup_ref[j, 1:2] += colsum(gu.astype(F32))

        at_chunk(60)
        part(0)
        at_chunk(61)
        part(1)
        at_chunk(62)
        acc_ref[...] += dot(a3_ref[...], weight_down(j), 1, 0)
        g2_ref[...] += dot(gu_ref[...], weight(up), 1, 1)
        at_chunk(63)
        gather.stage(6, up)
        w_ref[up] = dot(a2_ref[...], gu_ref[...], 0, 0).astype(BF16).reshape(4, 2, 2, 48, D)
        at_chunk(64)
        gather.stage(6, ("d", j))
        d_ref[j] = dot(a3_ref[...], cot_ref[...], 0, 0).astype(BF16).reshape(2, 2, 192, D)

    loop(4, feed)
    at(100)
    for j in range(4):
        vg_ref[8 + j : 9 + j, :] = bup_ref[j, 1:2]

    def second_back(r):
        rows = pl.ds(r * BLK, BLK)
        a3_ref[rows, :] = acc_ref[rows, :].astype(BF16)
        g2 = g2_ref[rows, :]
        normed = n2_ref[rows, :].astype(F32)
        add_vec(5, colsum(g2 * normed))
        add_vec(6, colsum(g2))
        inverse = jnp.broadcast_to(rs2_ref[0:1, lanes(r, BLK)], (128, BLK)).T[:, 0:1]
        t = g2 * vec(5)
        first = jnp.mean(t, -1, keepdims=True)
        second = jnp.mean(t * normed, -1, keepdims=True)
        grad = cot_ref[rows, :].astype(F32) + inverse * (t - first - normed * second)
        g2_ref[rows, :] = grad
        lowered = grad.astype(BF16)
        a2_ref[rows, :] = lowered
        add_vec(4, colsum(lowered.astype(F32)))

    loop(4, second_back)
    out_copies = [
        pltpu.make_async_copy(x_ref.at[micro * 512 : micro * 512 + 512], act_hbm.at[micro, 0], sem.at[3 + micro])
        for micro in range(2)
    ]
    begin(out_copies)
    at(101)
    gu_ref[...] = dot(a2_ref[...], weight(3), 1, 1).astype(BF16)
    at(102)
    gather.stage(6, 3)
    w_ref[3] = dot(o_ref[...], a2_ref[...], 0, 0).astype(BF16).reshape(4, 2, 2, 48, D)
    refs = (q_ref, k_ref, v_ref, gu_ref, p_ref)

    for g in range(3):
        cols = slice(256 * g, 256 * g + 256)

        def back(m):
            at_loop(120 + 10 * g, m, 2)
            backward_heads(m, g, refs, mine, (1, 2))
            backward_heads(m, g, refs, mine, (0,))

        loop(2, back)
        at(122 + 10 * g)
        scatter.finish_block(4 + g, g)
        mixed = jnp.concatenate([k_ref[:, cols], v_ref[:, cols]], 1)
        w_ref[4 + g, :, :, :, :, 0:256] = (
            dot(a1_ref[0:1024, :], q_ref[:, cols], 0, 0).astype(BF16).reshape(4, 2, 2, 48, 256)
        )
        w_ref[4 + g, :, :, :, :, 256:] = dot(a1_ref[...], mixed, 0, 0).astype(BF16).reshape(4, 2, 2, 48, 512)
    at(110)
    for g in range(3):
        cols = slice(256 * g, 256 * g + 256)
        mixed = jnp.concatenate([k_ref[1024:1536, cols], v_ref[1024:1536, cols]], 1)
        value = dot(mixed, weight(g)[:, 256:], 1, 1)
        acc_ref[0:512, :] = value if g == 0 else acc_ref[0:512, :] + value
    a2_ref[0:512, :] = acc_ref[0:512, :].astype(BF16)
    for copy in out_copies:
        copy.wait()
    load_x.start()

    for g in range(3):
        at(150 + g)
        cols = slice(256 * g, 256 * g + 256)
        mixed = jnp.concatenate([q_ref[:, cols], k_ref[0:1024, cols], v_ref[0:1024, cols]], 1)
        value = dot(mixed, weight(g), 1, 1)
        acc_ref[...] = value if g == 0 else acc_ref[...] + value
    at(153)
    add_vec(2, colsum(q_ref[...].astype(F32)))
    add_vec(3, colsum(v_ref[...].astype(F32)))
    at(154)

    def extra_back(r):
        rows = pl.ds(1024 + r * BLK, BLK)
        normed, _ = norm(x_ref[rows, :].astype(F32))
        g1 = a2_ref[pl.ds(r * BLK, BLK), :].astype(F32)
        add_vec(0, colsum(g1 * normed))
        add_vec(1, colsum(g1))

    loop(2, extra_back)

    def first_sums(r):
        rows = pl.ds(r * BLK, BLK)
        normed, inverse = norm(x_ref[rows, :].astype(F32))
        g1 = acc_ref[rows, :]
        add_vec(0, colsum(g1 * normed))
        add_vec(1, colsum(g1))

    load_x.wait()
    loop(4, first_sums)

    def first_back(micro, block):
        rows = pl.ds(pl.multiple_of(micro * 512 + block * BLK, BLK), BLK)
        normed, inverse = norm(x_ref[rows, :].astype(F32))
        t = acc_ref[rows, :] * vec(0)
        first = jnp.mean(t, -1, keepdims=True)
        second = jnp.mean(t * normed, -1, keepdims=True)
        gu_ref[rows, :] = (g2_ref[rows, :] + inverse * (t - first - normed * second)).astype(BF16)

    at(155)
    loop(2, lambda micro: first_back(micro, 1 - mine))
    at(156)
    for part in range(4):
        give_back(part).wait_recv()
    for micro in range(2):
        rows = pl.ds(pl.multiple_of(micro * 512 + mine * BLK, BLK), BLK)
        acc_ref[rows, :] += bias_ref[micro * BLK : micro * BLK + BLK, :].astype(F32)
    loop(2, lambda micro: first_back(micro, mine))
    gx_copies = [
        pltpu.make_async_copy(gu_ref.at[micro * 512 : micro * 512 + 512], gx_hbm.at[micro, 0], sem.at[3 + micro])
        for micro in range(2)
    ]
    begin(gx_copies)
    at(157)
    ends = [pltpu.make_async_copy(small_ref, vg_hbm, sem.at[2])]
    begin(ends)
    for block in (4, 5, 6, 8, 9, 10, 7, 3, 11, 0, 1, 2):
        scatter.stage(5, piece(block), places[block])
        if block < 8:
            copies = scatter.store(block, fin_hbm.at[block], out_sem.at[block])
            begin(copies)
            ends += copies
        elif block == 11:
            copies = scatter.store(("d", 0), find_hbm, out_sem.at[8])
            begin(copies)
            ends += copies
    for block in range(12):
        if 4 <= block < 7:
            scatter.last(block).wait_send()
        else:
            scatter.finish(piece(block), places[block])
    for part in (None, 0, 1, 2):
        gather.stage(6, part)
    gather.finish()
    for part in range(4):
        give(part).wait_send()
        give_back(part).wait_send()
    for copy in gx_copies:
        copy.wait()
    for copy in ends:
        copy.wait()


def hand_out(
    act_ref, gx_ref, fin_ref, find_ref, small_ref, act_out, gx_out, qkv_ref, out_ref, up_ref, down_ref, *rest
):
    vectors = rest
    act_out[...] = act_ref[...]
    gx_out[...] = gx_ref[...]

    @pl.when(pl.program_id(0) == 0)
    def _():
        for part in range(3):
            for g in range(3):
                start = D * part + 256 * g
                qkv_ref[:, start : start + 256] = fin_ref[g, :, 256 * part : 256 * part + 256].astype(F32)
        out_ref[...] = fin_ref[3].astype(F32)
        for j in range(4):
            up_ref[:, D * j : D * j + D] = fin_ref[4 + j].astype(F32)
        down_ref[...] = find_ref[...].astype(F32)
        for i in range(8):
            vectors[i][...] = small_ref[i : i + 1, 0:48]
        vectors[8][:, 0:128] = small_ref[8:9, :]
        vectors[8][:, 128:192] = small_ref[9:10, 0:64]


def fast_device(
    layer_input, segments, ln1_gain, ln1_bias, w_qkv, q_bias, v_bias, w_attn_out, b_attn_out,
    ln2_gain, ln2_bias, w_up, b_up, w_down, b_down, cotangent,
):
    rows = jnp.stack([ln1_gain, ln1_bias, q_bias, v_bias, b_attn_out, ln2_gain, ln2_bias, b_down])
    big = lambda *shape, dtype=BF16: jax.ShapeDtypeStruct(shape, dtype)
    hbm = pl.BlockSpec(memory_space=pltpu.HBM)
    vmem = pl.BlockSpec(memory_space=pltpu.VMEM)
    act, gx, fin, find, small = pl.pallas_call(
        layer_kernel,
        out_shape=(
            big(2, 1, 512, D), big(2, 1, 512, D), big(8, 48, D), big(192, D), big(16, 128, dtype=F32),
        ),
        in_specs=[hbm, hbm, vmem, hbm, hbm, hbm, vmem, vmem, hbm],
        out_specs=(hbm,) * 5,
        scratch_shapes=[
            pltpu.VMEM((8, 4, 2, 2, 48, D), BF16),
            pltpu.VMEM((4, 2, 2, 192, D), BF16),
            pltpu.VMEM((4, 2, 2, 16, D), BF16),
            pltpu.VMEM((16, D), F32),
            pltpu.VMEM((1536, D), BF16),
            pltpu.VMEM((1024, D), BF16),
            pltpu.VMEM((1024, D), BF16),
            pltpu.VMEM((1536, D), BF16),
            pltpu.VMEM((1536, D), BF16),
            pltpu.VMEM((1024, D), BF16),
            pltpu.VMEM((12, 2, 3 * BLK, BLK), BF16),
            pltpu.VMEM((2 * BLK, 3 * BLK), BF16),
            pltpu.VMEM((1024, D), F32),
            pltpu.VMEM((1024, D), BF16),
            pltpu.VMEM((1024, D), BF16),
            pltpu.VMEM((8, 1024), F32),
            pltpu.VMEM((1024, D), F32),
            pltpu.VMEM((1536, D), BF16),
            pltpu.VMEM((1024, D), BF16),
            pltpu.VMEM((16, D), F32),
            pltpu.VMEM((4, 8, D), F32),
            pltpu.VMEM((3, 4, 2, 48, D), BF16),
            pltpu.VMEM((2, 2, 192, D), BF16),
            pltpu.VMEM((4, 4, 2, 48, HALF), BF16),
            pltpu.VMEM((4, 2, 192, HALF), BF16),
            pltpu.VMEM((4, 4, 48, HALF), BF16),
            pltpu.VMEM((4, 192, HALF), BF16),
            pltpu.VMEM((4, 3, 48, HALF), BF16),
            pltpu.VMEM((3, 192, HALF), BF16),
            pltpu.VMEM((8, 48, HALF), BF16),
            pltpu.VMEM((192, HALF), BF16),
            pltpu.VMEM((8, 48, HALF), BF16),
            pltpu.VMEM((192, HALF), BF16),
            pltpu.VMEM((3, 16, D), F32),
            pltpu.VMEM((48, 3 * D), BF16),
            pltpu.VMEM((16, D), BF16),
            pltpu.VMEM((16, 128), F32),
            pltpu.VMEM((4, 16, 128), F32),
            pltpu.VMEM((3, 16, 128), F32),
            pltpu.SemaphoreType.DMA((14, 12)),
            pltpu.SemaphoreType.DMA((14, 12)),
            pltpu.SemaphoreType.DMA((13,)),
            pltpu.SemaphoreType.DMA((12, 8)),
            pltpu.SemaphoreType.DMA((12, 8)),
            pltpu.SemaphoreType.DMA((6,)),
            pltpu.SemaphoreType.DMA((6,)),
            pltpu.SemaphoreType.DMA((8,)),
            pltpu.SemaphoreType.DMA((8,)),
            pltpu.SemaphoreType.DMA((14,)),
            pltpu.SemaphoreType.DMA((9, 2)),
        ],
        compiler_params=pltpu.CompilerParams(
            vmem_limit_bytes=66_500_000, collective_id=0, has_side_effects=True
        ),
        name="layer",
    )(
        layer_input.reshape(1024, D), cotangent.reshape(1024, D), segments,
        w_qkv, w_attn_out, w_up, rows, b_up[None], w_down,
    )
    rows_of = pl.BlockSpec((2, 1, 128, D), lambda i: (0, 0, i, 0))

    def whole(*shape):
        return pl.BlockSpec(shape, lambda i: (0,) * len(shape))

    f32 = lambda *shape: jax.ShapeDtypeStruct(shape, F32)
    act, gx, g_qkv, g_out, g_up, g_down, *vectors = pl.pallas_call(
        hand_out,
        out_shape=(
            big(2, 1, 512, D), big(2, 1, 512, D), f32(48, 3 * D), f32(48, D), f32(48, 4 * D), f32(192, D),
        ) + (f32(1, 48),) * 8 + (f32(1, 192),),
        grid=(4,),
        in_specs=[rows_of, rows_of, whole(8, 48, D), whole(192, D), whole(16, 128)],
        out_specs=(rows_of, rows_of, whole(48, 3 * D), whole(48, D), whole(48, 4 * D), whole(192, D))
        + (whole(1, 48),) * 8
        + (whole(1, 192),),
        name="hand_out",
    )(act, gx, fin, find, small)
    part = [v[0] for v in vectors]
    return (
        act, gx, part[0], part[1], g_qkv, part[2], part[3], g_out, part[4], part[5], part[6], g_up, part[8], g_down, part[7],
    )


def solution(mesh):
    in_specs = (
        P(None, "fsdp", "ctx", None),
        P(None, "fsdp", None),
        P("fsdp"),
        P("fsdp"),
        P("fsdp", None),
        P("fsdp"),
        P("fsdp"),
        P("fsdp", None),
        P("fsdp"),
        P("fsdp"),
        P("fsdp"),
        P("fsdp", None),
        P("fsdp"),
        P("fsdp", None),
        P("fsdp"),
        P(None, "fsdp", "ctx", None),
    )
    out_specs = (
        P(None, "fsdp", "ctx", None),
        P(None, "fsdp", "ctx", None),
        P("fsdp"),
        P("fsdp"),
        P("fsdp", None),
        P("fsdp"),
        P("fsdp"),
        P("fsdp", None),
        P("fsdp"),
        P("fsdp"),
        P("fsdp"),
        P("fsdp", None),
        P("fsdp"),
        P("fsdp", None),
        P("fsdp"),
    )
    fast = mesh.shape["ctx"] == 2 and mesh.shape["fsdp"] == 16
    return jax.shard_map(
        fast_device if fast else on_device, mesh=mesh, in_specs=in_specs, out_specs=out_specs, check_vma=False
    )
```
